256 devices in a mesh: dir: 8 (over z_hi, core), dom: 32 (over y, z_lo, x).
Axes of the slice: x: 4, y: 4, z: 8 (z_hi: 4, z_lo: 2; z = z_hi * 2 + z_lo), core: 2. Of those that a mesh axis runs over, the one named last changes fastest.
Arguments:
- images: bfloat16 [8192, 4096], P('dom'), may hold values from -12 to 12
- refs: bfloat16 [2048, 4096], P(('dir', 'dom')), may hold values from -0.8 to 0.8
- ctf: float32 [64, 2048], replicated, may hold values from -1 to 1
- noise_var: float32 [2048], replicated, may hold values from 0.5 to 2
- shifts: int32 [8192, 2], P('dom'), may hold values from -4 to 4
- ctf_class: int32 [8192], P('dom'), may hold values from 0 to 63
- psi_prev: int32 [8192], P('dom'), may hold values from 0 to 15
- earlier_direction_range: int32 [8192], P('dom'), may hold values from 0 to 7
- view_range: int32 [128], P('dir'), may hold values from 0 to 7
Outputs:
- class_sums: float32 [2048, 4096], P(('dir', 'dom'))
- weight_sums: float32 [2048, 2048], P(('dir', 'dom'))
- log_norm: float32 [8192], P('dom')
- peak_prob: float32 [8192], P('dom')
The draws below stay inside these ranges and needn't reach their ends.
All inputs are finite; a program needn't handle non-finite values.
Results may differ from the reference program's by a relative error of at most 0.0095.
The reference program's roundings to bfloat16 on the way count: a program that leaves them out, or rounds other values in their place, can miss the bound.
Values may be sent and summed in bfloat16 or wider, within the bound.
A program may use at most 64 MiB of HBM per device.

```python
import math
import jax
import jax.numpy as jnp
from jax import lax

CROP = 64
HALF = 32
PIX = 2048
FEAT = 4096
PART_DEV = 256
REF_GROUP = 256
OFFSETS = 9
PSI_STEPS = 16
CTF_GROUPS = 64
RANGES = 8
PARTICLES = 8192
REFS = 2048
VIEWS = 128


def draw_images(key, part):
    first = jax.random.fold_in(jax.random.fold_in(key, 101), 0)
    values = jax.random.normal(first, (PARTICLES, FEAT), jnp.float32)
    return jnp.clip(values, -6.0, 6.0).astype(jnp.bfloat16)


def draw_refs(key, part):
    first = jax.random.fold_in(jax.random.fold_in(key, 202), 0)
    rows = jnp.arange(REFS, dtype=jnp.int32)
    groups = REFS // REF_GROUP
    rise = 1.0 + 0.12 * (rows // REF_GROUP).astype(jnp.float32) / max(groups - 1, 1)
    values = jax.random.normal(first, (REFS, FEAT), jnp.float32)
    return jnp.clip(0.07 * rise[:, None] * values, -0.789, 0.789).astype(jnp.bfloat16)


def with_ends(entries, rng, smallest, top_value):
    longest = entries.shape.index(max(entries.shape))
    spots = []
    for shift in (0, 1):
        where = [jax.random.randint(jax.random.fold_in(rng, axis), (), 0, length) for axis, length in enumerate(entries.shape)]
        where[longest] = (where[longest] + shift) % entries.shape[longest]
        spots.append(tuple(where))
    return entries.at[spots[0]].set(smallest).at[spots[1]].set(top_value)


def setup_inputs(seed: int = 0) -> dict:
    key_list = jax.random.split(jax.random.key(seed), 10)
    return {
        "images": draw_images(jax.random.fold_in(key_list[9], 71), 0),
        "refs": draw_refs(jax.random.fold_in(key_list[9], 71), 0),
        "ctf": jnp.clip(jax.random.uniform(key_list[2], (CTF_GROUPS, PIX), jnp.float32, -1.0, 1.0), -1.0, 1.0),
        "noise_var": jnp.clip(jnp.exp(jax.random.uniform(key_list[3], (PIX,), jnp.float32, math.log(0.5), math.log(2.0))), 0.5, 2.0),
        "shifts": with_ends(jax.random.randint(key_list[4], (PARTICLES, 2), -4, 5), jax.random.fold_in(key_list[4], 1), -4, 4).astype(jnp.int32),
        "ctf_class": with_ends(jax.random.randint(key_list[5], (PARTICLES,), 0, CTF_GROUPS), jax.random.fold_in(key_list[5], 1), 0, CTF_GROUPS - 1).astype(jnp.int32),
        "psi_prev": with_ends(jax.random.randint(key_list[6], (PARTICLES,), 0, PSI_STEPS), jax.random.fold_in(key_list[6], 1), 0, PSI_STEPS - 1).astype(jnp.int32),
        "earlier_direction_range": with_ends(jax.random.randint(key_list[7], (PARTICLES,), 0, RANGES), jax.random.fold_in(key_list[7], 1), 0, RANGES - 1).astype(jnp.int32),
        "view_range": with_ends(jax.random.randint(key_list[8], (VIEWS,), 0, RANGES), jax.random.fold_in(key_list[8], 1), 0, RANGES - 1).astype(jnp.int32),
    }


range_reward = 1.5
inplane_angle_width = 3.0


def phase_angles(shift_y, shift_x):
    pixels = jnp.arange(CROP * HALF, dtype=jnp.int32)
    freq_y = pixels // HALF
    freq_x = pixels % HALF
    index = (freq_y * shift_y[..., None] + freq_x * shift_x[..., None]) % CROP
    return index.astype(jnp.float32) * (2.0 * math.pi / CROP)


def offset_tables():
    offsets = jnp.arange(OFFSETS, dtype=jnp.int32)
    angles = phase_angles(offsets // 3 - 1, offsets % 3 - 1)
    return jnp.cos(angles), jnp.sin(angles)


def align_images(images, shifts, ctf_class, ctf, noise_var):
    angles = phase_angles(shifts[:, 0], shifts[:, 1])
    cosine_part = jnp.cos(angles)
    sine_part = jnp.sin(angles)
    pixels = CROP * HALF
    real_part = images[:, :pixels].astype(jnp.float32)
    imag_part = images[:, pixels:].astype(jnp.float32)
    weighting = jnp.take(ctf, ctf_class, axis=0) / noise_var[None, :]
    aligned_real = (real_part * cosine_part + imag_part * sine_part) * weighting
    aligned_imag = (imag_part * cosine_part - real_part * sine_part) * weighting
    return jnp.concatenate([aligned_real, aligned_imag], axis=1).astype(jnp.bfloat16)


def shift_block(ref_rows, cosine_row, sine_row):
    pixels = CROP * HALF
    real_part = ref_rows[:, :pixels].astype(jnp.float32)
    imag_part = ref_rows[:, pixels:].astype(jnp.float32)
    shifted_real = real_part * cosine_row[None, :] - imag_part * sine_row[None, :]
    shifted_imag = real_part * sine_row[None, :] + imag_part * cosine_row[None, :]
    return jnp.concatenate([shifted_real, shifted_imag], axis=1).astype(jnp.bfloat16)


def ref_energy(ref_rows, gain_table):
    pixels = CROP * HALF
    real_part = ref_rows[:, :pixels].astype(jnp.float32)
    imag_part = ref_rows[:, pixels:].astype(jnp.float32)
    magnitude = real_part * real_part + imag_part * imag_part
    return lax.dot_general(gain_table, magnitude, (((1,), (1,)), ((), ())), precision=lax.Precision.HIGHEST, preferred_element_type=jnp.float32)


def prior_terms(row_index, psi_prev, earlier_direction_range, view_table):
    psi_rows = row_index % PSI_STEPS
    angular_separation = jnp.abs(psi_rows[None, :] - psi_prev[:, None])
    angular_separation = jnp.minimum(angular_separation, PSI_STEPS - angular_separation).astype(jnp.float32)
    views = row_index // PSI_STEPS
    view_ids = jnp.arange(view_table.shape[0], dtype=jnp.int32)
    row_span = jnp.sum(jnp.where(views[:, None] == view_ids[None, :], view_table[None, :], 0), axis=1)
    prior_reward = jnp.where(row_span[None, :] == earlier_direction_range[:, None], jnp.float32(range_reward), jnp.float32(0.0))
    return prior_reward - angular_separation * angular_separation * jnp.float32(0.5 / (inplane_angle_width * inplane_angle_width))


def combine_scores(cross, energy, ctf_class, prior):
    penalty = 0.5 * jnp.take(energy, ctf_class, axis=0)
    return (cross - penalty[None, :, :]) + prior[None, :, :]


def insert_images(posterior, aligned, offset_cos, offset_sin):
    pixels = CROP * HALF

    def add_offset(offset, total):
        weights_now = posterior[offset]
        summed = lax.dot_general(weights_now, aligned, (((0,), (0,)), ((), ())), preferred_element_type=jnp.float32)
        cosine_row = offset_cos[offset][None, :]
        sine_row = offset_sin[offset][None, :]
        summed_real = summed[:, :pixels]
        imaginary_total = summed[:, pixels:]
        turned = jnp.concatenate([summed_real * cosine_row + imaginary_total * sine_row, imaginary_total * cosine_row - summed_real * sine_row], axis=1)
        return total + turned

    initial = jnp.zeros((posterior.shape[2], 2 * pixels), jnp.float32)
    return lax.fori_loop(0, OFFSETS, add_offset, initial)


def class_mass(posterior, ctf_class):
    particle_mass = jnp.sum(posterior.astype(jnp.float32), axis=0)
    onehot_table = (ctf_class[:, None] == jnp.arange(CTF_GROUPS, dtype=jnp.int32)[None, :]).astype(jnp.float32)
    return lax.dot_general(particle_mass, onehot_table, (((0,), (0,)), ((), ())), precision=lax.Precision.HIGHEST, preferred_element_type=jnp.float32)


def reference(images, refs, ctf, noise_var, shifts, ctf_class, psi_prev, earlier_direction_range, view_range):
    aligned = align_images(images, shifts, ctf_class, ctf, noise_var)
    offset_cos, offset_sin = offset_tables()
    gain_table = ctf * ctf / noise_var[None, :]
    shifted = lax.map(lambda tables: shift_block(refs, tables[0], tables[1]), (offset_cos, offset_sin))
    energy = ref_energy(refs, gain_table)
    row_index = jnp.arange(REFS, dtype=jnp.int32)
    blocks = PARTICLES // PART_DEV

    def step(carry, block_payload):
        class_total, mass_total = carry
        block_aligned, block_class, block_psi, block_range = block_payload
        cross = lax.map(lambda refs_now: lax.dot_general(block_aligned, refs_now, (((1,), (1,)), ((), ())), preferred_element_type=jnp.float32), shifted)
        scores = combine_scores(cross, energy, block_class, prior_terms(row_index, block_psi, block_range, view_range))
        top = jnp.max(scores, axis=(0, 2))
        total = jnp.sum(jnp.exp(scores - top[None, :, None]), axis=(0, 2))
        log_norm = top + jnp.log(total)
        peak_prob = jnp.exp(top - log_norm)
        posterior = jnp.exp(scores - log_norm[None, :, None]).astype(jnp.bfloat16)
        class_total = class_total + insert_images(posterior, block_aligned, offset_cos, offset_sin)
        mass_total = mass_total + class_mass(posterior, block_class)
        return (class_total, mass_total), (log_norm, peak_prob)

    initial = (jnp.zeros((REFS, FEAT), jnp.float32), jnp.zeros((REFS, CTF_GROUPS), jnp.float32))
    blocked = (aligned.reshape(blocks, PART_DEV, FEAT), ctf_class.reshape(blocks, PART_DEV), psi_prev.reshape(blocks, PART_DEV), earlier_direction_range.reshape(blocks, PART_DEV))
    (class_sums, mass_sums), (log_norm, peak_prob) = lax.scan(step, initial, blocked)
    weight_sums = jnp.dot(mass_sums, gain_table, precision=lax.Precision.HIGHEST)
    return class_sums, weight_sums, log_norm.reshape(PARTICLES), peak_prob.reshape(PARTICLES)
```

```python
import math

import jax
import jax.numpy as jnp
import numpy as np
from jax import lax
from jax.experimental import pallas as pl
from jax.experimental.pallas import tpu as pltpu
from jax.sharding import PartitionSpec as P

CROP = 64
HALF = 32
PIX = 2048
OFFSETS = 9
GROUPS = 64
N = 256
BLOCKS = 32
HP = 1024
WIDTHS = (HP + 128, HP)
THETA = 2.0 * math.pi / CROP

F32 = jnp.float32
BF16 = jnp.bfloat16
MESH = pl.DeviceIdType.MESH

PAIRS = ((0, 1), (1, 0), (1, 1), (1, -1))


def offset_index(ty, tx):
    return (ty + 1) * 3 + (tx + 1)


def phase_constants():
    pixels = np.arange(PIX)
    alpha = THETA * (pixels // HALF)
    beta = THETA * (pixels % HALF)
    rows = []
    for ty, tx in PAIRS:
        angle = ty * alpha + tx * beta
        rows += [np.cos(angle), np.sin(angle)]
    ca, sa, cb, sb = np.cos(alpha), np.sin(alpha), np.cos(beta), np.sin(beta)
    rows += [cb, ca, ca * cb, -sa * sb, sb, ca * sb, sa, sa * cb]
    return np.stack(rows).astype(np.float32)


def cos_sin(index):
    m = jnp.bitwise_and(index, 63) + 8
    quarter = jnp.bitwise_and(jnp.right_shift(m, 4), 3)
    x = (jnp.bitwise_and(m, 15) - 8).astype(F32) * F32(THETA)
    x2 = x * x
    c = 1.0 + x2 * (-0.5 + x2 * (1 / 24 + x2 * (-1 / 720 + x2 * (1 / 40320))))
    s = x * (1.0 + x2 * (-1 / 6 + x2 * (1 / 120 + x2 * (-1 / 5040 + x2 * (1 / 362880)))))
    odd = jnp.bitwise_and(quarter, 1) == 1
    cc = jnp.where(odd, s, c)
    ss = jnp.where(odd, c, s)
    cos = jnp.where((quarter == 1) | (quarter == 2), -cc, cc)
    sin = jnp.where(quarter >= 2, -ss, ss)
    return cos, sin


def split3(value):
    high = value.astype(BF16)
    rest = value - high.astype(F32)
    middle = rest.astype(BF16)
    low = (rest - middle.astype(F32)).astype(BF16)
    return high, middle, low


def dot(a, b, dims):
    return lax.dot_general(a, b, (dims, ((), ())), preferred_element_type=F32)


def ring(i):
    return lax.rem(i + 8, 4)


def kernel(
    images_ref, refs_ref, ctf_ref, noise_ref, ints_ref, views_ref, table_ref,
    sums_ref, weights_ref, norm_ref, peak_ref,
    img, ctf, g_a, g_b, al_a, al_b, wsel, spin, s_a, s_b, mag, gain, en, onehot_t,
    sc, massn, l_a, l_b, rp_a, rp_b,
    st, sb_a, sb_b, rb_a, rb_b, sb2_a, sb2_b, rb2_a, rb2_b, sb3_a, sb3_b, rb3_a, rb3_b,
    load_sem, ag_send, ag_recv, dir_send, dir_recv, rs_send, rs_recv,
):
    g = (g_a, g_b)
    al = (al_a, al_b)
    s_buf = (s_a, s_b)
    l_buf = (l_a, l_b)
    rp = (rp_a, rp_b)
    sb, rb = (sb_a, sb_b), (rb_a, rb_b)
    sb2, rb2 = (sb2_a, sb2_b), (rb2_a, rb2_b)
    sb3, rb3 = (sb3_a, sb3_b), (rb3_a, rb3_b)

    me_dir = lax.axis_index("dir")
    me_dom = lax.axis_index("dom")
    y = me_dom // 8
    z = lax.rem(me_dom // 4, 2)
    x = lax.rem(me_dom, 4)

    def device(yy, zz, xx):
        return (me_dir, (yy * 2 + zz) * 4 + xx)

    x_up, x_down = device(y, z, ring(x + 1)), device(y, z, ring(x - 1))
    y_up, y_down = device(ring(y + 1), z, x), device(ring(y - 1), z, x)
    z_other = device(y, 1 - z, x)
    dir_peers = [(lax.rem(me_dir + o, 8), me_dom) for o in range(1, 8)]

    c2, c1 = (y, x), (x, y)
    up2, down2 = (y_up, x_up), (y_down, x_down)
    up1, down1 = (x_up, y_up), (x_down, y_down)

    def rel(r):
        return lax.rem(z + r, 2)

    load_images = pltpu.make_async_copy(images_ref, img, load_sem.at[0])
    load_images.start()
    load_ctf = pltpu.make_async_copy(ctf_ref, ctf, load_sem.at[1])
    load_ctf.start()

    barrier = pltpu.get_barrier_semaphore()
    partners = [z_other, x_up, x_down, y_up, y_down] + dir_peers
    for p in partners:
        pl.semaphore_signal(barrier, inc=1, device_id=p, device_id_type=MESH)

    for h in range(2):
        real = refs_ref[:, h * HP:(h + 1) * HP].astype(F32)
        imag = refs_ref[:, PIX + h * HP:PIX + (h + 1) * HP].astype(F32)
        g[h][c2[h], z, c1[h]] = jnp.concatenate([real, imag], axis=0).astype(BF16)

    pl.semaphore_wait(barrier, len(partners))

    def ag_copy(h, k, ref, target):
        return pltpu.make_async_remote_copy(
            src_ref=ref, dst_ref=ref, send_sem=ag_send.at[h, k], recv_sem=ag_recv.at[h, k],
            device_id=target, device_id_type=MESH,
        )

    def block(h, r, d):
        return g[h].at[c2[h], rel(r), ring(c1[h] + d)]

    def slab(h, r, d):
        return g[h].at[ring(c2[h] + d), rel(r)]

    def ag(h, k):
        if k == 0:
            return ag_copy(h, k, block(h, 0, 0), z_other)
        if k == 1:
            return ag_copy(h, k, block(h, 0, 0), up1[h])
        if k == 2:
            return ag_copy(h, k, block(h, 1, 0), up1[h])
        if k == 3:
            return ag_copy(h, k, block(h, 0, -1), up1[h])
        if k == 4:
            return ag_copy(h, k, block(h, 0, 0), down1[h])
        if k == 5:
            return ag_copy(h, k, block(h, 1, 0), down1[h])
        if k == 6:
            return ag_copy(h, k, block(h, 1, 1), down1[h])
        if k == 7:
            return ag_copy(h, k, slab(h, 0, 0), up2[h])
        if k == 8:
            return ag_copy(h, k, slab(h, 1, 0), up2[h])
        if k == 9:
            return ag_copy(h, k, slab(h, 0, -1), up2[h])
        if k == 10:
            return ag_copy(h, k, slab(h, 1, 0), down2[h])
        if k == 11:
            return ag_copy(h, k, slab(h, 0, 0), down2[h])
        return ag_copy(h, k, slab(h, 1, 1), down2[h])

    def ag_start(*ks):
        for k in ks:
            for h in range(2):
                ag(h, k).start()

    def ag_wait(*ks):
        for k in ks:
            for h in range(2):
                ag(h, k).wait_recv()

    ag_start(0, 1, 4)

    classes = ints_ref[0:1, :]
    psi_prev = ints_ref[1:2, :]
    ranges = ints_ref[2:3, :]

    def column(row):
        wide = jnp.broadcast_to(row.astype(F32), (128, N))
        return jnp.transpose(wide).astype(jnp.int32)

    shift_y = column(ints_ref[3:4, :])
    shift_x = column(ints_ref[4:5, :])
    lane = lax.broadcasted_iota(jnp.int32, (N, 128), 1)
    fc, fs = cos_sin(
        jnp.bitwise_and(lane, 31) * shift_x + jnp.right_shift(lane, 5) * shift_y
    )
    spin[0], spin[1] = fc, fs
    rc, rs = cos_sin(4 * shift_y)
    spin[2], spin[3] = rc, rs
    qc, qs = cos_sin(16 * shift_y)
    spin[4], spin[5] = qc, qs

    class_rows = lax.broadcasted_iota(jnp.int32, (128, N), 0)
    mask_t = (class_rows == classes).astype(F32)
    onehot_t[...] = mask_t.astype(BF16)
    onehot = jnp.transpose(mask_t).astype(BF16)

    load_ctf.wait()
    noise = noise_ref[...]
    for j in range(8):
        lanes = slice(j * 256, (j + 1) * 256)
        ctf_now = ctf[:, lanes]
        noise_now = noise[:, lanes]
        gain_now = ctf_now * ctf_now / noise_now
        gain[0:GROUPS, lanes] = gain_now
        gain[GROUPS:128, lanes] = jnp.zeros_like(gain_now)
        high, middle, low = split3(ctf_now / noise_now)
        pick = onehot[:, 0:GROUPS]
        wsel[:, lanes] = (
            dot(pick, high, ((1,), (0,))) + dot(pick, middle, ((1,), (0,)))
        ) + dot(pick, low, ((1,), (0,)))

    ag_wait(0)
    ag_start(5, 2)

    load_images.wait()

    def align(part, carry):
        rows = pl.ds(pl.multiple_of(part * 32, 32), 32)
        base_c, base_s = [spin[0, rows]], [spin[1, rows]]
        step_c, step_s = spin[2, rows], spin[3, rows]
        turn_c, turn_s = spin[4, rows], spin[5, rows]
        for j in range(16):
            if j == 0:
                c, s = base_c[0], base_s[0]
            elif j < 4:
                pc, ps = base_c[j - 1], base_s[j - 1]
                c, s = pc * step_c - ps * step_s, ps * step_c + pc * step_s
                base_c.append(c)
                base_s.append(s)
            else:
                pc, ps = base_c[j % 4], base_s[j % 4]
                c, s = pc * turn_c - ps * turn_s, ps * turn_c + pc * turn_s
                base_c[j % 4], base_s[j % 4] = c, s
            lanes = slice(j * 128, (j + 1) * 128)
            real = img[rows, lanes].astype(F32)
            imag = img[rows, PIX + j * 128:PIX + (j + 1) * 128].astype(F32)
            weight = wsel[rows, lanes]
            h, jj = j // 8, j % 8
            al[h][rows, jj * 128:(jj + 1) * 128] = ((real * c + imag * s) * weight).astype(BF16)
            al[h][rows, HP + jj * 128:HP + (jj + 1) * 128] = (
                (imag * c - real * s) * weight
            ).astype(BF16)
        return carry

    lax.fori_loop(0, 3, align, 0)
    ag_wait(1)
    ag_start(3)
    ag_wait(5)
    ag_start(6)
    lax.fori_loop(3, 6, align, 0)
    ag_wait(4, 3)
    ag_start(7, 11)
    ag_wait(2, 6)
    ag_start(10, 8)
    lax.fori_loop(6, 8, align, 0)

    def cross_chunk(h, now):
        for j in range(8):
            lanes = slice(j * 128, (j + 1) * 128)
            wide = slice(h * HP + j * 128, h * HP + (j + 1) * 128)
            value = g[h][now, :, :, :, lanes].astype(F32).reshape(8, 16, 128)
            real, imag = value[:, 0:8], value[:, 8:16]
            mag[:, lanes] = (real * real + imag * imag).reshape(64, 128)

            def put(t, shifted_real, shifted_imag):
                rows = slice(t * 64, (t + 1) * 64)
                s_buf[h][rows, lanes] = shifted_real.reshape(64, 128).astype(BF16)
                s_buf[h][rows, HP + j * 128:HP + (j + 1) * 128] = (
                    shifted_imag.reshape(64, 128).astype(BF16)
                )

            put(4, real, imag)
            for q, (ty, tx) in enumerate(PAIRS):
                c = table_ref[2 * q:2 * q + 1, wide][None]
                s = table_ref[2 * q + 1:2 * q + 2, wide][None]
                rc_, is_, rs_, ic_ = real * c, imag * s, real * s, imag * c
                put(offset_index(ty, tx), rc_ - is_, rs_ + ic_)
                put(offset_index(-ty, -tx), rc_ + is_, ic_ - rs_)
        en[h, now] = lax.dot_general(
            mag[...], gain[:, h * HP:(h + 1) * HP], (((1,), (1,)), ((), ())),
            precision=lax.Precision.HIGHEST, preferred_element_type=F32,
        ).reshape(8, 8, 128)
        sc[h, now] = dot(s_buf[h][...], al[h][...], ((1,), (1,))).reshape(OFFSETS, 8, 8, N)

    def cross_step(i, carry):
        @pl.when(i == 1)
        def _():
            ag_wait(7)
            ag_start(9)
            ag_wait(10)
            ag_start(12)
            ag_wait(8, 11)

        @pl.when(i == 3)
        def _():
            ag_wait(9, 12)

        ahead = lax.rem((i * (i + 1)) // 2, 4)
        for h in range(2):
            cross_chunk(h, ring(c2[h] + ahead))
        return carry

    lax.fori_loop(0, 4, cross_step, 0)

    psi_rows = lax.broadcasted_iota(jnp.int32, (16, N), 0)
    apart = jnp.abs(psi_rows - psi_prev)
    apart = jnp.minimum(apart, 16 - apart).astype(F32)
    psi_term = -(apart * apart * F32(0.5 / 9.0))

    def score_pass(yy, top):
        for zz in range(2):
            for xp in range(2):
                rows = [
                    en[0, yy, zz * 4 + 2 * xp + xx] + en[1, 2 * xp + xx, zz * 4 + yy]
                    for xx in range(2)
                ]
                high, middle, low = split3(jnp.concatenate(rows, axis=0))
                picked = (
                    dot(high, onehot_t[...], ((1,), (0,)))
                    + dot(middle, onehot_t[...], ((1,), (0,)))
                ) + dot(low, onehot_t[...], ((1,), (0,)))
                view = views_ref[yy * 4 + zz * 2 + xp]
                reward = jnp.where(ranges == view, F32(1.5), F32(0.0))
                prior = psi_term + reward
                penalty = 0.5 * picked
                for xx in range(2):
                    part = slice(xx * 8, (xx + 1) * 8)
                    for t in range(OFFSETS):
                        value = (
                            sc[0, yy, t, zz * 4 + 2 * xp + xx]
                            + sc[1, 2 * xp + xx, t, zz * 4 + yy]
                        )
                        value = (value - penalty[part]) + prior[part]
                        sc[0, yy, t, zz * 4 + 2 * xp + xx] = value
                        top = jnp.maximum(top, value)
        return top

    top = lax.fori_loop(0, 4, score_pass, jnp.full((8, N), -jnp.inf, F32))
    top = jnp.max(top, axis=0, keepdims=True)

    def exp_pass(yy, total):
        for t in range(OFFSETS):
            for b in range(8):
                value = jnp.exp(sc[0, yy, t, b] - top)
                sc[0, yy, t, b] = value
                total = total + value
        return total

    total = lax.fori_loop(0, 4, exp_pass, jnp.zeros((8, N), F32))
    total = jnp.sum(total, axis=0, keepdims=True)

    st[me_dir] = jnp.concatenate(
        [jnp.broadcast_to(top, (8, N)), jnp.broadcast_to(total, (8, N))], axis=0
    )

    def dir_copy(o):
        return pltpu.make_async_remote_copy(
            src_ref=st.at[me_dir], dst_ref=st.at[me_dir], send_sem=dir_send.at[o - 1],
            recv_sem=dir_recv.at[o - 1], device_id=dir_peers[o - 1], device_id_type=MESH,
        )

    def dir_arrival(o):
        source = lax.rem(me_dir + 8 - o, 8)
        return pltpu.make_async_remote_copy(
            src_ref=st.at[source], dst_ref=st.at[source], send_sem=dir_send.at[o - 1],
            recv_sem=dir_recv.at[o - 1], device_id=dir_peers[o - 1], device_id_type=MESH,
        )

    for o in range(1, 8):
        dir_copy(o).start()
    for o in range(1, 8):
        dir_arrival(o).wait_recv()

    best = st[0, 0:1]
    for d in range(1, 8):
        best = jnp.maximum(best, st[d, 0:1])
    mass_all = st[0, 8:9] * jnp.exp(st[0, 0:1] - best)
    for d in range(1, 8):
        mass_all = mass_all + st[d, 8:9] * jnp.exp(st[d, 0:1] - best)
    log_norm = best + jnp.log(mass_all)
    norm_ref[...] = log_norm
    peak_ref[...] = jnp.exp(best - log_norm)
    factor = jnp.exp(top - log_norm)

    def posterior_pass(yy, carry):
        for b in range(8):
            p = [
                (sc[0, yy, t, b] * factor).astype(BF16).astype(F32) for t in range(OFFSETS)
            ]
            by_row = []
            for ty in range(3):
                minus, zero, plus = p[3 * ty], p[3 * ty + 1], p[3 * ty + 2]
                by_row.append((zero, plus + minus, plus - minus))
            out = []
            for k in range(3):
                minus, zero, plus = by_row[0][k], by_row[1][k], by_row[2][k]
                out.append((zero, plus + minus, plus - minus))
            order = (
                out[0][0], out[1][0], out[0][1], out[1][1], out[2][2],
                out[2][0], out[2][1], out[0][2], out[1][2],
            )
            for k in range(OFFSETS):
                sc[1, yy, k, b] = order[k]
            massn[yy, b] = (out[0][0] + out[1][0]) + (out[0][1] + out[1][1])
        return carry

    lax.fori_loop(0, 4, posterior_pass, 0)

    def insert_chunk(h, i, now):
        for zz in range(2):
            for cp in range(2):
                pair = []
                for c in range(2):
                    cc = 2 * cp + c
                    if h == 0:
                        pair.append(sc[1, now, :, zz * 4 + cc])
                    else:
                        pair.append(sc[1, cc, :, zz * 4 + now])
                l_buf[h][:, zz * 2 + cp] = jnp.concatenate(pair, axis=1).astype(BF16)
        left = l_buf[h][...].reshape(OFFSETS * 64, N)
        for q in range(4):
            lanes = slice(q * 256, (q + 1) * 256)
            wide = slice(h * HP + q * 256, h * HP + (q + 1) * 256)
            real = dot(left, al[h][:, lanes], ((1,), (0,))).reshape(OFFSETS, 64, 256)
            imag = dot(
                left, al[h][:, HP + q * 256:HP + (q + 1) * 256], ((1,), (0,))
            ).reshape(OFFSETS, 64, 256)
            total_real, total_imag = real[0], imag[0]
            for k in range(4):
                w = table_ref[8 + k:9 + k, wide]
                total_real = total_real + w * real[1 + k]
                total_imag = total_imag + w * imag[1 + k]
            for k in range(4):
                w = table_ref[12 + k:13 + k, wide]
                total_real = total_real + w * imag[5 + k]
                total_imag = total_imag - w * real[5 + k]
            rp[h][i, :, 0:8, lanes] = total_real.reshape(8, 8, 256)
            rp[h][i, :, 8:16, lanes] = total_imag.reshape(8, 8, 256)
        if h == 0:
            high, middle, _ = split3(massn[now].reshape(64, N))
            masses = dot(high, onehot_t[...], ((1,), (1,))) + dot(
                middle, onehot_t[...], ((1,), (1,))
            )
            rp[h][i, :, 0:8, HP:HP + 128] = masses.reshape(8, 8, 128)
            rp[h][i, :, 8:16, HP:HP + 128] = jnp.zeros((8, 8, 128), F32)

    def rs_copy(h, k, src, dst, target):
        return pltpu.make_async_remote_copy(
            src_ref=src, dst_ref=dst, send_sem=rs_send.at[h, k], recv_sem=rs_recv.at[h, k],
            device_id=target, device_id_type=MESH,
        )

    def rs(h, k):
        if k < 6:
            target = up2[h] if k < 3 else down2[h]
            return rs_copy(h, k, sb[h].at[k], rb[h].at[k], target)
        if k < 12:
            target = up1[h] if k < 9 else down1[h]
            return rs_copy(h, k, sb2[h].at[k - 6], rb2[h].at[k - 6], target)
        return rs_copy(h, k, sb3[h], rb3[h], z_other)

    def send_half(h, k, i, zz, add=None):
        part = rp[h][i, zz * 4:(zz + 1) * 4]
        if add is not None:
            part = part + rb[h][add].astype(F32)
        sb[h][k] = part.astype(BF16)
        rs(h, k).start()

    def insert_step(i, carry):
        back = 3 - i
        ahead = lax.rem((back * (back + 1)) // 2, 4)
        for h in range(2):
            insert_chunk(h, i, ring(c2[h] + ahead))

            @pl.when(i == 0)
            def _():
                send_half(h, 0, 0, 0)
                send_half(h, 3, 0, 1)

            @pl.when(i == 1)
            def _():
                send_half(h, 4, 1, 0)

            @pl.when(i == 2)
            def _():
                send_half(h, 1, 2, 1)
                rs(h, 0).wait_recv()
                send_half(h, 2, 2, 0, add=0)
                rs(h, 3).wait_recv()
                send_half(h, 5, 1, 1, add=3)

        return carry

    lax.fori_loop(0, 4, insert_step, 0)

    for h in range(2):
        for k in (1, 2, 4, 5):
            rs(h, k).wait_recv()
        for zz, (from_below, from_above) in enumerate(((2, 4), (1, 5))):
            part = slice(zz * 4, (zz + 1) * 4)
            rp[h][3, part] = (
                rp[h][3, part] + rb[h][from_below].astype(F32)
            ) + rb[h][from_above].astype(F32)

        far, above, below = ring(c1[h] + 2), ring(c1[h] + 1), ring(c1[h] - 1)
        for k, zz, cc in ((6, 0, far), (9, 1, far), (7, 1, above), (10, 0, below)):
            sb2[h][k - 6] = rp[h][3, zz * 4 + cc].astype(BF16)
            rs(h, k).start()

    for h in range(2):
        far, above, below = ring(c1[h] + 2), ring(c1[h] + 1), ring(c1[h] - 1)
        for k, zz, cc, add in ((8, 0, above, 6), (11, 1, below, 9)):
            rs(h, add).wait_recv()
            sb2[h][k - 6] = (
                rp[h][3, zz * 4 + cc] + rb2[h][add - 6].astype(F32)
            ).astype(BF16)
            rs(h, k).start()

    own = []
    for h in range(2):
        for k in (7, 8, 10, 11):
            rs(h, k).wait_recv()
        sums = []
        for zz, (from_below, from_above) in enumerate(((8, 10), (7, 11))):
            sums.append(
                (rp[h][3, zz * 4 + c1[h]] + rb2[h][from_below - 6].astype(F32))
                + rb2[h][from_above - 6].astype(F32)
            )
        is_low = z == 0
        mine = jnp.where(is_low, sums[0], sums[1])
        sb3[h][...] = jnp.where(is_low, sums[1], sums[0]).astype(BF16)
        rs(h, 12).start()
        own.append(mine)

    for h in range(2):
        rs(h, 12).wait_recv()
        result = own[h] + rb3[h][...].astype(F32)
        sums_ref[:, h * HP:(h + 1) * HP] = result[0:8, 0:HP]
        sums_ref[:, PIX + h * HP:PIX + (h + 1) * HP] = result[8:16, 0:HP]
        if h == 0:
            weights_ref[...] = lax.dot_general(
                result[0:8, HP:HP + 128], gain[...], (((1,), (0,)), ((), ())),
                precision=lax.Precision.HIGHEST, preferred_element_type=F32,
            )

    for h in range(2):
        for k in range(13):
            ag(h, k).wait_send()
            rs(h, k).wait_send()
    for o in range(1, 8):
        dir_copy(o).wait_send()


def per_device(
    images, refs, ctf, noise_var, shifts, ctf_class, psi_prev, earlier_direction_range, view_range
):
    ints = jnp.stack(
        [ctf_class, psi_prev, earlier_direction_range, shifts[:, 0], shifts[:, 1]]
    )
    vmem = pl.BlockSpec(memory_space=pltpu.VMEM)
    hbm = pl.BlockSpec(memory_space=pl.ANY)
    smem = pl.BlockSpec(memory_space=pltpu.SMEM)
    wa, wb = WIDTHS
    dma = pltpu.SemaphoreType.DMA
    out = pl.pallas_call(
        kernel,
        out_shape=(
            jax.ShapeDtypeStruct((8, 2 * PIX), F32),
            jax.ShapeDtypeStruct((8, PIX), F32),
            jax.ShapeDtypeStruct((1, N), F32),
            jax.ShapeDtypeStruct((1, N), F32),
        ),
        in_specs=[hbm, vmem, hbm, vmem, vmem, smem, vmem],
        out_specs=(vmem, vmem, vmem, vmem),
        scratch_shapes=[
            pltpu.VMEM((N, 2 * PIX), BF16),
            pltpu.VMEM((GROUPS, PIX), F32),
            pltpu.VMEM((4, 2, 4, 16, HP), BF16),
            pltpu.VMEM((4, 2, 4, 16, HP), BF16),
            pltpu.VMEM((N, 2 * HP), BF16),
            pltpu.VMEM((N, 2 * HP), BF16),
            pltpu.VMEM((N, PIX), F32),
            pltpu.VMEM((6, N, 128), F32),
            pltpu.VMEM((OFFSETS * 64, 2 * HP), BF16),
            pltpu.VMEM((OFFSETS * 64, 2 * HP), BF16),
            pltpu.VMEM((64, HP), F32),
            pltpu.VMEM((128, PIX), F32),
            pltpu.VMEM((2, 4, 8, 8, 128), F32),
            pltpu.VMEM((128, N), BF16),
            pltpu.VMEM((2, 4, OFFSETS, 8, 8, N), F32),
            pltpu.VMEM((4, 8, 8, N), F32),
            pltpu.VMEM((OFFSETS, 4, 16, N), BF16),
            pltpu.VMEM((OFFSETS, 4, 16, N), BF16),
            pltpu.VMEM((4, 8, 16, wa), F32),
            pltpu.VMEM((4, 8, 16, wb), F32),
            pltpu.VMEM((8, 16, N), F32),
            pltpu.VMEM((6, 4, 16, wa), BF16),
            pltpu.VMEM((6, 4, 16, wb), BF16),
            pltpu.VMEM((6, 4, 16, wa), BF16),
            pltpu.VMEM((6, 4, 16, wb), BF16),
            pltpu.VMEM((6, 16, wa), BF16),
            pltpu.VMEM((6, 16, wb), BF16),
            pltpu.VMEM((6, 16, wa), BF16),
            pltpu.VMEM((6, 16, wb), BF16),
            pltpu.VMEM((16, wa), BF16),
            pltpu.VMEM((16, wb), BF16),
            pltpu.VMEM((16, wa), BF16),
            pltpu.VMEM((16, wb), BF16),
            dma((2,)),
            dma((2, 13)),
            dma((2, 13)),
            dma((7,)),
            dma((7,)),
            dma((2, 13)),
            dma((2, 13)),
        ],
        compiler_params=pltpu.CompilerParams(
            collective_id=0, has_side_effects=True, vmem_limit_bytes=60 * 2**20
        ),
        cost_estimate=pl.CostEstimate(
            flops=10_000_000_000, bytes_accessed=4_000_000, transcendentals=600_000
        ),
        name="expectation_step",
    )(
        images, refs, ctf, noise_var.reshape(1, PIX), ints, view_range,
        jnp.asarray(phase_constants()),
    )
    class_sums, weight_sums, log_norm, peak_prob = out
    return class_sums, weight_sums, log_norm.reshape(N), peak_prob.reshape(N)


def solution(mesh):
    placed = (
        P("dom", None),
        P(("dir", "dom"), None),
        P(),
        P(),
        P("dom", None),
        P("dom"),
        P("dom"),
        P("dom"),
        P("dir"),
    )
    return jax.shard_map(
        per_device,
        mesh=mesh,
        in_specs=placed,
        out_specs=(P(("dir", "dom"), None), P(("dir", "dom"), None), P("dom"), P("dom")),
        check_vma=False,
    )
```

```python
import math

import jax
import jax.numpy as jnp
import numpy as np
from jax import lax
from jax.experimental import pallas as pl
from jax.experimental.pallas import tpu as pltpu
from jax.sharding import PartitionSpec as P

CROP = 64
HALF = 32
PIX = 2048
OFFSETS = 9
GROUPS = 64
N = 256
BLOCKS = 32
HP = 1024
WIDTHS = (HP + 128, HP)
THETA = 2.0 * math.pi / CROP

F32 = jnp.float32
BF16 = jnp.bfloat16
MESH = pl.DeviceIdType.MESH

PAIRS = ((0, 1), (1, 0), (1, 1), (1, -1))


def offset_index(ty, tx):
    return (ty + 1) * 3 + (tx + 1)


def phase_constants():
    pixels = np.arange(PIX)
    alpha = THETA * (pixels // HALF)
    beta = THETA * (pixels % HALF)
    rows = []
    for ty, tx in PAIRS:
        angle = ty * alpha + tx * beta
        rows += [np.cos(angle), np.sin(angle)]
    ca, sa, cb, sb = np.cos(alpha), np.sin(alpha), np.cos(beta), np.sin(beta)
    rows += [cb, ca, ca * cb, -sa * sb, sb, ca * sb, sa, sa * cb]
    return np.stack(rows).astype(np.float32)


def cos_sin(index):
    m = jnp.bitwise_and(index, 63) + 8
    quarter = jnp.bitwise_and(jnp.right_shift(m, 4), 3)
    x = (jnp.bitwise_and(m, 15) - 8).astype(F32) * F32(THETA)
    x2 = x * x
    c = 1.0 + x2 * (-0.5 + x2 * (1 / 24 + x2 * (-1 / 720 + x2 * (1 / 40320))))
    s = x * (1.0 + x2 * (-1 / 6 + x2 * (1 / 120 + x2 * (-1 / 5040 + x2 * (1 / 362880)))))
    odd = jnp.bitwise_and(quarter, 1) == 1
    cc = jnp.where(odd, s, c)
    ss = jnp.where(odd, c, s)
    cos = jnp.where((quarter == 1) | (quarter == 2), -cc, cc)
    sin = jnp.where(quarter >= 2, -ss, ss)
    return cos, sin


def split3(value):
    high = value.astype(BF16)
    rest = value - high.astype(F32)
    middle = rest.astype(BF16)
    low = (rest - middle.astype(F32)).astype(BF16)
    return high, middle, low


def dot(a, b, dims):
    return lax.dot_general(a, b, (dims, ((), ())), preferred_element_type=F32)


def ring(i):
    return lax.rem(i + 8, 4)


def ahead_of(place):
    return lax.rem((place * (place + 1)) // 2, 4)


PIECES = (slice(0, 1), slice(1, 3), slice(3, 4))
PARTS = (slice(1, 4), slice(0, 1))


def kernel(
    images_ref, refs_ref, ctf_ref, noise_ref, class_ref, psi_ref, range_ref, shift_ref,
    views_ref, table_in,
    sums_ref, weights_ref, stats_ref,
    img, refs_in, ctf, noise_in, ints, shift_in, table_ref,
    g_a, g_b, al_a, al_b, wsel, spin, s_a, s_b, mag, gain, gain3, en, onehot_t, psi_rows_sc,
    sc, massn, l_a, l_b, rp_a, rp_b,
    st, sb_a, sb_b, rb_a, rb_b, sb2_a, sb2_b, rb2_a, rb2_b, sb3_a, sb3_b, rb3_a, rb3_b,
    load_sem, ag_send, ag_recv, dir_send, dir_recv, rs_send, rs_recv,
):
    g = (g_a, g_b)
    al = (al_a, al_b)
    s_buf = (s_a, s_b)
    l_buf = (l_a, l_b)
    rp = (rp_a, rp_b)
    sb, rb = (sb_a, sb_b), (rb_a, rb_b)
    sb2, rb2 = (sb2_a, sb2_b), (rb2_a, rb2_b)
    sb3, rb3 = (sb3_a, sb3_b), (rb3_a, rb3_b)

    me_dir = lax.axis_index("dir")
    me_dom = lax.axis_index("dom")
    y = me_dom // 8
    z = lax.rem(me_dom // 4, 2)
    x = lax.rem(me_dom, 4)

    def device(yy, zz, xx):
        return (me_dir, (yy * 2 + zz) * 4 + xx)

    x_up, x_down = device(y, z, ring(x + 1)), device(y, z, ring(x - 1))
    y_up, y_down = device(ring(y + 1), z, x), device(ring(y - 1), z, x)
    z_other = device(y, 1 - z, x)
    dir_peers = [(lax.rem(me_dir + o, 8), me_dom) for o in range(1, 8)]

    up2, down2 = (y_up, x_up), (y_down, x_down)
    up1, down1 = (x_up, y_up), (x_down, y_down)

    barrier = pltpu.get_barrier_semaphore()
    partners = [z_other, x_up, x_down, y_up, y_down] + dir_peers
    for p in partners:
        pl.semaphore_signal(barrier, inc=1, device_id=p, device_id_type=MESH)

    loads = [
        pltpu.make_async_copy(src, dst, load_sem.at[k])
        for k, (src, dst) in enumerate((
            (refs_ref, refs_in), (shift_ref, shift_in), (class_ref, ints.at[0:1]),
            (psi_ref, ints.at[1:2]), (range_ref, ints.at[2:3]), (noise_ref, noise_in),
            (ctf_ref, ctf), (images_ref, img), (table_in, table_ref),
        ))
    ]
    for load in loads:
        load.start()

    loads[0].wait()
    for h in range(2):
        real = refs_in[:, h * HP:(h + 1) * HP].astype(F32)
        imag = refs_in[:, PIX + h * HP:PIX + (h + 1) * HP].astype(F32)
        g[h][0, 0, 0] = jnp.concatenate([real, imag], axis=0).astype(BF16)

    pl.semaphore_wait(barrier, len(partners))

    def ag(h, k):
        buf = g[h]
        if k == 0:
            src, dst, target = buf.at[0, 0, 0], buf.at[0, 1, 0], z_other
        elif k < 7:
            kind = (k - 1) % 3
            upward = k < 4
            target = up1[h] if upward else down1[h]
            side = 2 if upward else 1
            if kind < 2:
                src, dst = buf.at[0, kind, 0], buf.at[0, kind, side]
            else:
                r = 0 if upward else 1
                src, dst = buf.at[0, r, side], buf.at[0, r, 3]
        else:
            piece = PIECES[(k - 7) % 3]
            kind = (k - 7) // 3
            upward = kind < 3
            target = up2[h] if upward else down2[h]
            side = 2 if upward else 1
            if kind % 3 < 2:
                r = kind % 3
                src, dst = buf.at[0, r, piece], buf.at[side, r, piece]
            else:
                r = 0 if upward else 1
                src, dst = buf.at[side, r, piece], buf.at[3, r, piece]
        return pltpu.make_async_remote_copy(
            src_ref=src, dst_ref=dst, send_sem=ag_send.at[h, k], recv_sem=ag_recv.at[h, k],
            device_id=target, device_id_type=MESH,
        )

    def ag_start(*ks):
        for k in ks:
            for h in range(2):
                ag(h, k).start()

    def ag_wait(*ks):
        for k in ks:
            for h in range(2):
                ag(h, k).wait_recv()

    Z_, UP, DOWN = 0, (1, 2, 3), (4, 5, 6)

    def outer(kind, piece):
        return 7 + 3 * kind + piece

    U0, U1, UR, D0, D1, DR = range(6)

    ag_start(Z_, UP[0], DOWN[0])
    ag_start(outer(U0, 0), outer(D0, 0))

    for k in range(1, 7):
        loads[k].wait()
    classes = ints[0:1, :]
    psi_prev = ints[1:2, :]
    ranges = ints[2:3, :]

    def column(row):
        wide = jnp.broadcast_to(row.astype(F32), (128, N))
        return jnp.transpose(wide).astype(jnp.int32)

    shift_y = column(shift_in[0:1, :])
    shift_x = column(shift_in[1:2, :])
    lane = lax.broadcasted_iota(jnp.int32, (N, 128), 1)
    fc, fs = cos_sin(
        jnp.bitwise_and(lane, 31) * shift_x + jnp.right_shift(lane, 5) * shift_y
    )
    spin[0], spin[1] = fc, fs
    rc, rs_ = cos_sin(4 * shift_y)
    spin[2], spin[3] = rc, rs_
    qc, qs = cos_sin(16 * shift_y)
    spin[4], spin[5] = qc, qs

    class_rows = lax.broadcasted_iota(jnp.int32, (128, N), 0)
    mask_t = (class_rows == classes).astype(F32)
    onehot_t[...] = mask_t.astype(BF16)
    onehot = jnp.transpose(mask_t).astype(BF16)

    psi_rows = lax.broadcasted_iota(jnp.int32, (16, N), 0)
    apart = jnp.abs(psi_rows - psi_prev)
    apart = jnp.minimum(apart, 16 - apart).astype(F32)
    psi_term = -(apart * apart * F32(0.5 / 9.0))
    psi_rows_sc[0] = psi_term[0:8]
    psi_rows_sc[1] = psi_term[8:16]

    ag_wait(Z_)
    ag_start(UP[1], DOWN[1])
    ag_start(outer(U1, 0), outer(D1, 0))

    noise = noise_in[...]
    for j in range(8):
        lanes = slice(j * 256, (j + 1) * 256)
        ctf_now = ctf[:, lanes]
        noise_now = noise[:, lanes]
        gain_now = ctf_now * ctf_now / noise_now
        gain[:, lanes] = gain_now
        for k, piece in enumerate(split3(gain_now)):
            gain3[k, :, lanes] = piece
        high, middle, low = split3(ctf_now / noise_now)
        pick = onehot[:, 0:GROUPS]
        wsel[:, lanes] = (
            dot(pick, high, ((1,), (0,))) + dot(pick, middle, ((1,), (0,)))
        ) + dot(pick, low, ((1,), (0,)))

    loads[7].wait()
    loads[8].wait()

    ag_wait(UP[0])
    ag_start(UP[2])
    ag_wait(DOWN[0])
    ag_start(outer(U0, 1), outer(D0, 1))

    def align(part, carry):
        rows = pl.ds(pl.multiple_of(part * 32, 32), 32)
        base_c, base_s = [spin[0, rows]], [spin[1, rows]]
        step_c, step_s = spin[2, rows], spin[3, rows]
        turn_c, turn_s = spin[4, rows], spin[5, rows]
        for j in range(16):
            if j == 0:
                c, s = base_c[0], base_s[0]
            elif j < 4:
                pc, ps = base_c[j - 1], base_s[j - 1]
                c, s = pc * step_c - ps * step_s, ps * step_c + pc * step_s
                base_c.append(c)
                base_s.append(s)
            else:
                pc, ps = base_c[j % 4], base_s[j % 4]
                c, s = pc * turn_c - ps * turn_s, ps * turn_c + pc * turn_s
                base_c[j % 4], base_s[j % 4] = c, s
            lanes = slice(j * 128, (j + 1) * 128)
            real = img[rows, lanes].astype(F32)
            imag = img[rows, PIX + j * 128:PIX + (j + 1) * 128].astype(F32)
            weight = wsel[rows, lanes]
            h, jj = j // 8, j % 8
            al[h][rows, jj * 128:(jj + 1) * 128] = ((real * c + imag * s) * weight).astype(BF16)
            al[h][rows, HP + jj * 128:HP + (jj + 1) * 128] = (
                (imag * c - real * s) * weight
            ).astype(BF16)
        return carry

    lax.fori_loop(0, 4, align, 0)
    ag_wait(outer(U0, 0))
    ag_start(outer(UR, 0))
    ag_wait(DOWN[1])
    ag_start(DOWN[2])
    ag_wait(UP[1])
    ag_start(outer(D1, 1), outer(U1, 1))
    ag_wait(outer(D1, 0))
    ag_start(outer(DR, 0))
    lax.fori_loop(4, 8, align, 0)
    ag_wait(UP[2])
    ag_start(outer(U0, 2), outer(D0, 2))
    ag_wait(DOWN[2])
    ag_start(outer(D1, 2), outer(U1, 2))

    def cross_chunk(h, now):
        for j in range(8):
            lanes = slice(j * 128, (j + 1) * 128)
            wide = slice(h * HP + j * 128, h * HP + (j + 1) * 128)
            value = g[h][now, :, :, :, lanes].astype(F32).reshape(8, 16, 128)
            real, imag = value[:, 0:8], value[:, 8:16]
            mag[:, lanes] = (real * real + imag * imag).reshape(64, 128)

            def put(t, shifted_real, shifted_imag):
                rows = slice(t * 64, (t + 1) * 64)
                s_buf[h][rows, lanes] = shifted_real.reshape(64, 128).astype(BF16)
                s_buf[h][rows, HP + j * 128:HP + (j + 1) * 128] = (
                    shifted_imag.reshape(64, 128).astype(BF16)
                )

            put(4, real, imag)
            for q, (ty, tx) in enumerate(PAIRS):
                c = table_ref[2 * q:2 * q + 1, wide][None]
                s = table_ref[2 * q + 1:2 * q + 2, wide][None]
                rc_, is_, rs_, ic_ = real * c, imag * s, real * s, imag * c
                put(offset_index(ty, tx), rc_ - is_, rs_ + ic_)
                put(offset_index(-ty, -tx), rc_ + is_, ic_ - rs_)
        high, middle, low = split3(mag[...])
        half = slice(h * HP, (h + 1) * HP)
        by_high = dot(jnp.concatenate([high, middle, low], axis=0), gain3[0, :, half], ((1,), (1,)))
        by_middle = dot(jnp.concatenate([high, middle], axis=0), gain3[1, :, half], ((1,), (1,)))
        by_low = dot(high, gain3[2, :, half], ((1,), (1,)))
        small = (by_low + by_high[128:192]) + by_middle[64:128]
        energy = (small + (by_middle[0:64] + by_high[64:128])) + by_high[0:64]
        en[h, now, :, :, 0:GROUPS] = energy.reshape(8, 8, GROUPS)
        sc[h, now] = dot(s_buf[h][...], al[h][...], ((1,), (1,))).reshape(OFFSETS, 8, 8, N)

    def cross_step(i, carry):
        @pl.when(i == 1)
        def _():
            ag_wait(outer(U0, 1))
            ag_start(outer(UR, 1))
            ag_wait(outer(D1, 1))
            ag_start(outer(DR, 1))
            ag_wait(outer(U0, 2))
            ag_start(outer(UR, 2))
            ag_wait(outer(D1, 2))
            ag_start(outer(DR, 2))
            ag_wait(outer(D0, 0), outer(D0, 1), outer(D0, 2))

        @pl.when(i == 2)
        def _():
            ag_wait(outer(U1, 0), outer(U1, 1), outer(U1, 2))

        @pl.when(i == 3)
        def _():
            for p in range(3):
                ag_wait(outer(UR, p), outer(DR, p))

        for h in range(2):
            cross_chunk(h, i)
        return carry

    lax.fori_loop(0, 4, cross_step, 0)

    def score_pass(py, top):
        energies = [
            en[0, py, r * 4 + px, :, 0:GROUPS] + en[1, px, r * 4 + py, :, 0:GROUPS]
            for r in range(2) for px in range(4)
        ]
        high, middle, low = split3(jnp.concatenate(energies, axis=0))
        picks = onehot_t[0:GROUPS]
        picked = (
            dot(high, picks, ((1,), (0,))) + dot(middle, picks, ((1,), (0,)))
        ) + dot(low, picks, ((1,), (0,)))
        penalty = 0.5 * picked
        owner_y = ring(y + ahead_of(py))
        for r in range(2):
            owner_z = lax.rem(z + r, 2)
            for px in range(4):
                owner_x = ring(x + (0, 1, 3, 2)[px])
                view = views_ref[owner_y * 4 + owner_z * 2 + owner_x // 2]
                prior = psi_rows_sc[lax.rem(owner_x, 2)] + jnp.where(
                    ranges == view, F32(1.5), F32(0.0)
                )
                b = r * 4 + px
                less = penalty[b * 8:(b + 1) * 8]
                for t in range(OFFSETS):
                    value = sc[0, py, t, b] + sc[1, px, t, r * 4 + py]
                    value = (value - less) + prior
                    sc[0, py, t, b] = value
                    top = jnp.maximum(top, value)
        return top

    top = lax.fori_loop(0, 4, score_pass, jnp.full((8, N), -jnp.inf, F32))
    top = jnp.max(top, axis=0, keepdims=True)

    def exp_pass(yy, total):
        for t in range(OFFSETS):
            for b in range(8):
                value = jnp.exp(sc[0, yy, t, b] - top)
                sc[0, yy, t, b] = value
                total = total + value
        return total

    total = lax.fori_loop(0, 4, exp_pass, jnp.zeros((8, N), F32))
    total = jnp.sum(total, axis=0, keepdims=True)

    for half in range(2):
        lanes = slice(half * 128, (half + 1) * 128)
        st[me_dir, half:half + 1] = top[:, lanes]
        st[me_dir, 2 + half:3 + half] = total[:, lanes]

    def dir_copy(o):
        return pltpu.make_async_remote_copy(
            src_ref=st.at[me_dir], dst_ref=st.at[me_dir], send_sem=dir_send.at[o - 1],
            recv_sem=dir_recv.at[o - 1], device_id=dir_peers[o - 1], device_id_type=MESH,
        )

    def dir_arrival(o):
        source = lax.rem(me_dir + 8 - o, 8)
        return pltpu.make_async_remote_copy(
            src_ref=st.at[source], dst_ref=st.at[source], send_sem=dir_send.at[o - 1],
            recv_sem=dir_recv.at[o - 1], device_id=dir_peers[o - 1], device_id_type=MESH,
        )

    for o in range(1, 8):
        dir_copy(o).start()
    for o in range(1, 8):
        dir_arrival(o).wait_recv()

    def joined(d, row):
        return jnp.concatenate([st[d, row:row + 1], st[d, row + 1:row + 2]], axis=1)

    tops = [joined(d, 0) for d in range(8)]
    best = tops[0]
    for d in range(1, 8):
        best = jnp.maximum(best, tops[d])
    mass_all = joined(0, 2) * jnp.exp(tops[0] - best)
    for d in range(1, 8):
        mass_all = mass_all + joined(d, 2) * jnp.exp(tops[d] - best)
    log_norm = best + jnp.log(mass_all)
    stats_ref[0:1] = log_norm
    stats_ref[1:2] = jnp.exp(best - log_norm)
    factor = jnp.exp(top - log_norm)

    def posterior_pass(yy, carry):
        for b in range(8):
            p = [
                (sc[0, yy, t, b] * factor).astype(BF16).astype(F32) for t in range(OFFSETS)
            ]
            by_row = []
            for ty in range(3):
                minus, zero, plus = p[3 * ty], p[3 * ty + 1], p[3 * ty + 2]
                by_row.append((zero, plus + minus, plus - minus))
            out = []
            for k in range(3):
                minus, zero, plus = by_row[0][k], by_row[1][k], by_row[2][k]
                out.append((zero, plus + minus, plus - minus))
            order = (
                out[0][0], out[1][0], out[0][1], out[1][1], out[2][2],
                out[2][0], out[2][1], out[0][2], out[1][2],
            )
            for k in range(OFFSETS):
                sc[1, yy, k, b] = order[k]
            massn[yy, b] = (out[0][0] + out[1][0]) + (out[0][1] + out[1][1])
        return carry

    lax.fori_loop(0, 4, posterior_pass, 0)

    def insert_chunk(h, now):
        for zz in range(2):
            for cp in range(2):
                pair = []
                for c in range(2):
                    cc = 2 * cp + c
                    if h == 0:
                        pair.append(sc[1, now, :, zz * 4 + cc])
                    else:
                        pair.append(sc[1, cc, :, zz * 4 + now])
                l_buf[h][:, zz * 2 + cp] = jnp.concatenate(pair, axis=1).astype(BF16)
        left = l_buf[h][...].reshape(OFFSETS * 64, N)
        for q in range(4):
            lanes = slice(q * 256, (q + 1) * 256)
            wide = slice(h * HP + q * 256, h * HP + (q + 1) * 256)
            real = dot(left, al[h][:, lanes], ((1,), (0,))).reshape(OFFSETS, 64, 256)
            imag = dot(
                left, al[h][:, HP + q * 256:HP + (q + 1) * 256], ((1,), (0,))
            ).reshape(OFFSETS, 64, 256)
            total_real, total_imag = real[0], imag[0]
            for k in range(4):
                w = table_ref[8 + k:9 + k, wide]
                total_real = total_real + w * real[1 + k]
                total_imag = total_imag + w * imag[1 + k]
            for k in range(4):
                w = table_ref[12 + k:13 + k, wide]
                total_real = total_real + w * imag[5 + k]
                total_imag = total_imag - w * real[5 + k]
            rp[h][now, :, 0:8, lanes] = total_real.reshape(8, 8, 256)
            rp[h][now, :, 8:16, lanes] = total_imag.reshape(8, 8, 256)
        if h == 0:
            high, middle, _ = split3(massn[now].reshape(64, N))
            masses = dot(high, onehot_t[...], ((1,), (1,))) + dot(
                middle, onehot_t[...], ((1,), (1,))
            )
            rp[h][now, :, 0:8, HP:HP + 128] = masses.reshape(8, 8, 128)
            rp[h][now, :, 8:16, HP:HP + 128] = jnp.zeros((8, 8, 128), F32)

    def rs(h, k):
        if k < 12:
            kind, part = k // 2, PARTS[k % 2]
            src, dst = sb[h].at[kind, part], rb[h].at[kind, part]
            target = up2[h] if kind < 3 else down2[h]
        elif k < 18:
            src, dst = sb2[h].at[k - 12], rb2[h].at[k - 12]
            target = up1[h] if k < 15 else down1[h]
        else:
            src, dst, target = sb3[h], rb3[h], z_other
        return pltpu.make_async_remote_copy(
            src_ref=src, dst_ref=dst, send_sem=rs_send.at[h, k], recv_sem=rs_recv.at[h, k],
            device_id=target, device_id_type=MESH,
        )

    def put(h, kind, place, r, p, add=None):
        part = PARTS[p]
        rows = slice(r * 4 + part.start, r * 4 + part.stop)
        value = rp[h][place, rows]
        if add is not None:
            rs(h, 2 * add + p).wait_recv()
            value = value + rb[h][add, part].astype(F32)
        sb[h][kind, part] = value.astype(BF16)
        rs(h, 2 * kind + p).start()

    def insert_step(i, carry):
        @pl.when(i == 3)
        def _():
            for h in range(2):
                put(h, 2, 1, 0, 0, add=0)
                put(h, 5, 2, 1, 0, add=3)

        for h in range(2):
            insert_chunk(h, 3 - i)

            @pl.when(i == 0)
            def _():
                for p in range(2):
                    put(h, 0, 3, 0, p)
                    put(h, 3, 3, 1, p)

            @pl.when(i == 1)
            def _():
                put(h, 4, 2, 0, 0)

            @pl.when(i == 2)
            def _():
                put(h, 1, 1, 1, 0)

        return carry

    lax.fori_loop(0, 4, insert_step, 0)

    for h in range(2):
        put(h, 4, 2, 0, 1)
        put(h, 1, 1, 1, 1)
        put(h, 2, 1, 0, 1, add=0)
        put(h, 5, 2, 1, 1, add=3)

    def take(h, p):
        part = PARTS[p]
        for kind in (1, 2, 4, 5):
            rs(h, 2 * kind + p).wait_recv()
        for r, (from_below, from_above) in enumerate(((2, 4), (1, 5))):
            rows = slice(r * 4 + part.start, r * 4 + part.stop)
            rp[h][0, rows] = (
                rp[h][0, rows] + rb[h][from_below, part].astype(F32)
            ) + rb[h][from_above, part].astype(F32)

    def put_inner(h, kind, place, r, add=None):
        value = rp[h][0, r * 4 + place]
        if add is not None:
            rs(h, 12 + add).wait_recv()
            value = value + rb2[h][add].astype(F32)
        sb2[h][kind] = value.astype(BF16)
        rs(h, 12 + kind).start()

    for h in range(2):
        take(h, 0)
        put_inner(h, 0, 3, 0)
        put_inner(h, 3, 3, 1)
        put_inner(h, 1, 1, 1)
        put_inner(h, 4, 2, 0)
    for h in range(2):
        put_inner(h, 2, 1, 0, add=0)
        put_inner(h, 5, 2, 1, add=3)
    for h in range(2):
        take(h, 1)

    def own(h, r):
        from_below, from_above = ((2, 4), (1, 5))[r]
        return (
            rp[h][0, r * 4] + rb2[h][from_below].astype(F32)
        ) + rb2[h][from_above].astype(F32)

    for h in range(2):
        for k in (1, 2, 4, 5):
            rs(h, 12 + k).wait_recv()
        sb3[h][...] = own(h, 1).astype(BF16)
        rs(h, 18).start()

    for h in range(2):
        mine = own(h, 0)
        rs(h, 18).wait_recv()
        result = mine + rb3[h][...].astype(F32)
        sums_ref[:, h * HP:(h + 1) * HP] = result[0:8, 0:HP]
        sums_ref[:, PIX + h * HP:PIX + (h + 1) * HP] = result[8:16, 0:HP]
        if h == 0:
            weights_ref[...] = lax.dot_general(
                result[0:8, HP:HP + GROUPS], gain[...], (((1,), (0,)), ((), ())),
                precision=lax.Precision.HIGHEST, preferred_element_type=F32,
            )

    for h in range(2):
        for k in range(25):
            ag(h, k).wait_send()
        for k in range(19):
            rs(h, k).wait_send()
    for o in range(1, 8):
        dir_copy(o).wait_send()


def finish(sums_in, weights_in, stats_in, sums_ref, weights_ref, norm_ref, peak_ref):
    sums_ref[...] = sums_in[...]
    weights_ref[...] = weights_in[...]
    norm_ref[...] = stats_in[0:1]
    peak_ref[...] = stats_in[1:2]


def per_device(
    images, refs, ctf, noise_var, shifts, ctf_class, psi_prev, earlier_direction_range, view_range
):
    vmem = pl.BlockSpec(memory_space=pltpu.VMEM)
    hbm = pl.BlockSpec(memory_space=pl.ANY)
    smem = pl.BlockSpec(memory_space=pltpu.SMEM)
    wa, wb = WIDTHS
    dma = pltpu.SemaphoreType.DMA
    out = pl.pallas_call(
        kernel,
        out_shape=(
            jax.ShapeDtypeStruct((8, 2 * PIX), F32),
            jax.ShapeDtypeStruct((8, PIX), F32),
            jax.ShapeDtypeStruct((8, N), F32),
        ),
        in_specs=[hbm] * 8 + [smem, hbm],
        out_specs=(vmem, vmem, vmem),
        scratch_shapes=[
            pltpu.VMEM((N, 2 * PIX), BF16),
            pltpu.VMEM((8, 2 * PIX), BF16),
            pltpu.VMEM((GROUPS, PIX), F32),
            pltpu.VMEM((1, PIX), F32),
            pltpu.VMEM((8, N), jnp.int32),
            pltpu.VMEM((2, N), jnp.int32),
            pltpu.VMEM((16, PIX), F32),
            pltpu.VMEM((4, 2, 4, 16, HP), BF16),
            pltpu.VMEM((4, 2, 4, 16, HP), BF16),
            pltpu.VMEM((N, 2 * HP), BF16),
            pltpu.VMEM((N, 2 * HP), BF16),
            pltpu.VMEM((N, PIX), F32),
            pltpu.VMEM((6, N, 128), F32),
            pltpu.VMEM((OFFSETS * 64, 2 * HP), BF16),
            pltpu.VMEM((OFFSETS * 64, 2 * HP), BF16),
            pltpu.VMEM((64, HP), F32),
            pltpu.VMEM((GROUPS, PIX), F32),
            pltpu.VMEM((3, GROUPS, PIX), BF16),
            pltpu.VMEM((2, 4, 8, 8, 128), F32),
            pltpu.VMEM((128, N), BF16),
            pltpu.VMEM((2, 8, N), F32),
            pltpu.VMEM((2, 4, OFFSETS, 8, 8, N), F32),
            pltpu.VMEM((4, 8, 8, N), F32),
            pltpu.VMEM((OFFSETS, 4, 16, N), BF16),
            pltpu.VMEM((OFFSETS, 4, 16, N), BF16),
            pltpu.VMEM((4, 8, 16, wa), F32),
            pltpu.VMEM((4, 8, 16, wb), F32),
            pltpu.VMEM((8, 8, 128), F32),
            pltpu.VMEM((6, 4, 16, wa), BF16),
            pltpu.VMEM((6, 4, 16, wb), BF16),
            pltpu.VMEM((6, 4, 16, wa), BF16),
            pltpu.VMEM((6, 4, 16, wb), BF16),
            pltpu.VMEM((6, 16, wa), BF16),
            pltpu.VMEM((6, 16, wb), BF16),
            pltpu.VMEM((6, 16, wa), BF16),
            pltpu.VMEM((6, 16, wb), BF16),
            pltpu.VMEM((16, wa), BF16),
            pltpu.VMEM((16, wb), BF16),
            pltpu.VMEM((16, wa), BF16),
            pltpu.VMEM((16, wb), BF16),
            dma((9,)),
            dma((2, 25)),
            dma((2, 25)),
            dma((7,)),
            dma((7,)),
            dma((2, 19)),
            dma((2, 19)),
        ],
        compiler_params=pltpu.CompilerParams(
            collective_id=0, has_side_effects=True, vmem_limit_bytes=60 * 2**20
        ),
        cost_estimate=pl.CostEstimate(
            flops=10_000_000_000, bytes_accessed=4_000_000, transcendentals=600_000
        ),
        name="expectation_step",
    )(
        images, refs, ctf, noise_var.reshape(1, PIX), ctf_class.reshape(1, N),
        psi_prev.reshape(1, N), earlier_direction_range.reshape(1, N), shifts.T, view_range,
        jnp.asarray(phase_constants()),
    )
    class_sums, weight_sums, log_norm, peak_prob = pl.pallas_call(
        finish,
        out_shape=(
            jax.ShapeDtypeStruct((8, 2 * PIX), F32),
            jax.ShapeDtypeStruct((8, PIX), F32),
            jax.ShapeDtypeStruct((1, N), F32),
            jax.ShapeDtypeStruct((1, N), F32),
        ),
        in_specs=[vmem] * 3,
        out_specs=(vmem,) * 4,
        name="finish",
    )(*out)
    return class_sums, weight_sums, log_norm.reshape(N), peak_prob.reshape(N)


def solution(mesh):
    placed = (
        P("dom", None),
        P(("dir", "dom"), None),
        P(),
        P(),
        P("dom", None),
        P("dom"),
        P("dom"),
        P("dom"),
        P("dir"),
    )
    return jax.shard_map(
        per_device,
        mesh=mesh,
        in_specs=placed,
        out_specs=(P(("dir", "dom"), None), P(("dir", "dom"), None), P("dom"), P("dom")),
        check_vma=False,
    )
```

```python
import math

import jax
import jax.numpy as jnp
import numpy as np
from jax import lax
from jax.experimental import pallas as pl
from jax.experimental.pallas import tpu as pltpu
from jax.sharding import PartitionSpec as P

CROP = 64
HALF = 32
PIX = 2048
OFFSETS = 9
GROUPS = 64
N = 256
BLOCKS = 32
HP = 1024
WIDTHS = (HP + 128, HP)
THETA = 2.0 * math.pi / CROP

F32 = jnp.float32
BF16 = jnp.bfloat16
MESH = pl.DeviceIdType.MESH

PAIRS = ((0, 1), (1, 0), (1, 1), (1, -1))


def offset_index(ty, tx):
    return (ty + 1) * 3 + (tx + 1)


def phase_constants():
    pixels = np.arange(PIX)
    alpha = THETA * (pixels // HALF)
    beta = THETA * (pixels % HALF)
    rows = []
    for ty, tx in PAIRS:
        angle = ty * alpha + tx * beta
        rows += [np.cos(angle), np.sin(angle)]
    ca, sa, cb, sb = np.cos(alpha), np.sin(alpha), np.cos(beta), np.sin(beta)
    rows += [cb, ca, ca * cb, -sa * sb, sb, ca * sb, sa, sa * cb]
    return np.stack(rows).astype(np.float32)


def cos_sin(index):
    m = jnp.bitwise_and(index, 63) + 8
    quarter = jnp.bitwise_and(jnp.right_shift(m, 4), 3)
    x = (jnp.bitwise_and(m, 15) - 8).astype(F32) * F32(THETA)
    x2 = x * x
    c = 1.0 + x2 * (-0.5 + x2 * (1 / 24 + x2 * (-1 / 720 + x2 * (1 / 40320))))
    s = x * (1.0 + x2 * (-1 / 6 + x2 * (1 / 120 + x2 * (-1 / 5040 + x2 * (1 / 362880)))))
    odd = jnp.bitwise_and(quarter, 1) == 1
    cc = jnp.where(odd, s, c)
    ss = jnp.where(odd, c, s)
    cos = jnp.where((quarter == 1) | (quarter == 2), -cc, cc)
    sin = jnp.where(quarter >= 2, -ss, ss)
    return cos, sin


def split3(value):
    high = value.astype(BF16)
    rest = value - high.astype(F32)
    middle = rest.astype(BF16)
    low = (rest - middle.astype(F32)).astype(BF16)
    return high, middle, low


def dot(a, b, dims):
    return lax.dot_general(a, b, (dims, ((), ())), preferred_element_type=F32)


def tree(op, values):
    while len(values) > 1:
        pairs = [op(a, b) for a, b in zip(values[::2], values[1::2])]
        values = pairs + values[len(pairs) * 2:]
    return values[0]


def ring(i):
    return lax.rem(i + 8, 4)


def ahead_of(place):
    return lax.rem((place * (place + 1)) // 2, 4)


PIECES = (slice(0, 1), slice(1, 3), slice(3, 4))
PARTS = (slice(1, 4), slice(0, 1))


def kernel(
    images_ref, refs_ref, ctf_ref, noise_ref, class_ref, psi_ref, range_ref, shift_ref,
    views_ref, table_in,
    sums_ref, weights_ref, stats_ref,
    img, refs_in, ctf, noise_in, ints, shift_in, table_ref,
    g_a, g_b, al_a, al_b, wsel, spin, s_a, s_b, mag, gain, gain3, en, onehot_t, psi_rows_sc,
    sc, massn, l_a, l_b, rp_a, rp_b,
    st, sb_a, sb_b, rb_a, rb_b, sb2_a, sb2_b, rb2_a, rb2_b, sb3_a, sb3_b, rb3_a, rb3_b,
    load_sem, ag_send, ag_recv, dir_send, dir_recv, rs_send, rs_recv,
):
    g = (g_a, g_b)
    al = (al_a, al_b)
    s_buf = (s_a, s_b)
    l_buf = (l_a, l_b)
    rp = (rp_a, rp_b)
    sb, rb = (sb_a, sb_b), (rb_a, rb_b)
    sb2, rb2 = (sb2_a, sb2_b), (rb2_a, rb2_b)
    sb3, rb3 = (sb3_a, sb3_b), (rb3_a, rb3_b)

    me_dir = lax.axis_index("dir")
    me_dom = lax.axis_index("dom")
    y = me_dom // 8
    z = lax.rem(me_dom // 4, 2)
    x = lax.rem(me_dom, 4)

    def device(yy, zz, xx):
        return (me_dir, (yy * 2 + zz) * 4 + xx)

    x_up, x_down = device(y, z, ring(x + 1)), device(y, z, ring(x - 1))
    y_up, y_down = device(ring(y + 1), z, x), device(ring(y - 1), z, x)
    z_other = device(y, 1 - z, x)
    dir_peers = [(lax.rem(me_dir + o, 8), me_dom) for o in range(1, 8)]

    up2, down2 = (y_up, x_up), (y_down, x_down)
    up1, down1 = (x_up, y_up), (x_down, y_down)
    far1 = (device(y, z, ring(x + 2)), device(ring(y + 2), z, x))

    barrier = pltpu.get_barrier_semaphore()
    partners = [z_other, x_up, x_down, y_up, y_down, *far1] + dir_peers
    for p in partners:
        pl.semaphore_signal(barrier, inc=1, device_id=p, device_id_type=MESH)

    loads = [
        pltpu.make_async_copy(src, dst, load_sem.at[k])
        for k, (src, dst) in enumerate((
            (refs_ref, refs_in), (shift_ref, shift_in), (class_ref, ints.at[0:1]),
            (psi_ref, ints.at[1:2]), (range_ref, ints.at[2:3]), (noise_ref, noise_in),
            (ctf_ref, ctf), (images_ref, img), (table_in, table_ref),
        ))
    ]
    for load in loads:
        load.start()

    loads[0].wait()
    for h in range(2):
        real = refs_in[:, h * HP:(h + 1) * HP].astype(F32)
        imag = refs_in[:, PIX + h * HP:PIX + (h + 1) * HP].astype(F32)
        g[h][0, 0, 0] = jnp.concatenate([real, imag], axis=0).astype(BF16)

    pl.semaphore_wait(barrier, len(partners))

    def ag(h, k):
        buf = g[h]
        if k == 0:
            src, dst, target = buf.at[0, 0, 0], buf.at[0, 1, 0], z_other
        elif k < 7:
            r, way = (k - 1) % 2, (k - 1) // 2
            target = (up1, down1, far1)[way][h]
            src, dst = buf.at[0, r, 0], buf.at[0, r, (2, 1, 3)[way]]
        else:
            piece = PIECES[(k - 7) % 3]
            kind = (k - 7) // 3
            upward = kind < 3
            target = up2[h] if upward else down2[h]
            side = 2 if upward else 1
            if kind % 3 < 2:
                r = kind % 3
                src, dst = buf.at[0, r, piece], buf.at[side, r, piece]
            else:
                r = 0 if upward else 1
                src, dst = buf.at[side, r, piece], buf.at[3, r, piece]
        return pltpu.make_async_remote_copy(
            src_ref=src, dst_ref=dst, send_sem=ag_send.at[h, k], recv_sem=ag_recv.at[h, k],
            device_id=target, device_id_type=MESH,
        )

    def ag_start(*ks):
        for k in ks:
            for h in range(2):
                ag(h, k).start()

    def ag_wait(*ks):
        for k in ks:
            for h in range(2):
                ag(h, k).wait_recv()

    Z_, INNER = 0, ((1, 3, 5), (2, 4, 6))

    def outer(kind, piece):
        return 7 + 3 * kind + piece

    U0, U1, UR, D0, D1, DR = range(6)

    ag_start(Z_, *INNER[0])
    ag_start(outer(U0, 0), outer(D0, 0))

    for k in range(1, 7):
        loads[k].wait()
    classes = ints[0:1, :]
    psi_prev = ints[1:2, :]
    ranges = ints[2:3, :]

    def column(row):
        wide = jnp.broadcast_to(row.astype(F32), (128, N))
        return jnp.transpose(wide).astype(jnp.int32)

    shift_y = column(shift_in[0:1, :])
    shift_x = column(shift_in[1:2, :])
    lane = lax.broadcasted_iota(jnp.int32, (N, 128), 1)
    fc, fs = cos_sin(
        jnp.bitwise_and(lane, 31) * shift_x + jnp.right_shift(lane, 5) * shift_y
    )
    spin[0], spin[1] = fc, fs
    rc, rs_ = cos_sin(4 * shift_y)
    spin[2], spin[3] = rc, rs_
    qc, qs = cos_sin(16 * shift_y)
    spin[4], spin[5] = qc, qs

    class_rows = lax.broadcasted_iota(jnp.int32, (128, N), 0)
    mask_t = (class_rows == classes).astype(F32)
    onehot_t[...] = mask_t.astype(BF16)
    onehot = jnp.transpose(mask_t).astype(BF16)

    psi_rows = lax.broadcasted_iota(jnp.int32, (16, N), 0)
    apart = jnp.abs(psi_rows - psi_prev)
    apart = jnp.minimum(apart, 16 - apart).astype(F32)
    psi_term = -(apart * apart * F32(0.5 / 9.0))
    psi_rows_sc[0] = psi_term[0:8]
    psi_rows_sc[1] = psi_term[8:16]

    ag_wait(Z_)
    ag_start(*INNER[1])
    ag_start(outer(U1, 0), outer(D1, 0))
    ag_wait(*INNER[0])
    for p in (1, 2):
        ag_start(outer(U0, p), outer(D0, p))

    noise = noise_in[...]
    for j in range(8):
        lanes = slice(j * 256, (j + 1) * 256)
        ctf_now = ctf[:, lanes]
        noise_now = noise[:, lanes]
        gain_now = ctf_now * ctf_now / noise_now
        gain[:, lanes] = gain_now
        for k, piece in enumerate(split3(gain_now)):
            gain3[k, :, lanes] = piece
        high, middle, low = split3(ctf_now / noise_now)
        pick = onehot[:, 0:GROUPS]
        wsel[:, lanes] = (
            dot(pick, high, ((1,), (0,))) + dot(pick, middle, ((1,), (0,)))
        ) + dot(pick, low, ((1,), (0,)))

    loads[7].wait()
    loads[8].wait()

    ag_wait(outer(U0, 0))
    ag_start(outer(UR, 0))

    def align(part, carry):
        rows = pl.ds(pl.multiple_of(part * 32, 32), 32)
        base_c, base_s = [spin[0, rows]], [spin[1, rows]]
        step_c, step_s = spin[2, rows], spin[3, rows]
        turn_c, turn_s = spin[4, rows], spin[5, rows]
        for j in range(16):
            if j == 0:
                c, s = base_c[0], base_s[0]
            elif j < 4:
                pc, ps = base_c[j - 1], base_s[j - 1]
                c, s = pc * step_c - ps * step_s, ps * step_c + pc * step_s
                base_c.append(c)
                base_s.append(s)
            else:
                pc, ps = base_c[j % 4], base_s[j % 4]
                c, s = pc * turn_c - ps * turn_s, ps * turn_c + pc * turn_s
                base_c[j % 4], base_s[j % 4] = c, s
            lanes = slice(j * 128, (j + 1) * 128)
            real = img[rows, lanes].astype(F32)
            imag = img[rows, PIX + j * 128:PIX + (j + 1) * 128].astype(F32)
            weight = wsel[rows, lanes]
            h, jj = j // 8, j % 8
            al[h][rows, jj * 128:(jj + 1) * 128] = ((real * c + imag * s) * weight).astype(BF16)
            al[h][rows, HP + jj * 128:HP + (jj + 1) * 128] = (
                (imag * c - real * s) * weight
            ).astype(BF16)
        return carry

    lax.fori_loop(0, 4, align, 0)
    ag_wait(*INNER[1])
    for p in (1, 2):
        ag_start(outer(D1, p), outer(U1, p))
    ag_wait(outer(D1, 0))
    ag_start(outer(DR, 0))
    lax.fori_loop(4, 8, align, 0)
    for p in (1, 2):
        ag_wait(outer(U0, p))
        ag_start(outer(UR, p))

    def cross_chunk(h, now):
        for j in range(8):
            lanes = slice(j * 128, (j + 1) * 128)
            wide = slice(h * HP + j * 128, h * HP + (j + 1) * 128)
            value = g[h][now, :, :, :, lanes].astype(F32).reshape(8, 16, 128)
            real, imag = value[:, 0:8], value[:, 8:16]
            mag[:, lanes] = (real * real + imag * imag).reshape(64, 128)

            def put(t, shifted_real, shifted_imag):
                rows = slice(t * 64, (t + 1) * 64)
                s_buf[h][rows, lanes] = shifted_real.reshape(64, 128).astype(BF16)
                s_buf[h][rows, HP + j * 128:HP + (j + 1) * 128] = (
                    shifted_imag.reshape(64, 128).astype(BF16)
                )

            put(4, real, imag)
            for q, (ty, tx) in enumerate(PAIRS):
                c = table_ref[2 * q:2 * q + 1, wide][None]
                s = table_ref[2 * q + 1:2 * q + 2, wide][None]
                rc_, is_, rs_, ic_ = real * c, imag * s, real * s, imag * c
                put(offset_index(ty, tx), rc_ - is_, rs_ + ic_)
                put(offset_index(-ty, -tx), rc_ + is_, ic_ - rs_)
        high, middle, low = split3(mag[...])
        half = slice(h * HP, (h + 1) * HP)
        by_high = dot(jnp.concatenate([high, middle, low], axis=0), gain3[0, :, half], ((1,), (1,)))
        by_middle = dot(jnp.concatenate([high, middle], axis=0), gain3[1, :, half], ((1,), (1,)))
        by_low = dot(high, gain3[2, :, half], ((1,), (1,)))
        small = (by_low + by_high[128:192]) + by_middle[64:128]
        energy = (small + (by_middle[0:64] + by_high[64:128])) + by_high[0:64]
        en[h, now, :, :, 0:GROUPS] = energy.reshape(8, 8, GROUPS)
        sc[h, now] = dot(s_buf[h][...], al[h][...], ((1,), (1,))).reshape(OFFSETS, 8, 8, N)

    def cross_step(i, carry):
        @pl.when(i == 1)
        def _():
            for p in (1, 2):
                ag_wait(outer(D1, p))
                ag_start(outer(DR, p))
            ag_wait(outer(D0, 0), outer(D0, 1), outer(D0, 2))

        @pl.when(i == 2)
        def _():
            ag_wait(outer(U1, 0), outer(U1, 1), outer(U1, 2))

        @pl.when(i == 3)
        def _():
            for p in range(3):
                ag_wait(outer(UR, p), outer(DR, p))

        for h in range(2):
            cross_chunk(h, i)

        return carry

    lax.fori_loop(0, 4, cross_step, 0)

    def score_pass(py, top):
        energies = [
            en[0, py, r * 4 + px, :, 0:GROUPS] + en[1, px, r * 4 + py, :, 0:GROUPS]
            for r in range(2) for px in range(4)
        ]
        high, middle, low = split3(jnp.concatenate(energies, axis=0))
        picks = onehot_t[0:GROUPS]
        picked = (
            dot(high, picks, ((1,), (0,))) + dot(middle, picks, ((1,), (0,)))
        ) + dot(low, picks, ((1,), (0,)))
        penalty = 0.5 * picked
        owner_y = ring(y + ahead_of(py))
        tops = [top]
        for r in range(2):
            owner_z = lax.rem(z + r, 2)
            for px in range(4):
                owner_x = ring(x + (0, 1, 3, 2)[px])
                view = views_ref[owner_y * 4 + owner_z * 2 + owner_x // 2]
                prior = psi_rows_sc[lax.rem(owner_x, 2)] + jnp.where(
                    ranges == view, F32(1.5), F32(0.0)
                )
                b = r * 4 + px
                less = penalty[b * 8:(b + 1) * 8]
                best_now = []
                for t in range(OFFSETS):
                    value = sc[0, py, t, b] + sc[1, px, t, r * 4 + py]
                    value = (value - less) + prior
                    sc[0, py, t, b] = value
                    best_now.append(value)
                tops.append(tree(jnp.maximum, best_now))
        return tree(jnp.maximum, tops)

    top = lax.fori_loop(0, 4, score_pass, jnp.full((8, N), -jnp.inf, F32))
    top = jnp.max(top, axis=0, keepdims=True)

    def exp_pass(yy, total):
        sums = [total]
        for b in range(8):
            values = []
            for t in range(OFFSETS):
                value = jnp.exp(sc[0, yy, t, b] - top)
                sc[0, yy, t, b] = value
                values.append(value)
            sums.append(tree(jnp.add, values))
        return tree(jnp.add, sums)

    total = lax.fori_loop(0, 4, exp_pass, jnp.zeros((8, N), F32))
    total = jnp.sum(total, axis=0, keepdims=True)

    for half in range(2):
        lanes = slice(half * 128, (half + 1) * 128)
        st[me_dir, half:half + 1] = top[:, lanes]
        st[me_dir, 2 + half:3 + half] = total[:, lanes]

    def dir_copy(o):
        return pltpu.make_async_remote_copy(
            src_ref=st.at[me_dir], dst_ref=st.at[me_dir], send_sem=dir_send.at[o - 1],
            recv_sem=dir_recv.at[o - 1], device_id=dir_peers[o - 1], device_id_type=MESH,
        )

    def dir_arrival(o):
        source = lax.rem(me_dir + 8 - o, 8)
        return pltpu.make_async_remote_copy(
            src_ref=st.at[source], dst_ref=st.at[source], send_sem=dir_send.at[o - 1],
            recv_sem=dir_recv.at[o - 1], device_id=dir_peers[o - 1], device_id_type=MESH,
        )

    for o in range(1, 8):
        dir_copy(o).start()
    for o in range(1, 8):
        dir_arrival(o).wait_recv()

    def joined(d, row):
        return jnp.concatenate([st[d, row:row + 1], st[d, row + 1:row + 2]], axis=1)

    tops = [joined(d, 0) for d in range(8)]
    best = tops[0]
    for d in range(1, 8):
        best = jnp.maximum(best, tops[d])
    mass_all = joined(0, 2) * jnp.exp(tops[0] - best)
    for d in range(1, 8):
        mass_all = mass_all + joined(d, 2) * jnp.exp(tops[d] - best)
    log_norm = best + jnp.log(mass_all)
    stats_ref[0:1] = log_norm
    stats_ref[1:2] = jnp.exp(best - log_norm)
    factor = jnp.exp(top - log_norm)

    def posterior_pass(yy, carry):
        for b in range(8):
            p = [
                (sc[0, yy, t, b] * factor).astype(BF16).astype(F32) for t in range(OFFSETS)
            ]
            by_row = []
            for ty in range(3):
                minus, zero, plus = p[3 * ty], p[3 * ty + 1], p[3 * ty + 2]
                by_row.append((zero, plus + minus, plus - minus))
            out = []
            for k in range(3):
                minus, zero, plus = by_row[0][k], by_row[1][k], by_row[2][k]
                out.append((zero, plus + minus, plus - minus))
            order = (
                out[0][0], out[1][0], out[0][1], out[1][1], out[2][2],
                out[2][0], out[2][1], out[0][2], out[1][2],
            )
            for k in range(OFFSETS):
                sc[1, yy, k, b] = order[k]
            massn[yy, b] = (out[0][0] + out[1][0]) + (out[0][1] + out[1][1])
        return carry

    lax.fori_loop(0, 4, posterior_pass, 0)

    def insert_chunk(h, now):
        for zz in range(2):
            for cp in range(2):
                pair = []
                for c in range(2):
                    cc = 2 * cp + c
                    if h == 0:
                        pair.append(sc[1, now, :, zz * 4 + cc])
                    else:
                        pair.append(sc[1, cc, :, zz * 4 + now])
                l_buf[h][:, zz * 2 + cp] = jnp.concatenate(pair, axis=1).astype(BF16)
        left = l_buf[h][...].reshape(OFFSETS * 64, N)
        for q in range(4):
            lanes = slice(q * 256, (q + 1) * 256)
            wide = slice(h * HP + q * 256, h * HP + (q + 1) * 256)
            real = dot(left, al[h][:, lanes], ((1,), (0,))).reshape(OFFSETS, 64, 256)
            imag = dot(
                left, al[h][:, HP + q * 256:HP + (q + 1) * 256], ((1,), (0,))
            ).reshape(OFFSETS, 64, 256)
            total_real, total_imag = real[0], imag[0]
            for k in range(4):
                w = table_ref[8 + k:9 + k, wide]
                total_real = total_real + w * real[1 + k]
                total_imag = total_imag + w * imag[1 + k]
            for k in range(4):
                w = table_ref[12 + k:13 + k, wide]
                total_real = total_real + w * imag[5 + k]
                total_imag = total_imag - w * real[5 + k]
            rp[h][now, :, 0:8, lanes] = total_real.reshape(8, 8, 256)
            rp[h][now, :, 8:16, lanes] = total_imag.reshape(8, 8, 256)
        if h == 0:
            high, middle, _ = split3(massn[now].reshape(64, N))
            masses = dot(high, onehot_t[...], ((1,), (1,))) + dot(
                middle, onehot_t[...], ((1,), (1,))
            )
            rp[h][now, :, 0:8, HP:HP + 128] = masses.reshape(8, 8, 128)
            rp[h][now, :, 8:16, HP:HP + 128] = jnp.zeros((8, 8, 128), F32)

    def rs(h, k):
        if k < 12:
            kind, part = k // 2, PARTS[k % 2]
            src, dst = sb[h].at[kind, part], rb[h].at[kind, part]
            target = up2[h] if kind < 3 else down2[h]
        elif k < 18:
            src, dst = sb2[h].at[k - 12], rb2[h].at[k - 12]
            target = (far1, up1, down1)[(k - 12) % 3][h]
        else:
            src, dst, target = sb3[h], rb3[h], z_other
        return pltpu.make_async_remote_copy(
            src_ref=src, dst_ref=dst, send_sem=rs_send.at[h, k], recv_sem=rs_recv.at[h, k],
            device_id=target, device_id_type=MESH,
        )

    def put(h, kind, place, r, p, add=None):
        part = PARTS[p]
        rows = slice(r * 4 + part.start, r * 4 + part.stop)
        value = rp[h][place, rows]
        if add is not None:
            rs(h, 2 * add + p).wait_recv()
            value = value + rb[h][add, part].astype(F32)
        sb[h][kind, part] = value.astype(BF16)
        rs(h, 2 * kind + p).start()

    def insert_step(i, carry):
        @pl.when(i == 3)
        def _():
            for h in range(2):
                put(h, 2, 1, 0, 0, add=0)
                put(h, 5, 2, 1, 0, add=3)

        for h in range(2):
            insert_chunk(h, 3 - i)

            @pl.when(i == 0)
            def _():
                for p in range(2):
                    put(h, 0, 3, 0, p)
                    put(h, 3, 3, 1, p)

            @pl.when(i == 1)
            def _():
                put(h, 4, 2, 0, 0)

            @pl.when(i == 2)
            def _():
                put(h, 1, 1, 1, 0)

        return carry

    lax.fori_loop(0, 4, insert_step, 0)

    for h in range(2):
        put(h, 4, 2, 0, 1)
        put(h, 1, 1, 1, 1)
        put(h, 2, 1, 0, 1, add=0)
        put(h, 5, 2, 1, 1, add=3)

    def take(h, p, r):
        part = PARTS[p]
        from_below, from_above = ((2, 4), (1, 5))[r]
        rs(h, 2 * from_below + p).wait_recv()
        rs(h, 2 * from_above + p).wait_recv()
        rows = slice(r * 4 + part.start, r * 4 + part.stop)
        return (
            rp[h][0, rows] + rb[h][from_below, part].astype(F32)
        ) + rb[h][from_above, part].astype(F32)

    for r in (1, 0):
        for h in range(2):
            above, below, far = (0, 1, 2)
            taken = take(h, 0, r)
            for k, place in enumerate((far, above, below)):
                sb2[h][3 * r + k] = taken[place].astype(BF16)
                rs(h, 12 + 3 * r + k).start()

    def own(h, r):
        total = take(h, 1, r)[0]
        for k in range(3):
            rs(h, 12 + 3 * r + k).wait_recv()
            total = total + rb2[h][3 * r + k].astype(F32)
        return total

    for h in range(2):
        sb3[h][...] = own(h, 1).astype(BF16)
        rs(h, 18).start()
    mine = [own(h, 0) for h in range(2)]

    for h in range(2):
        rs(h, 18).wait_recv()
        result = mine[h] + rb3[h][...].astype(F32)
        sums_ref[:, h * HP:(h + 1) * HP] = result[0:8, 0:HP]
        sums_ref[:, PIX + h * HP:PIX + (h + 1) * HP] = result[8:16, 0:HP]
        if h == 0:
            weights_ref[...] = lax.dot_general(
                result[0:8, HP:HP + GROUPS], gain[...], (((1,), (0,)), ((), ())),
                precision=lax.Precision.HIGHEST, preferred_element_type=F32,
            )

    for h in range(2):
        for k in range(25):
            ag(h, k).wait_send()
        for k in range(19):
            rs(h, k).wait_send()
    for o in range(1, 8):
        dir_copy(o).wait_send()


def finish(sums_in, weights_in, stats_in, sums_ref, weights_ref, norm_ref, peak_ref):
    sums_ref[...] = sums_in[...]
    weights_ref[...] = weights_in[...]
    norm_ref[...] = stats_in[0:1]
    peak_ref[...] = stats_in[1:2]


def per_device(
    images, refs, ctf, noise_var, shifts, ctf_class, psi_prev, earlier_direction_range, view_range
):
    vmem = pl.BlockSpec(memory_space=pltpu.VMEM)
    hbm = pl.BlockSpec(memory_space=pl.ANY)
    smem = pl.BlockSpec(memory_space=pltpu.SMEM)
    wa, wb = WIDTHS
    dma = pltpu.SemaphoreType.DMA
    out = pl.pallas_call(
        kernel,
        out_shape=(
            jax.ShapeDtypeStruct((8, 2 * PIX), F32),
            jax.ShapeDtypeStruct((8, PIX), F32),
            jax.ShapeDtypeStruct((8, N), F32),
        ),
        in_specs=[hbm] * 8 + [smem, hbm],
        out_specs=(vmem, vmem, vmem),
        scratch_shapes=[
            pltpu.VMEM((N, 2 * PIX), BF16),
            pltpu.VMEM((8, 2 * PIX), BF16),
            pltpu.VMEM((GROUPS, PIX), F32),
            pltpu.VMEM((1, PIX), F32),
            pltpu.VMEM((8, N), jnp.int32),
            pltpu.VMEM((2, N), jnp.int32),
            pltpu.VMEM((16, PIX), F32),
            pltpu.VMEM((4, 2, 4, 16, HP), BF16),
            pltpu.VMEM((4, 2, 4, 16, HP), BF16),
            pltpu.VMEM((N, 2 * HP), BF16),
            pltpu.VMEM((N, 2 * HP), BF16),
            pltpu.VMEM((N, PIX), F32),
            pltpu.VMEM((6, N, 128), F32),
            pltpu.VMEM((OFFSETS * 64, 2 * HP), BF16),
            pltpu.VMEM((OFFSETS * 64, 2 * HP), BF16),
            pltpu.VMEM((64, HP), F32),
            pltpu.VMEM((GROUPS, PIX), F32),
            pltpu.VMEM((3, GROUPS, PIX), BF16),
            pltpu.VMEM((2, 4, 8, 8, 128), F32),
            pltpu.VMEM((128, N), BF16),
            pltpu.VMEM((2, 8, N), F32),
            pltpu.VMEM((2, 4, OFFSETS, 8, 8, N), F32),
            pltpu.VMEM((4, 8, 8, N), F32),
            pltpu.VMEM((OFFSETS, 4, 16, N), BF16),
            pltpu.VMEM((OFFSETS, 4, 16, N), BF16),
            pltpu.VMEM((4, 8, 16, wa), F32),
            pltpu.VMEM((4, 8, 16, wb), F32),
            pltpu.VMEM((8, 8, 128), F32),
            pltpu.VMEM((6, 4, 16, wa), BF16),
            pltpu.VMEM((6, 4, 16, wb), BF16),
            pltpu.VMEM((6, 4, 16, wa), BF16),
            pltpu.VMEM((6, 4, 16, wb), BF16),
            pltpu.VMEM((6, 16, wa), BF16),
            pltpu.VMEM((6, 16, wb), BF16),
            pltpu.VMEM((6, 16, wa), BF16),
            pltpu.VMEM((6, 16, wb), BF16),
            pltpu.VMEM((16, wa), BF16),
            pltpu.VMEM((16, wb), BF16),
            pltpu.VMEM((16, wa), BF16),
            pltpu.VMEM((16, wb), BF16),
            dma((9,)),
            dma((2, 25)),
            dma((2, 25)),
            dma((7,)),
            dma((7,)),
            dma((2, 19)),
            dma((2, 19)),
        ],
        compiler_params=pltpu.CompilerParams(
            collective_id=0, has_side_effects=True, vmem_limit_bytes=60 * 2**20
        ),
        cost_estimate=pl.CostEstimate(
            flops=10_000_000_000, bytes_accessed=4_000_000, transcendentals=600_000
        ),
        name="expectation_step",
    )(
        images, refs, ctf, noise_var.reshape(1, PIX), ctf_class.reshape(1, N),
        psi_prev.reshape(1, N), earlier_direction_range.reshape(1, N), shifts.T, view_range,
        jnp.asarray(phase_constants()),
    )
    class_sums, weight_sums, log_norm, peak_prob = pl.pallas_call(
        finish,
        out_shape=(
            jax.ShapeDtypeStruct((8, 2 * PIX), F32),
            jax.ShapeDtypeStruct((8, PIX), F32),
            jax.ShapeDtypeStruct((1, N), F32),
            jax.ShapeDtypeStruct((1, N), F32),
        ),
        in_specs=[vmem] * 3,
        out_specs=(vmem,) * 4,
        name="finish",
    )(*out)
    return class_sums, weight_sums, log_norm.reshape(N), peak_prob.reshape(N)


def solution(mesh):
    placed = (
        P("dom", None),
        P(("dir", "dom"), None),
        P(),
        P(),
        P("dom", None),
        P("dom"),
        P("dom"),
        P("dom"),
        P("dir"),
    )
    return jax.shard_map(
        per_device,
        mesh=mesh,
        in_specs=placed,
        out_specs=(P(("dir", "dom"), None), P(("dir", "dom"), None), P("dom"), P("dom")),
        check_vma=False,
    )
```

```python
import math

import jax
import jax.numpy as jnp
import numpy as np
from jax import lax
from jax.experimental import pallas as pl
from jax.experimental.pallas import tpu as pltpu
from jax.sharding import PartitionSpec as P

CROP = 64
HALF = 32
PIX = 2048
OFFSETS = 9
GROUPS = 64
N = 256
BLOCKS = 32
HP = 1024
WIDTHS = (HP + 128, HP)
THETA = 2.0 * math.pi / CROP

F32 = jnp.float32
BF16 = jnp.bfloat16
MESH = pl.DeviceIdType.MESH

PAIRS = ((0, 1), (1, 0), (1, 1), (1, -1))


def offset_index(ty, tx):
    return (ty + 1) * 3 + (tx + 1)


def phase_constants():
    pixels = np.arange(PIX)
    alpha = THETA * (pixels // HALF)
    beta = THETA * (pixels % HALF)
    rows = []
    for ty, tx in PAIRS:
        angle = ty * alpha + tx * beta
        rows += [np.cos(angle), np.sin(angle)]
    ca, sa, cb, sb = np.cos(alpha), np.sin(alpha), np.cos(beta), np.sin(beta)
    rows += [cb, ca, ca * cb, -sa * sb, sb, ca * sb, sa, sa * cb]
    return np.stack(rows).astype(np.float32)


def cos_sin(index):
    m = jnp.bitwise_and(index, 63) + 8
    quarter = jnp.bitwise_and(jnp.right_shift(m, 4), 3)
    x = (jnp.bitwise_and(m, 15) - 8).astype(F32) * F32(THETA)
    x2 = x * x
    c = 1.0 + x2 * (-0.5 + x2 * (1 / 24 + x2 * (-1 / 720 + x2 * (1 / 40320))))
    s = x * (1.0 + x2 * (-1 / 6 + x2 * (1 / 120 + x2 * (-1 / 5040 + x2 * (1 / 362880)))))
    odd = jnp.bitwise_and(quarter, 1) == 1
    cc = jnp.where(odd, s, c)
    ss = jnp.where(odd, c, s)
    cos = jnp.where((quarter == 1) | (quarter == 2), -cc, cc)
    sin = jnp.where(quarter >= 2, -ss, ss)
    return cos, sin


def split3(value):
    high = value.astype(BF16)
    rest = value - high.astype(F32)
    middle = rest.astype(BF16)
    low = (rest - middle.astype(F32)).astype(BF16)
    return high, middle, low


def dot(a, b, dims):
    return lax.dot_general(a, b, (dims, ((), ())), preferred_element_type=F32)


def tree(op, values):
    while len(values) > 1:
        pairs = [op(a, b) for a, b in zip(values[::2], values[1::2])]
        values = pairs + values[len(pairs) * 2:]
    return values[0]


def ring(i):
    return lax.rem(i + 8, 4)


def ahead_of(place):
    return lax.rem((place * (place + 1)) // 2, 4)


PIECES = (slice(0, 1), slice(1, 3), slice(3, 4))
PARTS = (slice(1, 4), slice(0, 1))


def kernel(
    images_ref, refs_ref, ctf_ref, noise_ref, class_ref, psi_ref, range_ref, shift_ref,
    views_ref, table_in,
    sums_ref, weights_ref, stats_ref,
    img, refs_in, ctf, noise_in, ints, shift_in, table_ref,
    g_a, g_b, al_a, al_b, wsel, spin, s_a, s_b, mag, gain, gain3, en, onehot_t, psi_rows_sc,
    sc, massn, early, factor, l_a, l_b, rp_a, rp_b,
    st, sb_a, sb_b, rb_a, rb_b, sb2_a, sb2_b, rb2_a, rb2_b, sb3_a, sb3_b, rb3_a, rb3_b,
    load_sem, ag_send, ag_recv, dir_send, dir_recv, rs_send, rs_recv,
):
    g = (g_a, g_b)
    al = (al_a, al_b)
    s_buf = (s_a, s_b)
    l_buf = (l_a, l_b)
    rp = (rp_a, rp_b)
    sb, rb = (sb_a, sb_b), (rb_a, rb_b)
    sb2, rb2 = (sb2_a, sb2_b), (rb2_a, rb2_b)
    sb3, rb3 = (sb3_a, sb3_b), (rb3_a, rb3_b)

    me_dir = lax.axis_index("dir")
    me_dom = lax.axis_index("dom")
    y = me_dom // 8
    z = lax.rem(me_dom // 4, 2)
    x = lax.rem(me_dom, 4)

    def device(yy, zz, xx):
        return (me_dir, (yy * 2 + zz) * 4 + xx)

    x_up, x_down = device(y, z, ring(x + 1)), device(y, z, ring(x - 1))
    y_up, y_down = device(ring(y + 1), z, x), device(ring(y - 1), z, x)
    z_other = device(y, 1 - z, x)
    dir_peers = [(lax.rem(me_dir + o, 8), me_dom) for o in range(1, 8)]

    up2, down2 = (y_up, x_up), (y_down, x_down)
    up1, down1 = (x_up, y_up), (x_down, y_down)
    far1 = (device(y, z, ring(x + 2)), device(ring(y + 2), z, x))

    barrier = pltpu.get_barrier_semaphore()
    partners = [z_other, x_up, x_down, y_up, y_down, *far1] + dir_peers
    for p in partners:
        pl.semaphore_signal(barrier, inc=1, device_id=p, device_id_type=MESH)

    loads = [
        pltpu.make_async_copy(src, dst, load_sem.at[k])
        for k, (src, dst) in enumerate((
            (refs_ref, refs_in), (shift_ref, shift_in), (class_ref, ints.at[0:1]),
            (psi_ref, ints.at[1:2]), (range_ref, ints.at[2:3]), (noise_ref, noise_in),
            (ctf_ref, ctf), (images_ref, img), (table_in, table_ref),
        ))
    ]
    for load in loads:
        load.start()

    loads[0].wait()
    for h in range(2):
        real = refs_in[:, h * HP:(h + 1) * HP].astype(F32)
        imag = refs_in[:, PIX + h * HP:PIX + (h + 1) * HP].astype(F32)
        g[h][0, 0, 0] = jnp.concatenate([real, imag], axis=0).astype(BF16)

    pl.semaphore_wait(barrier, len(partners))

    def ag(h, k):
        buf = g[h]
        if k == 0:
            src, dst, target = buf.at[0, 0, 0], buf.at[0, 1, 0], z_other
        elif k < 7:
            r, way = (k - 1) % 2, (k - 1) // 2
            target = (up1, down1, far1)[way][h]
            src, dst = buf.at[0, r, 0], buf.at[0, r, (2, 1, 3)[way]]
        else:
            piece = PIECES[(k - 7) % 3]
            kind = (k - 7) // 3
            upward = kind < 3
            target = up2[h] if upward else down2[h]
            side = 2 if upward else 1
            if kind % 3 < 2:
                r = kind % 3
                src, dst = buf.at[0, r, piece], buf.at[side, r, piece]
            else:
                r = 0 if upward else 1
                src, dst = buf.at[side, r, piece], buf.at[3, r, piece]
        return pltpu.make_async_remote_copy(
            src_ref=src, dst_ref=dst, send_sem=ag_send.at[h, k], recv_sem=ag_recv.at[h, k],
            device_id=target, device_id_type=MESH,
        )

    def ag_start(*ks):
        for k in ks:
            for h in range(2):
                ag(h, k).start()

    def ag_wait(*ks):
        for k in ks:
            for h in range(2):
                ag(h, k).wait_recv()

    Z_, INNER = 0, ((1, 3, 5), (2, 4, 6))

    def outer(kind, piece):
        return 7 + 3 * kind + piece

    U0, U1, UR, D0, D1, DR = range(6)

    ag_start(Z_, *INNER[0])
    ag_start(outer(U0, 0), outer(D0, 0))

    for k in range(1, 7):
        loads[k].wait()
    classes = ints[0:1, :]
    psi_prev = ints[1:2, :]
    ranges = ints[2:3, :]

    def column(row):
        wide = jnp.broadcast_to(row.astype(F32), (128, N))
        return jnp.transpose(wide).astype(jnp.int32)

    shift_y = column(shift_in[0:1, :])
    shift_x = column(shift_in[1:2, :])
    lane = lax.broadcasted_iota(jnp.int32, (N, 128), 1)
    fc, fs = cos_sin(
        jnp.bitwise_and(lane, 31) * shift_x + jnp.right_shift(lane, 5) * shift_y
    )
    spin[0], spin[1] = fc, fs
    rc, rs_ = cos_sin(4 * shift_y)
    spin[2], spin[3] = rc, rs_
    qc, qs = cos_sin(16 * shift_y)
    spin[4], spin[5] = qc, qs

    class_rows = lax.broadcasted_iota(jnp.int32, (128, N), 0)
    mask_t = (class_rows == classes).astype(F32)
    onehot_t[...] = mask_t.astype(BF16)
    onehot = jnp.transpose(mask_t).astype(BF16)

    psi_rows = lax.broadcasted_iota(jnp.int32, (16, N), 0)
    apart = jnp.abs(psi_rows - psi_prev)
    apart = jnp.minimum(apart, 16 - apart).astype(F32)
    psi_term = -(apart * apart * F32(0.5 / 9.0))
    psi_rows_sc[0] = psi_term[0:8]
    psi_rows_sc[1] = psi_term[8:16]

    ag_wait(Z_)
    ag_start(*INNER[1])
    ag_start(outer(U1, 0), outer(D1, 0))
    ag_wait(*INNER[0])
    for p in (1, 2):
        ag_start(outer(U0, p), outer(D0, p))

    noise = noise_in[...]
    for j in range(8):
        lanes = slice(j * 256, (j + 1) * 256)
        ctf_now = ctf[:, lanes]
        noise_now = noise[:, lanes]
        gain_now = ctf_now * ctf_now / noise_now
        gain[:, lanes] = gain_now
        for k, piece in enumerate(split3(gain_now)):
            gain3[k, :, lanes] = piece
        high, middle, low = split3(ctf_now / noise_now)
        pick = onehot[:, 0:GROUPS]
        wsel[:, lanes] = (
            dot(pick, high, ((1,), (0,))) + dot(pick, middle, ((1,), (0,)))
        ) + dot(pick, low, ((1,), (0,)))

    loads[7].wait()
    loads[8].wait()

    ag_wait(outer(U0, 0))
    ag_start(outer(UR, 0))

    def align(part, carry):
        rows = pl.ds(pl.multiple_of(part * 32, 32), 32)
        base_c, base_s = [spin[0, rows]], [spin[1, rows]]
        step_c, step_s = spin[2, rows], spin[3, rows]
        turn_c, turn_s = spin[4, rows], spin[5, rows]
        for j in range(16):
            if j == 0:
                c, s = base_c[0], base_s[0]
            elif j < 4:
                pc, ps = base_c[j - 1], base_s[j - 1]
                c, s = pc * step_c - ps * step_s, ps * step_c + pc * step_s
                base_c.append(c)
                base_s.append(s)
            else:
                pc, ps = base_c[j % 4], base_s[j % 4]
                c, s = pc * turn_c - ps * turn_s, ps * turn_c + pc * turn_s
                base_c[j % 4], base_s[j % 4] = c, s
            lanes = slice(j * 128, (j + 1) * 128)
            real = img[rows, lanes].astype(F32)
            imag = img[rows, PIX + j * 128:PIX + (j + 1) * 128].astype(F32)
            weight = wsel[rows, lanes]
            h, jj = j // 8, j % 8
            al[h][rows, jj * 128:(jj + 1) * 128] = ((real * c + imag * s) * weight).astype(BF16)
            al[h][rows, HP + jj * 128:HP + (jj + 1) * 128] = (
                (imag * c - real * s) * weight
            ).astype(BF16)
        return carry

    lax.fori_loop(0, 8, align, 0)

    def cross_chunk(h, now, r):
        for j in range(8):
            lanes = slice(j * 128, (j + 1) * 128)
            wide = slice(h * HP + j * 128, h * HP + (j + 1) * 128)
            value = g[h][now, r, :, :, lanes].astype(F32)
            real, imag = value[:, 0:8], value[:, 8:16]
            mag[:, lanes] = (real * real + imag * imag).reshape(32, 128)

            def put(t, shifted_real, shifted_imag):
                rows = slice(t * 32, (t + 1) * 32)
                s_buf[h][rows, lanes] = shifted_real.reshape(32, 128).astype(BF16)
                s_buf[h][rows, HP + j * 128:HP + (j + 1) * 128] = (
                    shifted_imag.reshape(32, 128).astype(BF16)
                )

            put(4, real, imag)
            for q, (ty, tx) in enumerate(PAIRS):
                c = table_ref[2 * q:2 * q + 1, wide][None]
                s = table_ref[2 * q + 1:2 * q + 2, wide][None]
                rc_, is_, rs_, ic_ = real * c, imag * s, real * s, imag * c
                put(offset_index(ty, tx), rc_ - is_, rs_ + ic_)
                put(offset_index(-ty, -tx), rc_ + is_, ic_ - rs_)
        high, middle, low = split3(mag[...])
        half = slice(h * HP, (h + 1) * HP)
        by_high = dot(jnp.concatenate([high, middle, low], axis=0), gain3[0, :, half], ((1,), (1,)))
        by_middle = dot(jnp.concatenate([high, middle], axis=0), gain3[1, :, half], ((1,), (1,)))
        by_low = dot(high, gain3[2, :, half], ((1,), (1,)))
        small = (by_low + by_high[64:96]) + by_middle[32:64]
        energy = (small + (by_middle[0:32] + by_high[32:64])) + by_high[0:32]
        blocks = pl.ds(r * 4, 4)
        en[h, now, blocks, :, 0:GROUPS] = energy.reshape(4, 8, GROUPS)
        sc[h, now, :, blocks] = dot(s_buf[h][...], al[h][...], ((1,), (1,))).reshape(
            OFFSETS, 4, 8, N
        )

    def score_slab(py, places, top):
        blocks = [(r, px) for r in range(2) for px in places]
        energies = [
            en[0, py, r * 4 + px, :, 0:GROUPS] + en[1, px, r * 4 + py, :, 0:GROUPS]
            for r, px in blocks
        ]
        high, middle, low = split3(jnp.concatenate(energies, axis=0))
        picks = onehot_t[0:GROUPS]
        picked = (
            dot(high, picks, ((1,), (0,))) + dot(middle, picks, ((1,), (0,)))
        ) + dot(low, picks, ((1,), (0,)))
        penalty = 0.5 * picked
        owner_y = ring(y + ahead_of(py))
        tops = [top]
        for k, (r, px) in enumerate(blocks):
            owner_z = lax.rem(z + r, 2)
            owner_x = ring(x + (0, 1, 3, 2)[px])
            view = views_ref[owner_y * 4 + owner_z * 2 + owner_x // 2]
            prior = psi_rows_sc[lax.rem(owner_x, 2)] + jnp.where(
                ranges == view, F32(1.5), F32(0.0)
            )
            less = penalty[k * 8:(k + 1) * 8]
            values = []
            for t in range(OFFSETS):
                value = sc[0, py, t, r * 4 + px] + sc[1, px, t, r * 4 + py]
                value = (value - less) + prior
                sc[0, py, t, r * 4 + px] = value
                values.append(value)
            tops.append(tree(jnp.maximum, values))
        return tree(jnp.maximum, tops)

    def combine(py, b, e):
        by_row = []
        for ty in range(3):
            minus, zero, plus = e[3 * ty], e[3 * ty + 1], e[3 * ty + 2]
            by_row.append((zero, plus + minus, plus - minus))
        out = []
        for k in range(3):
            minus, zero, plus = by_row[0][k], by_row[1][k], by_row[2][k]
            out.append((zero, plus + minus, plus - minus))
        order = (
            out[0][0], out[1][0], out[0][1], out[1][1], out[2][2],
            out[2][0], out[2][1], out[0][2], out[1][2],
        )
        for k in range(OFFSETS):
            sc[1, py, k, b] = order[k]
        massn[py, b] = (out[0][0] + out[1][0]) + (out[0][1] + out[1][1])

    def exp_slab(py, places, top, total, combined):
        sums = [total]
        for r in range(2):
            for px in places:
                b = r * 4 + px
                values = []
                for t in range(OFFSETS):
                    value = jnp.exp(sc[0, py, t, b] - top)
                    if not combined:
                        sc[0, py, t, b] = value
                    values.append(value)
                sums.append(tree(jnp.add, values))
                if combined:
                    combine(py, b, values)
        return tree(jnp.add, sums)

    def combine_slab(py, places):
        for r in range(2):
            for px in places:
                b = r * 4 + px
                combine(py, b, [sc[0, py, t, b] for t in range(OFFSETS)])

    nearby, every, lowest = (0, 1, 2), (0, 1, 2, 3), jnp.full((8, N), -jnp.inf, F32)
    nothing = jnp.zeros((8, N), F32)

    def early_scores():
        top = lax.fori_loop(0, 3, lambda py, v: score_slab(py, nearby, v), lowest)
        top = jnp.max(top, axis=0, keepdims=True)
        total = lax.fori_loop(
            0, 3, lambda py, v: exp_slab(py, nearby, top, v, True), nothing
        )
        early[0:1] = top
        early[1:2] = jnp.sum(total, axis=0, keepdims=True)

    def relay(arrived, onward, *ps):
        for p in ps:
            ag_wait(outer(arrived, p))
            ag_start(outer(onward, p))

    def cross_step(i, carry):
        @pl.when(i == 1)
        def _():
            ag_wait(*INNER[1])
            for p in (1, 2):
                ag_start(outer(D1, p), outer(U1, p))

        @pl.when(i == 2)
        def _():
            relay(U0, UR, 1, 2)
            relay(D1, DR, 0)
            ag_wait(outer(D0, 0), outer(D0, 1), outer(D0, 2))

        @pl.when(i == 4)
        def _():
            relay(D1, DR, 1, 2)

        @pl.when(i == 5)
        def _():
            ag_wait(outer(U1, 0), outer(U1, 1), outer(U1, 2))

        @pl.when(i == 6)
        def _():
            early_scores()
            ag_wait(outer(UR, 0), outer(UR, 1), outer(UR, 2))

        @pl.when(i == 7)
        def _():
            ag_wait(outer(DR, 0), outer(DR, 1), outer(DR, 2))

        u, v = i // 2, lax.rem(i, 2)
        sides = (u * (3 - u)) // 2
        now = sides * (1 + v) + (1 - sides) * u
        r = sides * (u - 1) + (1 - sides) * v
        for h in range(2):
            cross_chunk(h, now, r)
        return carry

    lax.fori_loop(0, 8, cross_step, 0)

    late_top = lax.fori_loop(0, 3, lambda py, v: score_slab(py, (3,), v), lowest)
    late_top = jnp.max(score_slab(3, every, late_top), axis=0, keepdims=True)
    late_total = lax.fori_loop(
        0, 3, lambda py, v: exp_slab(py, (3,), late_top, v, False), nothing
    )
    late_total = jnp.sum(
        exp_slab(3, every, late_top, late_total, False), axis=0, keepdims=True
    )
    early_top = early[0:1]
    top = jnp.maximum(early_top, late_top)
    total = early[1:2] * jnp.exp(early_top - top) + late_total * jnp.exp(late_top - top)

    for half in range(2):
        lanes = slice(half * 128, (half + 1) * 128)
        st[me_dir, half:half + 1] = top[:, lanes]
        st[me_dir, 2 + half:3 + half] = total[:, lanes]

    def dir_copy(o):
        return pltpu.make_async_remote_copy(
            src_ref=st.at[me_dir], dst_ref=st.at[me_dir], send_sem=dir_send.at[o - 1],
            recv_sem=dir_recv.at[o - 1], device_id=dir_peers[o - 1], device_id_type=MESH,
        )

    def dir_arrival(o):
        source = lax.rem(me_dir + 8 - o, 8)
        return pltpu.make_async_remote_copy(
            src_ref=st.at[source], dst_ref=st.at[source], send_sem=dir_send.at[o - 1],
            recv_sem=dir_recv.at[o - 1], device_id=dir_peers[o - 1], device_id_type=MESH,
        )

    for o in range(1, 8):
        dir_copy(o).start()

    def combine_late(py, carry):
        combine_slab(py, (3,))
        return carry

    lax.fori_loop(0, 3, combine_late, 0)
    combine_slab(3, every)

    for o in range(1, 8):
        dir_arrival(o).wait_recv()

    def joined(d, row):
        return jnp.concatenate([st[d, row:row + 1], st[d, row + 1:row + 2]], axis=1)

    tops = [joined(d, 0) for d in range(8)]
    best = tops[0]
    for d in range(1, 8):
        best = jnp.maximum(best, tops[d])
    mass_all = joined(0, 2) * jnp.exp(tops[0] - best)
    for d in range(1, 8):
        mass_all = mass_all + joined(d, 2) * jnp.exp(tops[d] - best)
    log_norm = best + jnp.log(mass_all)
    stats_ref[0:1] = log_norm
    stats_ref[1:2] = jnp.exp(best - log_norm)
    factor[0] = jnp.broadcast_to(jnp.exp(early_top - log_norm), (8, N))
    factor[1] = jnp.broadcast_to(jnp.exp(late_top - log_norm), (8, N))

    def insert_chunk(h, now):
        scale = [factor[now // 3]] * 3 + [factor[1]]
        for zz in range(2):
            for cp in range(2):
                pair = []
                for c in range(2):
                    cc = 2 * cp + c
                    if h == 0:
                        pair.append(sc[1, now, :, zz * 4 + cc] * scale[cc])
                    else:
                        pair.append(sc[1, cc, :, zz * 4 + now] * scale[cc])
                l_buf[h][:, zz * 2 + cp] = jnp.concatenate(pair, axis=1).astype(BF16)
        left = l_buf[h][...].reshape(OFFSETS * 64, N)
        for q in range(4):
            lanes = slice(q * 256, (q + 1) * 256)
            wide = slice(h * HP + q * 256, h * HP + (q + 1) * 256)
            real = dot(left, al[h][:, lanes], ((1,), (0,))).reshape(OFFSETS, 64, 256)
            imag = dot(
                left, al[h][:, HP + q * 256:HP + (q + 1) * 256], ((1,), (0,))
            ).reshape(OFFSETS, 64, 256)
            total_real, total_imag = real[0], imag[0]
            for k in range(4):
                w = table_ref[8 + k:9 + k, wide]
                total_real = total_real + w * real[1 + k]
                total_imag = total_imag + w * imag[1 + k]
            for k in range(4):
                w = table_ref[12 + k:13 + k, wide]
                total_real = total_real + w * imag[5 + k]
                total_imag = total_imag - w * real[5 + k]
            rp[h][now, :, 0:8, lanes] = total_real.reshape(8, 8, 256)
            rp[h][now, :, 8:16, lanes] = total_imag.reshape(8, 8, 256)
        if h == 0:
            weighted = [massn[now, b] * scale[b % 4] for b in range(8)]
            high, middle, _ = split3(jnp.concatenate(weighted, axis=0))
            masses = dot(high, onehot_t[...], ((1,), (1,))) + dot(
                middle, onehot_t[...], ((1,), (1,))
            )
            rp[h][now, :, 0:8, HP:HP + 128] = masses.reshape(8, 8, 128)
            rp[h][now, :, 8:16, HP:HP + 128] = jnp.zeros((8, 8, 128), F32)

    def rs(h, k):
        if k < 12:
            kind, part = k // 2, PARTS[k % 2]
            src, dst = sb[h].at[kind, part], rb[h].at[kind, part]
            target = up2[h] if kind < 3 else down2[h]
        elif k < 18:
            src, dst = sb2[h].at[k - 12], rb2[h].at[k - 12]
            target = (far1, up1, down1)[(k - 12) % 3][h]
        else:
            src, dst, target = sb3[h], rb3[h], z_other
        return pltpu.make_async_remote_copy(
            src_ref=src, dst_ref=dst, send_sem=rs_send.at[h, k], recv_sem=rs_recv.at[h, k],
            device_id=target, device_id_type=MESH,
        )

    def put(h, kind, place, r, p, add=None):
        part = PARTS[p]
        rows = slice(r * 4 + part.start, r * 4 + part.stop)
        value = rp[h][place, rows]
        if add is not None:
            rs(h, 2 * add + p).wait_recv()
            value = value + rb[h][add, part].astype(F32)
        sb[h][kind, part] = value.astype(BF16)
        rs(h, 2 * kind + p).start()

    def insert_step(i, carry):
        @pl.when(i == 3)
        def _():
            for h in range(2):
                put(h, 2, 1, 0, 0, add=0)
                put(h, 5, 2, 1, 0, add=3)

        for h in range(2):
            insert_chunk(h, 3 - i)

            @pl.when(i == 0)
            def _():
                for p in range(2):
                    put(h, 0, 3, 0, p)
                    put(h, 3, 3, 1, p)

            @pl.when(i == 1)
            def _():
                put(h, 4, 2, 0, 0)

            @pl.when(i == 2)
            def _():
                put(h, 1, 1, 1, 0)

        return carry

    lax.fori_loop(0, 4, insert_step, 0)

    for h in range(2):
        put(h, 4, 2, 0, 1)
        put(h, 1, 1, 1, 1)
        put(h, 2, 1, 0, 1, add=0)
        put(h, 5, 2, 1, 1, add=3)

    def take(h, p, r):
        part = PARTS[p]
        from_below, from_above = ((2, 4), (1, 5))[r]
        rs(h, 2 * from_below + p).wait_recv()
        rs(h, 2 * from_above + p).wait_recv()
        rows = slice(r * 4 + part.start, r * 4 + part.stop)
        return (
            rp[h][0, rows] + rb[h][from_below, part].astype(F32)
        ) + rb[h][from_above, part].astype(F32)

    for r in (1, 0):
        for h in range(2):
            above, below, far = (0, 1, 2)
            taken = take(h, 0, r)
            for k, place in enumerate((far, above, below)):
                sb2[h][3 * r + k] = taken[place].astype(BF16)
                rs(h, 12 + 3 * r + k).start()

    def own(h, r):
        total = take(h, 1, r)[0]
        for k in range(3):
            rs(h, 12 + 3 * r + k).wait_recv()
            total = total + rb2[h][3 * r + k].astype(F32)
        return total

    for h in range(2):
        sb3[h][...] = own(h, 1).astype(BF16)
        rs(h, 18).start()
    mine = [own(h, 0) for h in range(2)]

    for h in range(2):
        rs(h, 18).wait_recv()
        result = mine[h] + rb3[h][...].astype(F32)
        sums_ref[:, h * HP:(h + 1) * HP] = result[0:8, 0:HP]
        sums_ref[:, PIX + h * HP:PIX + (h + 1) * HP] = result[8:16, 0:HP]
        if h == 0:
            weights_ref[...] = lax.dot_general(
                result[0:8, HP:HP + GROUPS], gain[...], (((1,), (0,)), ((), ())),
                precision=lax.Precision.HIGHEST, preferred_element_type=F32,
            )

    for h in range(2):
        for k in range(25):
            ag(h, k).wait_send()
        for k in range(19):
            rs(h, k).wait_send()
    for o in range(1, 8):
        dir_copy(o).wait_send()


def finish(sums_in, weights_in, stats_in, sums_ref, weights_ref, norm_ref, peak_ref):
    sums_ref[...] = sums_in[...]
    weights_ref[...] = weights_in[...]
    norm_ref[...] = stats_in[0:1]
    peak_ref[...] = stats_in[1:2]


def per_device(
    images, refs, ctf, noise_var, shifts, ctf_class, psi_prev, earlier_direction_range, view_range
):
    vmem = pl.BlockSpec(memory_space=pltpu.VMEM)
    hbm = pl.BlockSpec(memory_space=pl.ANY)
    smem = pl.BlockSpec(memory_space=pltpu.SMEM)
    wa, wb = WIDTHS
    dma = pltpu.SemaphoreType.DMA
    out = pl.pallas_call(
        kernel,
        out_shape=(
            jax.ShapeDtypeStruct((8, 2 * PIX), F32),
            jax.ShapeDtypeStruct((8, PIX), F32),
            jax.ShapeDtypeStruct((8, N), F32),
        ),
        in_specs=[hbm] * 8 + [smem, hbm],
        out_specs=(vmem, vmem, vmem),
        scratch_shapes=[
            pltpu.VMEM((N, 2 * PIX), BF16),
            pltpu.VMEM((8, 2 * PIX), BF16),
            pltpu.VMEM((GROUPS, PIX), F32),
            pltpu.VMEM((1, PIX), F32),
            pltpu.VMEM((8, N), jnp.int32),
            pltpu.VMEM((2, N), jnp.int32),
            pltpu.VMEM((16, PIX), F32),
            pltpu.VMEM((4, 2, 4, 16, HP), BF16),
            pltpu.VMEM((4, 2, 4, 16, HP), BF16),
            pltpu.VMEM((N, 2 * HP), BF16),
            pltpu.VMEM((N, 2 * HP), BF16),
            pltpu.VMEM((N, PIX), F32),
            pltpu.VMEM((6, N, 128), F32),
            pltpu.VMEM((OFFSETS * 32, 2 * HP), BF16),
            pltpu.VMEM((OFFSETS * 32, 2 * HP), BF16),
            pltpu.VMEM((32, HP), F32),
            pltpu.VMEM((GROUPS, PIX), F32),
            pltpu.VMEM((3, GROUPS, PIX), BF16),
            pltpu.VMEM((2, 4, 8, 8, 128), F32),
            pltpu.VMEM((128, N), BF16),
            pltpu.VMEM((2, 8, N), F32),
            pltpu.VMEM((2, 4, OFFSETS, 8, 8, N), F32),
            pltpu.VMEM((4, 8, 8, N), F32),
            pltpu.VMEM((8, N), F32),
            pltpu.VMEM((2, 8, N), F32),
            pltpu.VMEM((OFFSETS, 4, 16, N), BF16),
            pltpu.VMEM((OFFSETS, 4, 16, N), BF16),
            pltpu.VMEM((4, 8, 16, wa), F32),
            pltpu.VMEM((4, 8, 16, wb), F32),
            pltpu.VMEM((8, 8, 128), F32),
            pltpu.VMEM((6, 4, 16, wa), BF16),
            pltpu.VMEM((6, 4, 16, wb), BF16),
            pltpu.VMEM((6, 4, 16, wa), BF16),
            pltpu.VMEM((6, 4, 16, wb), BF16),
            pltpu.VMEM((6, 16, wa), BF16),
            pltpu.VMEM((6, 16, wb), BF16),
            pltpu.VMEM((6, 16, wa), BF16),
            pltpu.VMEM((6, 16, wb), BF16),
            pltpu.VMEM((16, wa), BF16),
            pltpu.VMEM((16, wb), BF16),
            pltpu.VMEM((16, wa), BF16),
            pltpu.VMEM((16, wb), BF16),
            dma((9,)),
            dma((2, 25)),
            dma((2, 25)),
            dma((7,)),
            dma((7,)),
            dma((2, 19)),
            dma((2, 19)),
        ],
        compiler_params=pltpu.CompilerParams(
            collective_id=0, has_side_effects=True, vmem_limit_bytes=60 * 2**20
        ),
        cost_estimate=pl.CostEstimate(
            flops=10_000_000_000, bytes_accessed=4_000_000, transcendentals=600_000
        ),
        name="expectation_step",
    )(
        images, refs, ctf, noise_var.reshape(1, PIX), ctf_class.reshape(1, N),
        psi_prev.reshape(1, N), earlier_direction_range.reshape(1, N), shifts.T, view_range,
        jnp.asarray(phase_constants()),
    )
    class_sums, weight_sums, log_norm, peak_prob = pl.pallas_call(
        finish,
        out_shape=(
            jax.ShapeDtypeStruct((8, 2 * PIX), F32),
            jax.ShapeDtypeStruct((8, PIX), F32),
            jax.ShapeDtypeStruct((1, N), F32),
            jax.ShapeDtypeStruct((1, N), F32),
        ),
        in_specs=[vmem] * 3,
        out_specs=(vmem,) * 4,
        name="finish",
    )(*out)
    return class_sums, weight_sums, log_norm.reshape(N), peak_prob.reshape(N)


def solution(mesh):
    placed = (
        P("dom", None),
        P(("dir", "dom"), None),
        P(),
        P(),
        P("dom", None),
        P("dom"),
        P("dom"),
        P("dom"),
        P("dir"),
    )
    return jax.shard_map(
        per_device,
        mesh=mesh,
        in_specs=placed,
        out_specs=(P(("dir", "dom"), None), P(("dir", "dom"), None), P("dom"), P("dom")),
        check_vma=False,
    )
```

```python
import math

import jax
import jax.numpy as jnp
import numpy as np
from jax import lax
from jax.experimental import pallas as pl
from jax.experimental.pallas import tpu as pltpu
from jax.sharding import PartitionSpec as P

CROP = 64
HALF = 32
PIX = 2048
OFFSETS = 9
GROUPS = 64
N = 256
BLOCKS = 32
HP = 1024
WIDTHS = (HP + 128, HP)
THETA = 2.0 * math.pi / CROP

F32 = jnp.float32
BF16 = jnp.bfloat16
MESH = pl.DeviceIdType.MESH

PAIRS = ((0, 1), (1, 0), (1, 1), (1, -1))


def offset_index(ty, tx):
    return (ty + 1) * 3 + (tx + 1)


def phase_constants():
    pixels = np.arange(PIX)
    alpha = THETA * (pixels // HALF)
    beta = THETA * (pixels % HALF)
    rows = []
    for ty, tx in PAIRS:
        angle = ty * alpha + tx * beta
        rows += [np.cos(angle), np.sin(angle)]
    ca, sa, cb, sb = np.cos(alpha), np.sin(alpha), np.cos(beta), np.sin(beta)
    rows += [cb, ca, ca * cb, -sa * sb, sb, ca * sb, sa, sa * cb]
    return np.stack(rows).astype(np.float32)


def cos_sin(index):
    m = jnp.bitwise_and(index, 63) + 8
    quarter = jnp.bitwise_and(jnp.right_shift(m, 4), 3)
    x = (jnp.bitwise_and(m, 15) - 8).astype(F32) * F32(THETA)
    x2 = x * x
    c = 1.0 + x2 * (-0.5 + x2 * (1 / 24 + x2 * (-1 / 720 + x2 * (1 / 40320))))
    s = x * (1.0 + x2 * (-1 / 6 + x2 * (1 / 120 + x2 * (-1 / 5040 + x2 * (1 / 362880)))))
    odd = jnp.bitwise_and(quarter, 1) == 1
    cc = jnp.where(odd, s, c)
    ss = jnp.where(odd, c, s)
    cos = jnp.where((quarter == 1) | (quarter == 2), -cc, cc)
    sin = jnp.where(quarter >= 2, -ss, ss)
    return cos, sin


def split3(value):
    high = value.astype(BF16)
    rest = value - high.astype(F32)
    middle = rest.astype(BF16)
    low = (rest - middle.astype(F32)).astype(BF16)
    return high, middle, low


def dot(a, b, dims):
    return lax.dot_general(a, b, (dims, ((), ())), preferred_element_type=F32)


def tree(op, values):
    while len(values) > 1:
        pairs = [op(a, b) for a, b in zip(values[::2], values[1::2])]
        values = pairs + values[len(pairs) * 2:]
    return values[0]


def ring(i):
    return lax.rem(i + 8, 4)


def ahead_of(place):
    return lax.rem((place * (place + 1)) // 2, 4)


PIECES = (slice(0, 1), slice(1, 3), slice(3, 4))
PARTS = (slice(1, 4), slice(0, 1))


def kernel(
    images_ref, refs_ref, ctf_ref, noise_ref, class_ref, psi_ref, range_ref, shift_ref,
    views_in, table_in,
    sums_ref, weights_ref, stats_ref,
    views_ref, img, refs_in, ctf, noise_in, ints, shift_in, table_ref,
    g_a, g_b, al_a, al_b, wsel, spin, s_a, s_b, mag, gain, gain3, en, onehot_t, psi_rows_sc,
    sc, massn, early, factor, l_a, l_b, rp_a, rp_b,
    st, sb_a, sb_b, rb_a, rb_b, sb2_a, sb2_b, rb2_a, rb2_b, sb3_a, sb3_b, rb3_a, rb3_b,
    load_sem, ag_send, ag_recv, dir_send, dir_recv, rs_send, rs_recv,
):
    g = (g_a, g_b)
    al = (al_a, al_b)
    s_buf = (s_a, s_b)
    l_buf = (l_a, l_b)
    rp = (rp_a, rp_b)
    sb, rb = (sb_a, sb_b), (rb_a, rb_b)
    sb2, rb2 = (sb2_a, sb2_b), (rb2_a, rb2_b)
    sb3, rb3 = (sb3_a, sb3_b), (rb3_a, rb3_b)

    me_dir = lax.axis_index("dir")
    me_dom = lax.axis_index("dom")
    y = me_dom // 8
    z = lax.rem(me_dom // 4, 2)
    x = lax.rem(me_dom, 4)

    def device(yy, zz, xx):
        return (me_dir, (yy * 2 + zz) * 4 + xx)

    x_up, x_down = device(y, z, ring(x + 1)), device(y, z, ring(x - 1))
    y_up, y_down = device(ring(y + 1), z, x), device(ring(y - 1), z, x)
    z_other = device(y, 1 - z, x)
    dir_peers = [(lax.rem(me_dir + o, 8), me_dom) for o in range(1, 8)]

    up2, down2 = (y_up, x_up), (y_down, x_down)
    up1, down1 = (x_up, y_up), (x_down, y_down)
    far1 = (device(y, z, ring(x + 2)), device(ring(y + 2), z, x))

    barrier = pltpu.get_barrier_semaphore()
    partners = [z_other, x_up, x_down, y_up, y_down, *far1] + dir_peers
    for p in partners:
        pl.semaphore_signal(barrier, inc=1, device_id=p, device_id_type=MESH)

    loads = [
        pltpu.make_async_copy(src, dst, load_sem.at[k])
        for k, (src, dst) in enumerate((
            (refs_ref, refs_in), (shift_ref, shift_in), (class_ref, ints.at[0:1]),
            (psi_ref, ints.at[1:2]), (range_ref, ints.at[2:3]), (noise_ref, noise_in),
            (ctf_ref, ctf), (images_ref, img), (table_in, table_ref),
            (views_in, views_ref),
        ))
    ]
    for load in loads:
        load.start()

    loads[0].wait()
    for h in range(2):
        real = refs_in[:, h * HP:(h + 1) * HP].astype(F32)
        imag = refs_in[:, PIX + h * HP:PIX + (h + 1) * HP].astype(F32)
        g[h][0, 0, 0] = jnp.concatenate([real, imag], axis=0).astype(BF16)

    pl.semaphore_wait(barrier, len(partners))

    def ag(h, k):
        buf = g[h]
        if k == 0:
            src, dst, target = buf.at[0, 0, 0], buf.at[0, 1, 0], z_other
        elif k < 7:
            r, way = (k - 1) % 2, (k - 1) // 2
            target = (up1, down1, far1)[way][h]
            src, dst = buf.at[0, r, 0], buf.at[0, r, (2, 1, 3)[way]]
        else:
            piece = PIECES[(k - 7) % 3]
            kind = (k - 7) // 3
            upward = kind < 3
            target = up2[h] if upward else down2[h]
            side = 2 if upward else 1
            if kind % 3 < 2:
                r = kind % 3
                src, dst = buf.at[0, r, piece], buf.at[side, r, piece]
            else:
                r = 0 if upward else 1
                src, dst = buf.at[side, r, piece], buf.at[3, r, piece]
        return pltpu.make_async_remote_copy(
            src_ref=src, dst_ref=dst, send_sem=ag_send.at[h, k], recv_sem=ag_recv.at[h, k],
            device_id=target, device_id_type=MESH,
        )

    def ag_start(*ks):
        for k in ks:
            for h in range(2):
                ag(h, k).start()

    def ag_wait(*ks):
        for k in ks:
            for h in range(2):
                ag(h, k).wait_recv()

    Z_, INNER = 0, ((1, 3, 5), (2, 4, 6))

    def outer(kind, piece):
        return 7 + 3 * kind + piece

    U0, U1, UR, D0, D1, DR = range(6)

    ag_start(Z_, *INNER[0])
    ag_start(outer(U0, 0), outer(D0, 0))

    for k in range(1, 7):
        loads[k].wait()
    classes = ints[0:1, :]
    psi_prev = ints[1:2, :]
    ranges = ints[2:3, :]

    def column(row):
        wide = jnp.broadcast_to(row.astype(F32), (128, N))
        return jnp.transpose(wide).astype(jnp.int32)

    shift_y = column(shift_in[0:1, :])
    shift_x = column(shift_in[1:2, :])
    lane = lax.broadcasted_iota(jnp.int32, (N, 128), 1)
    fc, fs = cos_sin(
        jnp.bitwise_and(lane, 31) * shift_x + jnp.right_shift(lane, 5) * shift_y
    )
    spin[0], spin[1] = fc, fs
    rc, rs_ = cos_sin(4 * shift_y)
    spin[2], spin[3] = rc, rs_
    qc, qs = cos_sin(16 * shift_y)
    spin[4], spin[5] = qc, qs

    class_rows = lax.broadcasted_iota(jnp.int32, (128, N), 0)
    mask_t = (class_rows == classes).astype(F32)
    onehot_t[...] = mask_t.astype(BF16)
    onehot = jnp.transpose(mask_t).astype(BF16)

    psi_rows = lax.broadcasted_iota(jnp.int32, (16, N), 0)
    apart = jnp.abs(psi_rows - psi_prev)
    apart = jnp.minimum(apart, 16 - apart).astype(F32)
    psi_term = -(apart * apart * F32(0.5 / 9.0))
    psi_rows_sc[0] = psi_term[0:8]
    psi_rows_sc[1] = psi_term[8:16]

    ag_wait(Z_)
    ag_start(*INNER[1])
    ag_start(outer(U1, 0), outer(D1, 0))
    ag_wait(*INNER[0])
    for p in (1, 2):
        ag_start(outer(U0, p), outer(D0, p))

    noise = noise_in[...]
    for j in range(8):
        lanes = slice(j * 256, (j + 1) * 256)
        ctf_now = ctf[:, lanes]
        noise_now = noise[:, lanes]
        gain_now = ctf_now * ctf_now / noise_now
        gain[:, lanes] = gain_now
        for k, piece in enumerate(split3(gain_now)):
            gain3[k, :, lanes] = piece
        high, middle, low = split3(ctf_now / noise_now)
        pick = onehot[:, 0:GROUPS]
        wsel[:, lanes] = (
            dot(pick, high, ((1,), (0,))) + dot(pick, middle, ((1,), (0,)))
        ) + dot(pick, low, ((1,), (0,)))

    loads[7].wait()
    loads[8].wait()
    loads[9].wait()

    ag_wait(outer(U0, 0))
    ag_start(outer(UR, 0))

    def align(part, carry):
        rows = pl.ds(pl.multiple_of(part * 32, 32), 32)
        base_c, base_s = [spin[0, rows]], [spin[1, rows]]
        step_c, step_s = spin[2, rows], spin[3, rows]
        turn_c, turn_s = spin[4, rows], spin[5, rows]
        for j in range(16):
            if j == 0:
                c, s = base_c[0], base_s[0]
            elif j < 4:
                pc, ps = base_c[j - 1], base_s[j - 1]
                c, s = pc * step_c - ps * step_s, ps * step_c + pc * step_s
                base_c.append(c)
                base_s.append(s)
            else:
                pc, ps = base_c[j % 4], base_s[j % 4]
                c, s = pc * turn_c - ps * turn_s, ps * turn_c + pc * turn_s
                base_c[j % 4], base_s[j % 4] = c, s
            lanes = slice(j * 128, (j + 1) * 128)
            real = img[rows, lanes].astype(F32)
            imag = img[rows, PIX + j * 128:PIX + (j + 1) * 128].astype(F32)
            weight = wsel[rows, lanes]
            h, jj = j // 8, j % 8
            al[h][rows, jj * 128:(jj + 1) * 128] = ((real * c + imag * s) * weight).astype(BF16)
            al[h][rows, HP + jj * 128:HP + (jj + 1) * 128] = (
                (imag * c - real * s) * weight
            ).astype(BF16)
        return carry

    lax.fori_loop(0, 8, align, 0)

    def cross_chunk(h, now, r):
        for j in range(8):
            lanes = slice(j * 128, (j + 1) * 128)
            wide = slice(h * HP + j * 128, h * HP + (j + 1) * 128)
            value = g[h][now, r, :, :, lanes].astype(F32)
            real, imag = value[:, 0:8], value[:, 8:16]
            mag[:, lanes] = (real * real + imag * imag).reshape(32, 128)

            def put(t, shifted_real, shifted_imag):
                rows = slice(t * 32, (t + 1) * 32)
                s_buf[h][rows, lanes] = shifted_real.reshape(32, 128).astype(BF16)
                s_buf[h][rows, HP + j * 128:HP + (j + 1) * 128] = (
                    shifted_imag.reshape(32, 128).astype(BF16)
                )

            put(4, real, imag)
            for q, (ty, tx) in enumerate(PAIRS):
                c = table_ref[2 * q:2 * q + 1, wide][None]
                s = table_ref[2 * q + 1:2 * q + 2, wide][None]
                rc_, is_, rs_, ic_ = real * c, imag * s, real * s, imag * c
                put(offset_index(ty, tx), rc_ - is_, rs_ + ic_)
                put(offset_index(-ty, -tx), rc_ + is_, ic_ - rs_)
        high, middle, low = split3(mag[...])
        half = slice(h * HP, (h + 1) * HP)
        by_high = dot(jnp.concatenate([high, middle, low], axis=0), gain3[0, :, half], ((1,), (1,)))
        by_middle = dot(jnp.concatenate([high, middle], axis=0), gain3[1, :, half], ((1,), (1,)))
        by_low = dot(high, gain3[2, :, half], ((1,), (1,)))
        small = (by_low + by_high[64:96]) + by_middle[32:64]
        energy = (small + (by_middle[0:32] + by_high[32:64])) + by_high[0:32]
        blocks = pl.ds(r * 4, 4)
        en[h, now, blocks, :, 0:GROUPS] = energy.reshape(4, 8, GROUPS)
        sc[h, now, :, blocks] = dot(s_buf[h][...], al[h][...], ((1,), (1,))).reshape(
            OFFSETS, 4, 8, N
        )

    def score_slab(py, places, top):
        blocks = [(r, px) for r in range(2) for px in places]
        energies = [
            en[0, py, r * 4 + px, :, 0:GROUPS] + en[1, px, r * 4 + py, :, 0:GROUPS]
            for r, px in blocks
        ]
        high, middle, low = split3(jnp.concatenate(energies, axis=0))
        picks = onehot_t[0:GROUPS]
        picked = (
            dot(high, picks, ((1,), (0,))) + dot(middle, picks, ((1,), (0,)))
        ) + dot(low, picks, ((1,), (0,)))
        penalty = 0.5 * picked
        owner_y = ring(y + ahead_of(py))
        tops = [top]
        for k, (r, px) in enumerate(blocks):
            owner_z = lax.rem(z + r, 2)
            owner_x = ring(x + (0, 1, 3, 2)[px])
            view = views_ref[owner_y * 4 + owner_z * 2 + owner_x // 2]
            prior = psi_rows_sc[lax.rem(owner_x, 2)] + jnp.where(
                ranges == view, F32(1.5), F32(0.0)
            )
            less = penalty[k * 8:(k + 1) * 8]
            values = []
            for t in range(OFFSETS):
                value = sc[0, py, t, r * 4 + px] + sc[1, px, t, r * 4 + py]
                value = (value - less) + prior
                sc[0, py, t, r * 4 + px] = value
                values.append(value)
            tops.append(tree(jnp.maximum, values))
        return tree(jnp.maximum, tops)

    def combine(py, b, e):
        by_row = []
        for ty in range(3):
            minus, zero, plus = e[3 * ty], e[3 * ty + 1], e[3 * ty + 2]
            by_row.append((zero, plus + minus, plus - minus))
        out = []
        for k in range(3):
            minus, zero, plus = by_row[0][k], by_row[1][k], by_row[2][k]
            out.append((zero, plus + minus, plus - minus))
        order = (
            out[0][0], out[1][0], out[0][1], out[1][1], out[2][2],
            out[2][0], out[2][1], out[0][2], out[1][2],
        )
        for k in range(OFFSETS):
            sc[1, py, k, b] = order[k]
        massn[py, b] = (out[0][0] + out[1][0]) + (out[0][1] + out[1][1])

    def exp_slab(py, places, top, total, combined):
        sums = [total]
        for r in range(2):
            for px in places:
                b = r * 4 + px
                values = []
                for t in range(OFFSETS):
                    value = jnp.exp(sc[0, py, t, b] - top)
                    if not combined:
                        sc[0, py, t, b] = value
                    values.append(value)
                sums.append(tree(jnp.add, values))
                if combined:
                    combine(py, b, values)
        return tree(jnp.add, sums)

    def combine_slab(py, places):
        for r in range(2):
            for px in places:
                b = r * 4 + px
                combine(py, b, [sc[0, py, t, b] for t in range(OFFSETS)])

    nearby, every, lowest = (0, 1, 2), (0, 1, 2, 3), jnp.full((8, N), -jnp.inf, F32)
    nothing = jnp.zeros((8, N), F32)

    def early_scores():
        top = lax.fori_loop(0, 3, lambda py, v: score_slab(py, nearby, v), lowest)
        top = jnp.max(top, axis=0, keepdims=True)
        total = lax.fori_loop(
            0, 3, lambda py, v: exp_slab(py, nearby, top, v, True), nothing
        )
        early[0:1] = top
        early[1:2] = jnp.sum(total, axis=0, keepdims=True)

    def relay(arrived, onward, *ps):
        for p in ps:
            ag_wait(outer(arrived, p))
            ag_start(outer(onward, p))

    def cross_step(i, carry):
        @pl.when(i == 1)
        def _():
            ag_wait(*INNER[1])
            for p in (1, 2):
                ag_start(outer(D1, p), outer(U1, p))

        @pl.when(i == 2)
        def _():
            relay(U0, UR, 1, 2)
            relay(D1, DR, 0)
            ag_wait(outer(D0, 0), outer(D0, 1), outer(D0, 2))

        @pl.when(i == 4)
        def _():
            relay(D1, DR, 1, 2)

        @pl.when(i == 5)
        def _():
            ag_wait(outer(U1, 0), outer(U1, 1), outer(U1, 2))

        @pl.when(i == 6)
        def _():
            early_scores()
            ag_wait(outer(UR, 0), outer(UR, 1), outer(UR, 2))

        @pl.when(i == 7)
        def _():
            ag_wait(outer(DR, 0), outer(DR, 1), outer(DR, 2))

        u, v = i // 2, lax.rem(i, 2)
        sides = (u * (3 - u)) // 2
        now = sides * (1 + v) + (1 - sides) * u
        r = sides * (u - 1) + (1 - sides) * v
        for h in range(2):
            cross_chunk(h, now, r)
        return carry

    lax.fori_loop(0, 8, cross_step, 0)

    late_top = lax.fori_loop(0, 3, lambda py, v: score_slab(py, (3,), v), lowest)
    late_top = jnp.max(score_slab(3, every, late_top), axis=0, keepdims=True)
    late_total = lax.fori_loop(
        0, 3, lambda py, v: exp_slab(py, (3,), late_top, v, False), nothing
    )
    late_total = jnp.sum(
        exp_slab(3, every, late_top, late_total, False), axis=0, keepdims=True
    )
    early_top = early[0:1]
    top = jnp.maximum(early_top, late_top)
    total = early[1:2] * jnp.exp(early_top - top) + late_total * jnp.exp(late_top - top)

    for half in range(2):
        lanes = slice(half * 128, (half + 1) * 128)
        st[me_dir, half:half + 1] = top[:, lanes]
        st[me_dir, 2 + half:3 + half] = total[:, lanes]

    def dir_copy(o):
        return pltpu.make_async_remote_copy(
            src_ref=st.at[me_dir], dst_ref=st.at[me_dir], send_sem=dir_send.at[o - 1],
            recv_sem=dir_recv.at[o - 1], device_id=dir_peers[o - 1], device_id_type=MESH,
        )

    def dir_arrival(o):
        source = lax.rem(me_dir + 8 - o, 8)
        return pltpu.make_async_remote_copy(
            src_ref=st.at[source], dst_ref=st.at[source], send_sem=dir_send.at[o - 1],
            recv_sem=dir_recv.at[o - 1], device_id=dir_peers[o - 1], device_id_type=MESH,
        )

    for o in (4, 5, 3, 2, 6, 7, 1):
        dir_copy(o).start()

    def combine_late(py, carry):
        combine_slab(py, (3,))
        return carry

    lax.fori_loop(0, 3, combine_late, 0)
    combine_slab(3, every)
    for h in range(2):
        for k in range(25):
            ag(h, k).wait_send()

    for o in range(1, 8):
        dir_arrival(o).wait_recv()

    def joined(d, row):
        return jnp.concatenate([st[d, row:row + 1], st[d, row + 1:row + 2]], axis=1)

    tops = [joined(d, 0) for d in range(8)]
    best = tops[0]
    for d in range(1, 8):
        best = jnp.maximum(best, tops[d])
    mass_all = joined(0, 2) * jnp.exp(tops[0] - best)
    for d in range(1, 8):
        mass_all = mass_all + joined(d, 2) * jnp.exp(tops[d] - best)
    log_norm = best + jnp.log(mass_all)
    stats_ref[0:1] = log_norm
    stats_ref[1:2] = jnp.exp(best - log_norm)
    factor[0] = jnp.broadcast_to(jnp.exp(early_top - log_norm), (8, N))
    factor[1] = jnp.broadcast_to(jnp.exp(late_top - log_norm), (8, N))

    def insert_chunk(h, now):
        scale = [factor[now // 3]] * 3 + [factor[1]]
        for zz in range(2):
            for cp in range(2):
                pair = []
                for c in range(2):
                    cc = 2 * cp + c
                    if h == 0:
                        pair.append(sc[1, now, :, zz * 4 + cc] * scale[cc])
                    else:
                        pair.append(sc[1, cc, :, zz * 4 + now] * scale[cc])
                l_buf[h][:, zz * 2 + cp] = jnp.concatenate(pair, axis=1).astype(BF16)
        left = l_buf[h][...].reshape(OFFSETS * 64, N)
        for q in range(4):
            lanes = slice(q * 256, (q + 1) * 256)
            wide = slice(h * HP + q * 256, h * HP + (q + 1) * 256)
            real = dot(left, al[h][:, lanes], ((1,), (0,))).reshape(OFFSETS, 64, 256)
            imag = dot(
                left, al[h][:, HP + q * 256:HP + (q + 1) * 256], ((1,), (0,))
            ).reshape(OFFSETS, 64, 256)
            total_real, total_imag = real[0], imag[0]
            for k in range(4):
                w = table_ref[8 + k:9 + k, wide]
                total_real = total_real + w * real[1 + k]
                total_imag = total_imag + w * imag[1 + k]
            for k in range(4):
                w = table_ref[12 + k:13 + k, wide]
                total_real = total_real + w * imag[5 + k]
                total_imag = total_imag - w * real[5 + k]
            rp[h][now, :, 0:8, lanes] = total_real.reshape(8, 8, 256)
            rp[h][now, :, 8:16, lanes] = total_imag.reshape(8, 8, 256)
        if h == 0:
            weighted = [massn[now, b] * scale[b % 4] for b in range(8)]
            high, middle, _ = split3(jnp.concatenate(weighted, axis=0))
            masses = dot(high, onehot_t[...], ((1,), (1,))) + dot(
                middle, onehot_t[...], ((1,), (1,))
            )
            rp[h][now, :, 0:8, HP:HP + 128] = masses.reshape(8, 8, 128)
            rp[h][now, :, 8:16, HP:HP + 128] = jnp.zeros((8, 8, 128), F32)

    def rs(h, k):
        if k < 12:
            kind, part = k // 2, PARTS[k % 2]
            src, dst = sb[h].at[kind, part], rb[h].at[kind, part]
            target = up2[h] if kind < 3 else down2[h]
        elif k < 18:
            src, dst = sb2[h].at[k - 12], rb2[h].at[k - 12]
            target = (far1, up1, down1)[(k - 12) % 3][h]
        else:
            src, dst, target = sb3[h], rb3[h], z_other
        return pltpu.make_async_remote_copy(
            src_ref=src, dst_ref=dst, send_sem=rs_send.at[h, k], recv_sem=rs_recv.at[h, k],
            device_id=target, device_id_type=MESH,
        )

    def put(h, kind, place, r, p, add=None):
        part = PARTS[p]
        rows = slice(r * 4 + part.start, r * 4 + part.stop)
        value = rp[h][place, rows]
        if add is not None:
            rs(h, 2 * add + p).wait_recv()
            value = value + rb[h][add, part].astype(F32)
        sb[h][kind, part] = value.astype(BF16)
        rs(h, 2 * kind + p).start()

    def insert_step(i, carry):
        @pl.when(i == 3)
        def _():
            for h in range(2):
                put(h, 2, 1, 0, 0, add=0)
                put(h, 5, 2, 1, 0, add=3)

        for h in range(2):
            insert_chunk(h, 3 - i)

            @pl.when(i == 0)
            def _():
                for p in range(2):
                    put(h, 0, 3, 0, p)
                    put(h, 3, 3, 1, p)

            @pl.when(i == 1)
            def _():
                put(h, 4, 2, 0, 0)

            @pl.when(i == 2)
            def _():
                put(h, 1, 1, 1, 0)

        return carry

    lax.fori_loop(0, 4, insert_step, 0)

    for h in range(2):
        put(h, 4, 2, 0, 1)
        put(h, 1, 1, 1, 1)
        put(h, 2, 1, 0, 1, add=0)
        put(h, 5, 2, 1, 1, add=3)

    def take(h, p, r):
        part = PARTS[p]
        from_below, from_above = ((2, 4), (1, 5))[r]
        rs(h, 2 * from_below + p).wait_recv()
        rs(h, 2 * from_above + p).wait_recv()
        rows = slice(r * 4 + part.start, r * 4 + part.stop)
        return (
            rp[h][0, rows] + rb[h][from_below, part].astype(F32)
        ) + rb[h][from_above, part].astype(F32)

    for r in (1, 0):
        for h in range(2):
            above, below, far = (0, 1, 2)
            taken = take(h, 0, r)
            for k, place in enumerate((far, above, below)):
                sb2[h][3 * r + k] = taken[place].astype(BF16)
                rs(h, 12 + 3 * r + k).start()

    def own(h, r):
        total = take(h, 1, r)[0]
        for k in range(3):
            rs(h, 12 + 3 * r + k).wait_recv()
            total = total + rb2[h][3 * r + k].astype(F32)
        return total

    for h in range(2):
        sb3[h][...] = own(h, 1).astype(BF16)
        rs(h, 18).start()
    mine = [own(h, 0) for h in range(2)]

    for h in range(2):
        for k in range(18):
            rs(h, k).wait_send()
    for o in range(1, 8):
        dir_copy(o).wait_send()

    for h in range(2):
        rs(h, 18).wait_recv()
        result = mine[h] + rb3[h][...].astype(F32)
        sums_ref[:, h * HP:(h + 1) * HP] = result[0:8, 0:HP]
        sums_ref[:, PIX + h * HP:PIX + (h + 1) * HP] = result[8:16, 0:HP]
        if h == 0:
            weights_ref[...] = lax.dot_general(
                result[0:8, HP:HP + GROUPS], gain[...], (((1,), (0,)), ((), ())),
                precision=lax.Precision.HIGHEST, preferred_element_type=F32,
            )

    for h in range(2):
        rs(h, 18).wait_send()


def finish(sums_in, weights_in, stats_in, sums_ref, weights_ref, norm_ref, peak_ref):
    sums_ref[...] = sums_in[...]
    weights_ref[...] = weights_in[...]
    norm_ref[...] = stats_in[0:1]
    peak_ref[...] = stats_in[1:2]


def per_device(
    images, refs, ctf, noise_var, shifts, ctf_class, psi_prev, earlier_direction_range, view_range
):
    vmem = pl.BlockSpec(memory_space=pltpu.VMEM)
    hbm = pl.BlockSpec(memory_space=pl.ANY)
    wa, wb = WIDTHS
    dma = pltpu.SemaphoreType.DMA
    out = pl.pallas_call(
        kernel,
        out_shape=(
            jax.ShapeDtypeStruct((8, 2 * PIX), F32),
            jax.ShapeDtypeStruct((8, PIX), F32),
            jax.ShapeDtypeStruct((8, N), F32),
        ),
        in_specs=[hbm] * 10,
        out_specs=(vmem, vmem, vmem),
        scratch_shapes=[
            pltpu.SMEM((16,), jnp.int32),
            pltpu.VMEM((N, 2 * PIX), BF16),
            pltpu.VMEM((8, 2 * PIX), BF16),
            pltpu.VMEM((GROUPS, PIX), F32),
            pltpu.VMEM((1, PIX), F32),
            pltpu.VMEM((8, N), jnp.int32),
            pltpu.VMEM((2, N), jnp.int32),
            pltpu.VMEM((16, PIX), F32),
            pltpu.VMEM((4, 2, 4, 16, HP), BF16),
            pltpu.VMEM((4, 2, 4, 16, HP), BF16),
            pltpu.VMEM((N, 2 * HP), BF16),
            pltpu.VMEM((N, 2 * HP), BF16),
            pltpu.VMEM((N, PIX), F32),
            pltpu.VMEM((6, N, 128), F32),
            pltpu.VMEM((OFFSETS * 32, 2 * HP), BF16),
            pltpu.VMEM((OFFSETS * 32, 2 * HP), BF16),
            pltpu.VMEM((32, HP), F32),
            pltpu.VMEM((GROUPS, PIX), F32),
            pltpu.VMEM((3, GROUPS, PIX), BF16),
            pltpu.VMEM((2, 4, 8, 8, 128), F32),
            pltpu.VMEM((128, N), BF16),
            pltpu.VMEM((2, 8, N), F32),
            pltpu.VMEM((2, 4, OFFSETS, 8, 8, N), F32),
            pltpu.VMEM((4, 8, 8, N), F32),
            pltpu.VMEM((8, N), F32),
            pltpu.VMEM((2, 8, N), F32),
            pltpu.VMEM((OFFSETS, 4, 16, N), BF16),
            pltpu.VMEM((OFFSETS, 4, 16, N), BF16),
            pltpu.VMEM((4, 8, 16, wa), F32),
            pltpu.VMEM((4, 8, 16, wb), F32),
            pltpu.VMEM((8, 8, 128), F32),
            pltpu.VMEM((6, 4, 16, wa), BF16),
            pltpu.VMEM((6, 4, 16, wb), BF16),
            pltpu.VMEM((6, 4, 16, wa), BF16),
            pltpu.VMEM((6, 4, 16, wb), BF16),
            pltpu.VMEM((6, 16, wa), BF16),
            pltpu.VMEM((6, 16, wb), BF16),
            pltpu.VMEM((6, 16, wa), BF16),
            pltpu.VMEM((6, 16, wb), BF16),
            pltpu.VMEM((16, wa), BF16),
            pltpu.VMEM((16, wb), BF16),
            pltpu.VMEM((16, wa), BF16),
            pltpu.VMEM((16, wb), BF16),
            dma((10,)),
            dma((2, 25)),
            dma((2, 25)),
            dma((7,)),
            dma((7,)),
            dma((2, 19)),
            dma((2, 19)),
        ],
        compiler_params=pltpu.CompilerParams(
            collective_id=0, has_side_effects=True, vmem_limit_bytes=60 * 2**20
        ),
        cost_estimate=pl.CostEstimate(
            flops=10_000_000_000, bytes_accessed=4_000_000, transcendentals=600_000
        ),
        name="expectation_step",
    )(
        images, refs, ctf, noise_var.reshape(1, PIX), ctf_class.reshape(1, N),
        psi_prev.reshape(1, N), earlier_direction_range.reshape(1, N), shifts.T, view_range,
        jnp.asarray(phase_constants()),
    )
    class_sums, weight_sums, log_norm, peak_prob = pl.pallas_call(
        finish,
        out_shape=(
            jax.ShapeDtypeStruct((8, 2 * PIX), F32),
            jax.ShapeDtypeStruct((8, PIX), F32),
            jax.ShapeDtypeStruct((1, N), F32),
            jax.ShapeDtypeStruct((1, N), F32),
        ),
        in_specs=[vmem] * 3,
        out_specs=(vmem,) * 4,
        name="finish",
    )(*out)
    return class_sums, weight_sums, log_norm.reshape(N), peak_prob.reshape(N)


def solution(mesh):
    placed = (
        P("dom", None),
        P(("dir", "dom"), None),
        P(),
        P(),
        P("dom", None),
        P("dom"),
        P("dom"),
        P("dom"),
        P("dir"),
    )
    return jax.shard_map(
        per_device,
        mesh=mesh,
        in_specs=placed,
        out_specs=(P(("dir", "dom"), None), P(("dir", "dom"), None), P("dom"), P("dom")),
        check_vma=False,
    )
```

```python
import math

import jax
import jax.numpy as jnp
import numpy as np
from jax import lax
from jax.experimental import pallas as pl
from jax.experimental.pallas import tpu as pltpu
from jax.sharding import PartitionSpec as P

CROP = 64
HALF = 32
PIX = 2048
OFFSETS = 9
GROUPS = 64
N = 256
BLOCKS = 32
HP = 1024
WIDTHS = (HP + 128, HP)
THETA = 2.0 * math.pi / CROP

F32 = jnp.float32
BF16 = jnp.bfloat16
MESH = pl.DeviceIdType.MESH

PAIRS = ((0, 1), (1, 0), (1, 1), (1, -1))


def offset_index(ty, tx):
    return (ty + 1) * 3 + (tx + 1)


def phase_constants():
    pixels = np.arange(PIX)
    alpha = THETA * (pixels // HALF)
    beta = THETA * (pixels % HALF)
    rows = []
    for ty, tx in PAIRS:
        angle = ty * alpha + tx * beta
        rows += [np.cos(angle), np.sin(angle)]
    ca, sa, cb, sb = np.cos(alpha), np.sin(alpha), np.cos(beta), np.sin(beta)
    rows += [cb, ca, ca * cb, -sa * sb, sb, ca * sb, sa, sa * cb]
    return np.stack(rows).astype(np.float32)


def cos_sin(index):
    m = jnp.bitwise_and(index, 63) + 8
    quarter = jnp.bitwise_and(jnp.right_shift(m, 4), 3)
    x = (jnp.bitwise_and(m, 15) - 8).astype(F32) * F32(THETA)
    x2 = x * x
    c = 1.0 + x2 * (-0.5 + x2 * (1 / 24 + x2 * (-1 / 720 + x2 * (1 / 40320))))
    s = x * (1.0 + x2 * (-1 / 6 + x2 * (1 / 120 + x2 * (-1 / 5040 + x2 * (1 / 362880)))))
    odd = jnp.bitwise_and(quarter, 1) == 1
    cc = jnp.where(odd, s, c)
    ss = jnp.where(odd, c, s)
    cos = jnp.where((quarter == 1) | (quarter == 2), -cc, cc)
    sin = jnp.where(quarter >= 2, -ss, ss)
    return cos, sin


def split3(value):
    high = value.astype(BF16)
    rest = value - high.astype(F32)
    middle = rest.astype(BF16)
    low = (rest - middle.astype(F32)).astype(BF16)
    return high, middle, low


def dot(a, b, dims):
    return lax.dot_general(a, b, (dims, ((), ())), preferred_element_type=F32)


def tree(op, values):
    while len(values) > 1:
        pairs = [op(a, b) for a, b in zip(values[::2], values[1::2])]
        values = pairs + values[len(pairs) * 2:]
    return values[0]


def ring(i):
    return lax.rem(i + 8, 4)


def ahead_of(place):
    return lax.rem((place * (place + 1)) // 2, 4)


PIECES = (slice(0, 1), slice(1, 3), slice(3, 4))
PARTS = (slice(1, 4), slice(0, 1))


def kernel(
    images_ref, refs_ref, ctf_ref, noise_ref, class_ref, psi_ref, range_ref, shift_ref,
    views_in, table_in,
    sums_ref, weights_ref, stats_ref,
    views_ref, img, refs_in, ctf, noise_in, ints, shift_in, table_ref,
    g_a, g_b, al_a, al_b, wsel, spin, s_a, s_b, mag, gain, gain3, en, onehot_t, psi_rows_sc,
    sc, massn, early, factor, l_a, l_b, rp_a, rp_b,
    st, sb_a, sb_b, rb_a, rb_b, sb2_a, sb2_b, rb2_a, rb2_b, sb3_a, sb3_b, rb3_a, rb3_b,
    load_sem, ag_send, ag_recv, dir_send, dir_recv, rs_send, rs_recv,
):
    g = (g_a, g_b)
    al = (al_a, al_b)
    s_buf = (s_a, s_b)
    l_buf = (l_a, l_b)
    rp = (rp_a, rp_b)
    sb, rb = (sb_a, sb_b), (rb_a, rb_b)
    sb2, rb2 = (sb2_a, sb2_b), (rb2_a, rb2_b)
    sb3, rb3 = (sb3_a, sb3_b), (rb3_a, rb3_b)

    me_dir = lax.axis_index("dir")
    me_dom = lax.axis_index("dom")
    y = me_dom // 8
    z = lax.rem(me_dom // 4, 2)
    x = lax.rem(me_dom, 4)

    def device(yy, zz, xx):
        return (me_dir, (yy * 2 + zz) * 4 + xx)

    x_up, x_down = device(y, z, ring(x + 1)), device(y, z, ring(x - 1))
    y_up, y_down = device(ring(y + 1), z, x), device(ring(y - 1), z, x)
    z_other = device(y, 1 - z, x)
    dir_peers = [(lax.rem(me_dir + o, 8), me_dom) for o in range(1, 8)]

    up2, down2 = (y_up, x_up), (y_down, x_down)
    up1, down1 = (x_up, y_up), (x_down, y_down)
    far1 = (device(y, z, ring(x + 2)), device(ring(y + 2), z, x))

    barrier = pltpu.get_barrier_semaphore()
    partners = [z_other, x_up, x_down, y_up, y_down, *far1] + dir_peers
    for p in partners:
        pl.semaphore_signal(barrier, inc=1, device_id=p, device_id_type=MESH)

    loads = [
        pltpu.make_async_copy(src, dst, load_sem.at[k])
        for k, (src, dst) in enumerate((
            (refs_ref, refs_in), (shift_ref, shift_in), (class_ref, ints.at[0:1]),
            (psi_ref, ints.at[1:2]), (range_ref, ints.at[2:3]), (noise_ref, noise_in),
            (ctf_ref, ctf), (images_ref, img), (table_in, table_ref),
            (views_in, views_ref),
        ))
    ]
    for load in loads:
        load.start()

    loads[0].wait()
    for h in range(2):
        real = refs_in[:, h * HP:(h + 1) * HP].astype(F32)
        imag = refs_in[:, PIX + h * HP:PIX + (h + 1) * HP].astype(F32)
        g[h][0, 0, 0] = jnp.concatenate([real, imag], axis=0).astype(BF16)

    pl.semaphore_wait(barrier, len(partners))

    def ag(h, k):
        buf = g[h]
        if k == 0:
            src, dst, target = buf.at[0, 0, 0], buf.at[0, 1, 0], z_other
        elif k < 7:
            r, way = (k - 1) % 2, (k - 1) // 2
            target = (up1, down1, far1)[way][h]
            src, dst = buf.at[0, r, 0], buf.at[0, r, (2, 1, 3)[way]]
        else:
            piece = PIECES[(k - 7) % 3]
            kind = (k - 7) // 3
            upward = kind < 3
            target = up2[h] if upward else down2[h]
            side = 2 if upward else 1
            if kind % 3 < 2:
                r = kind % 3
                src, dst = buf.at[0, r, piece], buf.at[side, r, piece]
            else:
                r = 0 if upward else 1
                src, dst = buf.at[side, r, piece], buf.at[3, r, piece]
        return pltpu.make_async_remote_copy(
            src_ref=src, dst_ref=dst, send_sem=ag_send.at[h, k], recv_sem=ag_recv.at[h, k],
            device_id=target, device_id_type=MESH,
        )

    def ag_start(*ks):
        for k in ks:
            for h in range(2):
                ag(h, k).start()

    def ag_wait(*ks):
        for k in ks:
            for h in range(2):
                ag(h, k).wait_recv()

    Z_, INNER = 0, ((1, 3, 5), (2, 4, 6))

    def outer(kind, piece):
        return 7 + 3 * kind + piece

    U0, U1, UR, D0, D1, DR = range(6)

    ag_start(Z_, *INNER[0])
    ag_start(outer(U0, 0), outer(D0, 0))

    for k in range(1, 7):
        loads[k].wait()
    classes = ints[0:1, :]
    psi_prev = ints[1:2, :]
    ranges = ints[2:3, :]

    def column(row):
        wide = jnp.broadcast_to(row.astype(F32), (128, N))
        return jnp.transpose(wide).astype(jnp.int32)

    shift_y = column(shift_in[0:1, :])
    shift_x = column(shift_in[1:2, :])
    lane = lax.broadcasted_iota(jnp.int32, (N, 128), 1)
    fc, fs = cos_sin(
        jnp.bitwise_and(lane, 31) * shift_x + jnp.right_shift(lane, 5) * shift_y
    )
    spin[0], spin[1] = fc, fs
    rc, rs_ = cos_sin(4 * shift_y)
    spin[2], spin[3] = rc, rs_
    qc, qs = cos_sin(16 * shift_y)
    spin[4], spin[5] = qc, qs

    class_rows = lax.broadcasted_iota(jnp.int32, (128, N), 0)
    mask_t = (class_rows == classes).astype(F32)
    onehot_t[...] = mask_t.astype(BF16)
    onehot = jnp.transpose(mask_t).astype(BF16)

    psi_rows = lax.broadcasted_iota(jnp.int32, (16, N), 0)
    apart = jnp.abs(psi_rows - psi_prev)
    apart = jnp.minimum(apart, 16 - apart).astype(F32)
    psi_term = -(apart * apart * F32(0.5 / 9.0))
    psi_rows_sc[0] = psi_term[0:8]
    psi_rows_sc[1] = psi_term[8:16]

    ag_wait(Z_)
    ag_start(*INNER[1])
    ag_start(outer(U1, 0), outer(D1, 0))
    ag_wait(*INNER[0])
    for p in (1, 2):
        ag_start(outer(U0, p), outer(D0, p))

    noise = noise_in[...]
    for j in range(8):
        lanes = slice(j * 256, (j + 1) * 256)
        ctf_now = ctf[:, lanes]
        noise_now = noise[:, lanes]
        gain_now = ctf_now * ctf_now / noise_now
        gain[:, lanes] = gain_now
        for k, piece in enumerate(split3(gain_now)):
            gain3[k, :, lanes] = piece
        high, middle, low = split3(ctf_now / noise_now)
        pick = onehot[:, 0:GROUPS]
        wsel[:, lanes] = (
            dot(pick, high, ((1,), (0,))) + dot(pick, middle, ((1,), (0,)))
        ) + dot(pick, low, ((1,), (0,)))

    loads[7].wait()
    loads[8].wait()
    loads[9].wait()

    ag_wait(outer(U0, 0))
    ag_start(outer(UR, 0))

    def align(part, carry):
        rows = pl.ds(pl.multiple_of(part * 32, 32), 32)
        base_c, base_s = [spin[0, rows]], [spin[1, rows]]
        step_c, step_s = spin[2, rows], spin[3, rows]
        turn_c, turn_s = spin[4, rows], spin[5, rows]
        for j in range(16):
            if j == 0:
                c, s = base_c[0], base_s[0]
            elif j < 4:
                pc, ps = base_c[j - 1], base_s[j - 1]
                c, s = pc * step_c - ps * step_s, ps * step_c + pc * step_s
                base_c.append(c)
                base_s.append(s)
            else:
                pc, ps = base_c[j % 4], base_s[j % 4]
                c, s = pc * turn_c - ps * turn_s, ps * turn_c + pc * turn_s
                base_c[j % 4], base_s[j % 4] = c, s
            lanes = slice(j * 128, (j + 1) * 128)
            real = img[rows, lanes].astype(F32)
            imag = img[rows, PIX + j * 128:PIX + (j + 1) * 128].astype(F32)
            weight = wsel[rows, lanes]
            h, jj = j // 8, j % 8
            al[h][rows, jj * 128:(jj + 1) * 128] = ((real * c + imag * s) * weight).astype(BF16)
            al[h][rows, HP + jj * 128:HP + (jj + 1) * 128] = (
                (imag * c - real * s) * weight
            ).astype(BF16)
        return carry

    lax.fori_loop(0, 8, align, 0)

    def cross_chunk(h, slabs, r):
        many = 32 * len(slabs)
        for j in range(8):
            lanes = slice(j * 128, (j + 1) * 128)
            wide = slice(h * HP + j * 128, h * HP + (j + 1) * 128)
            value = jnp.concatenate(
                [g[h][now, r, :, :, lanes].astype(F32) for now in slabs], axis=0
            )
            real, imag = value[:, 0:8], value[:, 8:16]
            mag[0:many, lanes] = (real * real + imag * imag).reshape(many, 128)

            def put(t, shifted_real, shifted_imag):
                rows = slice(t * many, (t + 1) * many)
                s_buf[h][rows, lanes] = shifted_real.reshape(many, 128).astype(BF16)
                s_buf[h][rows, HP + j * 128:HP + (j + 1) * 128] = (
                    shifted_imag.reshape(many, 128).astype(BF16)
                )

            put(4, real, imag)
            for q, (ty, tx) in enumerate(PAIRS):
                c = table_ref[2 * q:2 * q + 1, wide][None]
                s = table_ref[2 * q + 1:2 * q + 2, wide][None]
                rc_, is_, rs_, ic_ = real * c, imag * s, real * s, imag * c
                put(offset_index(ty, tx), rc_ - is_, rs_ + ic_)
                put(offset_index(-ty, -tx), rc_ + is_, ic_ - rs_)
        high, middle, low = split3(mag[0:many])
        half = slice(h * HP, (h + 1) * HP)
        by_high = dot(jnp.concatenate([high, middle, low], axis=0), gain3[0, :, half], ((1,), (1,)))
        by_middle = dot(jnp.concatenate([high, middle], axis=0), gain3[1, :, half], ((1,), (1,)))
        by_low = dot(high, gain3[2, :, half], ((1,), (1,)))
        small = (by_low + by_high[2 * many:]) + by_middle[many:]
        energy = (small + (by_middle[0:many] + by_high[many:2 * many])) + by_high[0:many]
        energy = energy.reshape(len(slabs), 4, 8, GROUPS)
        cross = dot(s_buf[h][0:OFFSETS * many], al[h][...], ((1,), (1,))).reshape(
            OFFSETS, len(slabs), 4, 8, N
        )
        blocks = pl.ds(r * 4, 4)
        for k, now in enumerate(slabs):
            en[h, now, blocks, :, 0:GROUPS] = energy[k]
            sc[h, now, :, blocks] = cross[:, k]

    def score_slab(py, places, top):
        blocks = [(r, px) for r in range(2) for px in places]
        energies = [
            en[0, py, r * 4 + px, :, 0:GROUPS] + en[1, px, r * 4 + py, :, 0:GROUPS]
            for r, px in blocks
        ]
        high, middle, low = split3(jnp.concatenate(energies, axis=0))
        picks = onehot_t[0:GROUPS]
        picked = (
            dot(high, picks, ((1,), (0,))) + dot(middle, picks, ((1,), (0,)))
        ) + dot(low, picks, ((1,), (0,)))
        penalty = 0.5 * picked
        owner_y = ring(y + ahead_of(py))
        tops = [top]
        for k, (r, px) in enumerate(blocks):
            owner_z = lax.rem(z + r, 2)
            owner_x = ring(x + (0, 1, 3, 2)[px])
            view = views_ref[owner_y * 4 + owner_z * 2 + owner_x // 2]
            prior = psi_rows_sc[lax.rem(owner_x, 2)] + jnp.where(
                ranges == view, F32(1.5), F32(0.0)
            )
            less = penalty[k * 8:(k + 1) * 8]
            values = []
            for t in range(OFFSETS):
                value = sc[0, py, t, r * 4 + px] + sc[1, px, t, r * 4 + py]
                value = (value - less) + prior
                sc[0, py, t, r * 4 + px] = value
                values.append(value)
            tops.append(tree(jnp.maximum, values))
        return tree(jnp.maximum, tops)

    def combine(py, b, e):
        by_row = []
        for ty in range(3):
            minus, zero, plus = e[3 * ty], e[3 * ty + 1], e[3 * ty + 2]
            by_row.append((zero, plus + minus, plus - minus))
        out = []
        for k in range(3):
            minus, zero, plus = by_row[0][k], by_row[1][k], by_row[2][k]
            out.append((zero, plus + minus, plus - minus))
        order = (
            out[0][0], out[1][0], out[0][1], out[1][1], out[2][2],
            out[2][0], out[2][1], out[0][2], out[1][2],
        )
        for k in range(OFFSETS):
            sc[1, py, k, b] = order[k]
        massn[py, b] = (out[0][0] + out[1][0]) + (out[0][1] + out[1][1])

    def exp_slab(py, places, top, total, combined):
        sums = [total]
        for r in range(2):
            for px in places:
                b = r * 4 + px
                values = []
                for t in range(OFFSETS):
                    value = jnp.exp(sc[0, py, t, b] - top)
                    if not combined:
                        sc[0, py, t, b] = value
                    values.append(value)
                sums.append(tree(jnp.add, values))
                if combined:
                    combine(py, b, values)
        return tree(jnp.add, sums)

    def combine_slab(py, places):
        for r in range(2):
            for px in places:
                b = r * 4 + px
                combine(py, b, [sc[0, py, t, b] for t in range(OFFSETS)])

    nearby, every, lowest = (0, 1, 2), (0, 1, 2, 3), jnp.full((8, N), -jnp.inf, F32)
    nothing = jnp.zeros((8, N), F32)

    def early_scores():
        top = lax.fori_loop(0, 3, lambda py, v: score_slab(py, nearby, v), lowest)
        top = jnp.max(top, axis=0, keepdims=True)
        total = lax.fori_loop(
            0, 3, lambda py, v: exp_slab(py, nearby, top, v, True), nothing
        )
        early[0:1] = top
        early[1:2] = jnp.sum(total, axis=0, keepdims=True)

    def relay(arrived, onward, *ps):
        for p in ps:
            ag_wait(outer(arrived, p))
            ag_start(outer(onward, p))

    def own_step(r, carry):
        @pl.when(r == 1)
        def _():
            ag_wait(*INNER[1])
            for p in (1, 2):
                ag_start(outer(D1, p), outer(U1, p))

        for h in range(2):
            cross_chunk(h, (0,), r)
        return carry

    def sides_step(r, carry):
        @pl.when(r == 0)
        def _():
            relay(U0, UR, 1, 2)
            relay(D1, DR, 0)
            ag_wait(outer(D0, 0), outer(D0, 1), outer(D0, 2))

        @pl.when(r == 1)
        def _():
            relay(D1, DR, 1, 2)
            ag_wait(outer(U1, 0), outer(U1, 1), outer(U1, 2))

        for h in range(2):
            cross_chunk(h, (1, 2), r)
        return carry

    def far_step(r, carry):
        @pl.when(r == 0)
        def _():
            early_scores()
            ag_wait(outer(UR, 0), outer(UR, 1), outer(UR, 2))

        @pl.when(r == 1)
        def _():
            ag_wait(outer(DR, 0), outer(DR, 1), outer(DR, 2))

        for h in range(2):
            cross_chunk(h, (3,), r)
        return carry

    lax.fori_loop(0, 2, own_step, 0)
    lax.fori_loop(0, 2, sides_step, 0)
    lax.fori_loop(0, 2, far_step, 0)

    late_top = lax.fori_loop(0, 3, lambda py, v: score_slab(py, (3,), v), lowest)
    late_top = jnp.max(score_slab(3, every, late_top), axis=0, keepdims=True)
    late_total = lax.fori_loop(
        0, 3, lambda py, v: exp_slab(py, (3,), late_top, v, False), nothing
    )
    late_total = jnp.sum(
        exp_slab(3, every, late_top, late_total, False), axis=0, keepdims=True
    )
    early_top = early[0:1]
    top = jnp.maximum(early_top, late_top)
    total = early[1:2] * jnp.exp(early_top - top) + late_total * jnp.exp(late_top - top)

    for half in range(2):
        lanes = slice(half * 128, (half + 1) * 128)
        st[me_dir, half:half + 1] = top[:, lanes]
        st[me_dir, 2 + half:3 + half] = total[:, lanes]

    def dir_copy(o):
        return pltpu.make_async_remote_copy(
            src_ref=st.at[me_dir], dst_ref=st.at[me_dir], send_sem=dir_send.at[o - 1],
            recv_sem=dir_recv.at[o - 1], device_id=dir_peers[o - 1], device_id_type=MESH,
        )

    def dir_arrival(o):
        source = lax.rem(me_dir + 8 - o, 8)
        return pltpu.make_async_remote_copy(
            src_ref=st.at[source], dst_ref=st.at[source], send_sem=dir_send.at[o - 1],
            recv_sem=dir_recv.at[o - 1], device_id=dir_peers[o - 1], device_id_type=MESH,
        )

    for o in (4, 5, 3, 2, 6, 7, 1):
        dir_copy(o).start()

    def combine_late(py, carry):
        combine_slab(py, (3,))
        return carry

    lax.fori_loop(0, 3, combine_late, 0)
    combine_slab(3, every)
    for h in range(2):
        for k in range(25):
            ag(h, k).wait_send()

    for o in range(1, 8):
        dir_arrival(o).wait_recv()

    def joined(d, row):
        return jnp.concatenate([st[d, row:row + 1], st[d, row + 1:row + 2]], axis=1)

    tops = [joined(d, 0) for d in range(8)]
    best = tops[0]
    for d in range(1, 8):
        best = jnp.maximum(best, tops[d])
    mass_all = joined(0, 2) * jnp.exp(tops[0] - best)
    for d in range(1, 8):
        mass_all = mass_all + joined(d, 2) * jnp.exp(tops[d] - best)
    log_norm = best + jnp.log(mass_all)
    stats_ref[0:1] = log_norm
    stats_ref[1:2] = jnp.exp(best - log_norm)
    factor[0] = jnp.broadcast_to(jnp.exp(early_top - log_norm), (8, N))
    factor[1] = jnp.broadcast_to(jnp.exp(late_top - log_norm), (8, N))

    def insert_chunk(h, now):
        scale = [factor[now // 3]] * 3 + [factor[1]]
        for zz in range(2):
            for cp in range(2):
                pair = []
                for c in range(2):
                    cc = 2 * cp + c
                    if h == 0:
                        pair.append(sc[1, now, :, zz * 4 + cc] * scale[cc])
                    else:
                        pair.append(sc[1, cc, :, zz * 4 + now] * scale[cc])
                l_buf[h][:, zz * 2 + cp] = jnp.concatenate(pair, axis=1).astype(BF16)
        left = l_buf[h][...].reshape(OFFSETS * 64, N)
        for q in range(4):
            lanes = slice(q * 256, (q + 1) * 256)
            wide = slice(h * HP + q * 256, h * HP + (q + 1) * 256)
            real = dot(left, al[h][:, lanes], ((1,), (0,))).reshape(OFFSETS, 64, 256)
            imag = dot(
                left, al[h][:, HP + q * 256:HP + (q + 1) * 256], ((1,), (0,))
            ).reshape(OFFSETS, 64, 256)
            total_real, total_imag = real[0], imag[0]
            for k in range(4):
                w = table_ref[8 + k:9 + k, wide]
                total_real = total_real + w * real[1 + k]
                total_imag = total_imag + w * imag[1 + k]
            for k in range(4):
                w = table_ref[12 + k:13 + k, wide]
                total_real = total_real + w * imag[5 + k]
                total_imag = total_imag - w * real[5 + k]
            rp[h][now, :, 0:8, lanes] = total_real.reshape(8, 8, 256)
            rp[h][now, :, 8:16, lanes] = total_imag.reshape(8, 8, 256)
        if h == 0:
            weighted = [massn[now, b] * scale[b % 4] for b in range(8)]
            high, middle, _ = split3(jnp.concatenate(weighted, axis=0))
            masses = dot(high, onehot_t[...], ((1,), (1,))) + dot(
                middle, onehot_t[...], ((1,), (1,))
            )
            rp[h][now, :, 0:8, HP:HP + 128] = masses.reshape(8, 8, 128)
            rp[h][now, :, 8:16, HP:HP + 128] = jnp.zeros((8, 8, 128), F32)

    def rs(h, k):
        if k < 12:
            kind, part = k // 2, PARTS[k % 2]
            src, dst = sb[h].at[kind, part], rb[h].at[kind, part]
            target = up2[h] if kind < 3 else down2[h]
        elif k < 18:
            src, dst = sb2[h].at[k - 12], rb2[h].at[k - 12]
            target = (far1, up1, down1)[(k - 12) % 3][h]
        else:
            src, dst, target = sb3[h], rb3[h], z_other
        return pltpu.make_async_remote_copy(
            src_ref=src, dst_ref=dst, send_sem=rs_send.at[h, k], recv_sem=rs_recv.at[h, k],
            device_id=target, device_id_type=MESH,
        )

    def put(h, kind, place, r, p, add=None):
        part = PARTS[p]
        rows = slice(r * 4 + part.start, r * 4 + part.stop)
        value = rp[h][place, rows]
        if add is not None:
            rs(h, 2 * add + p).wait_recv()
            value = value + rb[h][add, part].astype(F32)
        sb[h][kind, part] = value.astype(BF16)
        rs(h, 2 * kind + p).start()

    def insert_step(i, carry):
        @pl.when(i == 3)
        def _():
            for h in range(2):
                put(h, 2, 1, 0, 0, add=0)
                put(h, 5, 2, 1, 0, add=3)

        for h in range(2):
            insert_chunk(h, 3 - i)

            @pl.when(i == 0)
            def _():
                for p in range(2):
                    put(h, 0, 3, 0, p)
                    put(h, 3, 3, 1, p)

            @pl.when(i == 1)
            def _():
                put(h, 4, 2, 0, 0)

            @pl.when(i == 2)
            def _():
                put(h, 1, 1, 1, 0)

        return carry

    lax.fori_loop(0, 4, insert_step, 0)

    for h in range(2):
        put(h, 4, 2, 0, 1)
        put(h, 1, 1, 1, 1)
        put(h, 2, 1, 0, 1, add=0)
        put(h, 5, 2, 1, 1, add=3)

    def take(h, p, r):
        part = PARTS[p]
        from_below, from_above = ((2, 4), (1, 5))[r]
        rs(h, 2 * from_below + p).wait_recv()
        rs(h, 2 * from_above + p).wait_recv()
        rows = slice(r * 4 + part.start, r * 4 + part.stop)
        return (
            rp[h][0, rows] + rb[h][from_below, part].astype(F32)
        ) + rb[h][from_above, part].astype(F32)

    for r in (1, 0):
        for h in range(2):
            above, below, far = (0, 1, 2)
            taken = take(h, 0, r)
            for k, place in enumerate((far, above, below)):
                sb2[h][3 * r + k] = taken[place].astype(BF16)
                rs(h, 12 + 3 * r + k).start()

    def own(h, r):
        total = take(h, 1, r)[0]
        for k in range(3):
            rs(h, 12 + 3 * r + k).wait_recv()
            total = total + rb2[h][3 * r + k].astype(F32)
        return total

    for h in range(2):
        sb3[h][...] = own(h, 1).astype(BF16)
        rs(h, 18).start()
    mine = [own(h, 0) for h in range(2)]

    for h in range(2):
        for k in range(18):
            rs(h, k).wait_send()
    for o in range(1, 8):
        dir_copy(o).wait_send()

    for h in range(2):
        rs(h, 18).wait_recv()
        result = mine[h] + rb3[h][...].astype(F32)
        sums_ref[:, h * HP:(h + 1) * HP] = result[0:8, 0:HP]
        sums_ref[:, PIX + h * HP:PIX + (h + 1) * HP] = result[8:16, 0:HP]
        if h == 0:
            weights_ref[...] = lax.dot_general(
                result[0:8, HP:HP + GROUPS], gain[...], (((1,), (0,)), ((), ())),
                precision=lax.Precision.HIGHEST, preferred_element_type=F32,
            )

    for h in range(2):
        rs(h, 18).wait_send()


def finish(sums_in, weights_in, stats_in, sums_ref, weights_ref, norm_ref, peak_ref):
    sums_ref[...] = sums_in[...]
    weights_ref[...] = weights_in[...]
    norm_ref[...] = stats_in[0:1]
    peak_ref[...] = stats_in[1:2]


def per_device(
    images, refs, ctf, noise_var, shifts, ctf_class, psi_prev, earlier_direction_range, view_range
):
    vmem = pl.BlockSpec(memory_space=pltpu.VMEM)
    hbm = pl.BlockSpec(memory_space=pl.ANY)
    wa, wb = WIDTHS
    dma = pltpu.SemaphoreType.DMA
    out = pl.pallas_call(
        kernel,
        out_shape=(
            jax.ShapeDtypeStruct((8, 2 * PIX), F32),
            jax.ShapeDtypeStruct((8, PIX), F32),
            jax.ShapeDtypeStruct((8, N), F32),
        ),
        in_specs=[hbm] * 10,
        out_specs=(vmem, vmem, vmem),
        scratch_shapes=[
            pltpu.SMEM((16,), jnp.int32),
            pltpu.VMEM((N, 2 * PIX), BF16),
            pltpu.VMEM((8, 2 * PIX), BF16),
            pltpu.VMEM((GROUPS, PIX), F32),
            pltpu.VMEM((1, PIX), F32),
            pltpu.VMEM((8, N), jnp.int32),
            pltpu.VMEM((2, N), jnp.int32),
            pltpu.VMEM((16, PIX), F32),
            pltpu.VMEM((4, 2, 4, 16, HP), BF16),
            pltpu.VMEM((4, 2, 4, 16, HP), BF16),
            pltpu.VMEM((N, 2 * HP), BF16),
            pltpu.VMEM((N, 2 * HP), BF16),
            pltpu.VMEM((N, PIX), F32),
            pltpu.VMEM((6, N, 128), F32),
            pltpu.VMEM((OFFSETS * 64, 2 * HP), BF16),
            pltpu.VMEM((OFFSETS * 64, 2 * HP), BF16),
            pltpu.VMEM((64, HP), F32),
            pltpu.VMEM((GROUPS, PIX), F32),
            pltpu.VMEM((3, GROUPS, PIX), BF16),
            pltpu.VMEM((2, 4, 8, 8, 128), F32),
            pltpu.VMEM((128, N), BF16),
            pltpu.VMEM((2, 8, N), F32),
            pltpu.VMEM((2, 4, OFFSETS, 8, 8, N), F32),
            pltpu.VMEM((4, 8, 8, N), F32),
            pltpu.VMEM((8, N), F32),
            pltpu.VMEM((2, 8, N), F32),
            pltpu.VMEM((OFFSETS, 4, 16, N), BF16),
            pltpu.VMEM((OFFSETS, 4, 16, N), BF16),
            pltpu.VMEM((4, 8, 16, wa), F32),
            pltpu.VMEM((4, 8, 16, wb), F32),
            pltpu.VMEM((8, 8, 128), F32),
            pltpu.VMEM((6, 4, 16, wa), BF16),
            pltpu.VMEM((6, 4, 16, wb), BF16),
            pltpu.VMEM((6, 4, 16, wa), BF16),
            pltpu.VMEM((6, 4, 16, wb), BF16),
            pltpu.VMEM((6, 16, wa), BF16),
            pltpu.VMEM((6, 16, wb), BF16),
            pltpu.VMEM((6, 16, wa), BF16),
            pltpu.VMEM((6, 16, wb), BF16),
            pltpu.VMEM((16, wa), BF16),
            pltpu.VMEM((16, wb), BF16),
            pltpu.VMEM((16, wa), BF16),
            pltpu.VMEM((16, wb), BF16),
            dma((10,)),
            dma((2, 25)),
            dma((2, 25)),
            dma((7,)),
            dma((7,)),
            dma((2, 19)),
            dma((2, 19)),
        ],
        compiler_params=pltpu.CompilerParams(
            collective_id=0, has_side_effects=True, vmem_limit_bytes=60 * 2**20
        ),
        cost_estimate=pl.CostEstimate(
            flops=10_000_000_000, bytes_accessed=4_000_000, transcendentals=600_000
        ),
        name="expectation_step",
    )(
        images, refs, ctf, noise_var.reshape(1, PIX), ctf_class.reshape(1, N),
        psi_prev.reshape(1, N), earlier_direction_range.reshape(1, N), shifts.T, view_range,
        jnp.asarray(phase_constants()),
    )
    class_sums, weight_sums, log_norm, peak_prob = pl.pallas_call(
        finish,
        out_shape=(
            jax.ShapeDtypeStruct((8, 2 * PIX), F32),
            jax.ShapeDtypeStruct((8, PIX), F32),
            jax.ShapeDtypeStruct((1, N), F32),
            jax.ShapeDtypeStruct((1, N), F32),
        ),
        in_specs=[vmem] * 3,
        out_specs=(vmem,) * 4,
        name="finish",
    )(*out)
    return class_sums, weight_sums, log_norm.reshape(N), peak_prob.reshape(N)


def solution(mesh):
    placed = (
        P("dom", None),
        P(("dir", "dom"), None),
        P(),
        P(),
        P("dom", None),
        P("dom"),
        P("dom"),
        P("dom"),
        P("dir"),
    )
    return jax.shard_map(
        per_device,
        mesh=mesh,
        in_specs=placed,
        out_specs=(P(("dir", "dom"), None), P(("dir", "dom"), None), P("dom"), P("dom")),
        check_vma=False,
    )
```

```python
import math

import jax
import jax.numpy as jnp
import numpy as np
from jax import lax
from jax.experimental import pallas as pl
from jax.experimental.pallas import tpu as pltpu
from jax.sharding import PartitionSpec as P

CROP = 64
HALF = 32
PIX = 2048
OFFSETS = 9
GROUPS = 64
N = 256
BLOCKS = 32
HP = 1024
WIDTHS = (HP + 128, HP)
THETA = 2.0 * math.pi / CROP

F32 = jnp.float32
BF16 = jnp.bfloat16
MESH = pl.DeviceIdType.MESH

PAIRS = ((0, 1), (1, 0), (1, 1), (1, -1))


def offset_index(ty, tx):
    return (ty + 1) * 3 + (tx + 1)


def phase_constants():
    pixels = np.arange(PIX)
    alpha = THETA * (pixels // HALF)
    beta = THETA * (pixels % HALF)
    rows = []
    for ty, tx in PAIRS:
        angle = ty * alpha + tx * beta
        rows += [np.cos(angle), np.sin(angle)]
    ca, sa, cb, sb = np.cos(alpha), np.sin(alpha), np.cos(beta), np.sin(beta)
    rows += [cb, ca, ca * cb, -sa * sb, sb, ca * sb, sa, sa * cb]
    return np.stack(rows).astype(np.float32)


def cos_sin(index):
    m = jnp.bitwise_and(index, 63) + 8
    quarter = jnp.bitwise_and(jnp.right_shift(m, 4), 3)
    x = (jnp.bitwise_and(m, 15) - 8).astype(F32) * F32(THETA)
    x2 = x * x
    c = 1.0 + x2 * (-0.5 + x2 * (1 / 24 + x2 * (-1 / 720 + x2 * (1 / 40320))))
    s = x * (1.0 + x2 * (-1 / 6 + x2 * (1 / 120 + x2 * (-1 / 5040 + x2 * (1 / 362880)))))
    odd = jnp.bitwise_and(quarter, 1) == 1
    cc = jnp.where(odd, s, c)
    ss = jnp.where(odd, c, s)
    cos = jnp.where((quarter == 1) | (quarter == 2), -cc, cc)
    sin = jnp.where(quarter >= 2, -ss, ss)
    return cos, sin


def split3(value):
    high = value.astype(BF16)
    rest = value - high.astype(F32)
    middle = rest.astype(BF16)
    low = (rest - middle.astype(F32)).astype(BF16)
    return high, middle, low


def dot(a, b, dims):
    return lax.dot_general(a, b, (dims, ((), ())), preferred_element_type=F32)


def tree(op, values):
    while len(values) > 1:
        pairs = [op(a, b) for a, b in zip(values[::2], values[1::2])]
        values = pairs + values[len(pairs) * 2:]
    return values[0]


def ring(i):
    return lax.rem(i + 8, 4)


def ahead_of(place):
    return lax.rem((place * (place + 1)) // 2, 4)


PIECES = (slice(0, 1), slice(1, 3), slice(3, 4))
PARTS = (slice(1, 4), slice(0, 1))


def kernel(
    images_ref, refs_ref, ctf_ref, noise_ref, class_ref, psi_ref, range_ref, shift_ref,
    views_in, table_in,
    sums_ref, weights_ref, stats_ref,
    views_ref, img, refs_in, ctf, noise_in, ints, shift_in, table_ref,
    g_a, g_b, al_a, al_b, wsel, spin, s_a, s_b, mag, gain, gain3, en, onehot_t, psi_rows_sc,
    sc, massn, early, factor, l_a, l_b, rp_a, rp_b,
    st, sb_a, sb_b, rb_a, rb_b, sb2_a, sb2_b, rb2_a, rb2_b, sb3_a, sb3_b, rb3_a, rb3_b,
    load_sem, ag_send, ag_recv, dir_send, dir_recv, rs_send, rs_recv,
):
    g = (g_a, g_b)
    al = (al_a, al_b)
    s_buf = (s_a, s_b)
    l_buf = (l_a, l_b)
    rp = (rp_a, rp_b)
    sb, rb = (sb_a, sb_b), (rb_a, rb_b)
    sb2, rb2 = (sb2_a, sb2_b), (rb2_a, rb2_b)
    sb3, rb3 = (sb3_a, sb3_b), (rb3_a, rb3_b)

    me_dir = lax.axis_index("dir")
    me_dom = lax.axis_index("dom")
    y = me_dom // 8
    z = lax.rem(me_dom // 4, 2)
    x = lax.rem(me_dom, 4)

    def device(yy, zz, xx):
        return (me_dir, (yy * 2 + zz) * 4 + xx)

    x_up, x_down = device(y, z, ring(x + 1)), device(y, z, ring(x - 1))
    y_up, y_down = device(ring(y + 1), z, x), device(ring(y - 1), z, x)
    z_other = device(y, 1 - z, x)
    dir_peers = [(lax.rem(me_dir + o, 8), me_dom) for o in range(1, 8)]

    up2, down2 = (y_up, x_up), (y_down, x_down)
    up1, down1 = (x_up, y_up), (x_down, y_down)
    far1 = (device(y, z, ring(x + 2)), device(ring(y + 2), z, x))

    barrier = pltpu.get_barrier_semaphore()
    partners = [z_other, x_up, x_down, y_up, y_down, *far1] + dir_peers
    for p in partners:
        pl.semaphore_signal(barrier, inc=1, device_id=p, device_id_type=MESH)

    loads = [
        pltpu.make_async_copy(src, dst, load_sem.at[k])
        for k, (src, dst) in enumerate((
            (refs_ref, refs_in), (shift_ref, shift_in), (class_ref, ints.at[0:1]),
            (psi_ref, ints.at[1:2]), (range_ref, ints.at[2:3]), (noise_ref, noise_in),
            (ctf_ref, ctf), (images_ref, img), (table_in, table_ref),
            (views_in, views_ref),
        ))
    ]
    for load in loads:
        load.start()

    loads[0].wait()
    for h in range(2):
        real = refs_in[:, h * HP:(h + 1) * HP].astype(F32)
        imag = refs_in[:, PIX + h * HP:PIX + (h + 1) * HP].astype(F32)
        g[h][0, 0, 0] = jnp.concatenate([real, imag], axis=0).astype(BF16)

    pl.semaphore_wait(barrier, len(partners))

    def ag(h, k):
        buf = g[h]
        if k == 0:
            src, dst, target = buf.at[0, 0, 0], buf.at[0, 1, 0], z_other
        elif k < 7:
            r, way = (k - 1) % 2, (k - 1) // 2
            target = (up1, down1, far1)[way][h]
            src, dst = buf.at[0, r, 0], buf.at[0, r, (2, 1, 3)[way]]
        else:
            piece = PIECES[(k - 7) % 3]
            kind = (k - 7) // 3
            upward = kind < 3
            target = up2[h] if upward else down2[h]
            side = 2 if upward else 1
            if kind % 3 < 2:
                r = kind % 3
                src, dst = buf.at[0, r, piece], buf.at[side, r, piece]
            else:
                r = 0 if upward else 1
                src, dst = buf.at[side, r, piece], buf.at[3, r, piece]
        return pltpu.make_async_remote_copy(
            src_ref=src, dst_ref=dst, send_sem=ag_send.at[h, k], recv_sem=ag_recv.at[h, k],
            device_id=target, device_id_type=MESH,
        )

    def ag_start(*ks):
        for k in ks:
            for h in range(2):
                ag(h, k).start()

    def ag_wait(*ks):
        for k in ks:
            for h in range(2):
                ag(h, k).wait_recv()

    Z_, INNER = 0, ((1, 3, 5), (2, 4, 6))

    def outer(kind, piece):
        return 7 + 3 * kind + piece

    U0, U1, UR, D0, D1, DR = range(6)

    ag_start(Z_, *INNER[0])
    ag_start(outer(U0, 0), outer(D0, 0))

    for k in range(1, 7):
        loads[k].wait()
    classes = ints[0:1, :]
    psi_prev = ints[1:2, :]
    ranges = ints[2:3, :]

    def column(row):
        wide = jnp.broadcast_to(row.astype(F32), (128, N))
        return jnp.transpose(wide).astype(jnp.int32)

    shift_y = column(shift_in[0:1, :])
    shift_x = column(shift_in[1:2, :])
    lane = lax.broadcasted_iota(jnp.int32, (N, 128), 1)
    fc, fs = cos_sin(
        jnp.bitwise_and(lane, 31) * shift_x + jnp.right_shift(lane, 5) * shift_y
    )
    spin[0], spin[1] = fc, fs
    rc, rs_ = cos_sin(4 * shift_y)
    spin[2], spin[3] = rc, rs_
    qc, qs = cos_sin(16 * shift_y)
    spin[4], spin[5] = qc, qs

    class_rows = lax.broadcasted_iota(jnp.int32, (128, N), 0)
    mask_t = (class_rows == classes).astype(F32)
    onehot_t[...] = mask_t.astype(BF16)
    onehot = jnp.transpose(mask_t).astype(BF16)

    psi_rows = lax.broadcasted_iota(jnp.int32, (16, N), 0)
    apart = jnp.abs(psi_rows - psi_prev)
    apart = jnp.minimum(apart, 16 - apart).astype(F32)
    psi_term = -(apart * apart * F32(0.5 / 9.0))
    psi_rows_sc[0] = psi_term[0:8]
    psi_rows_sc[1] = psi_term[8:16]

    ag_wait(Z_)
    ag_start(*INNER[1])
    ag_start(outer(U1, 0), outer(D1, 0))
    ag_wait(*INNER[0])
    for p in (1, 2):
        ag_start(outer(U0, p), outer(D0, p))

    noise = noise_in[...]
    for j in range(8):
        lanes = slice(j * 256, (j + 1) * 256)
        ctf_now = ctf[:, lanes]
        noise_now = noise[:, lanes]
        gain_now = ctf_now * ctf_now / noise_now
        gain[:, lanes] = gain_now
        for k, piece in enumerate(split3(gain_now)):
            gain3[k, :, lanes] = piece
        high, middle, low = split3(ctf_now / noise_now)
        pick = onehot[:, 0:GROUPS]
        wsel[:, lanes] = (
            dot(pick, high, ((1,), (0,))) + dot(pick, middle, ((1,), (0,)))
        ) + dot(pick, low, ((1,), (0,)))

    loads[7].wait()
    loads[8].wait()
    loads[9].wait()

    ag_wait(outer(U0, 0))
    ag_start(outer(UR, 0))

    def align(part, carry):
        rows = pl.ds(pl.multiple_of(part * 32, 32), 32)
        base_c, base_s = [spin[0, rows]], [spin[1, rows]]
        step_c, step_s = spin[2, rows], spin[3, rows]
        turn_c, turn_s = spin[4, rows], spin[5, rows]
        for j in range(16):
            if j == 0:
                c, s = base_c[0], base_s[0]
            elif j < 4:
                pc, ps = base_c[j - 1], base_s[j - 1]
                c, s = pc * step_c - ps * step_s, ps * step_c + pc * step_s
                base_c.append(c)
                base_s.append(s)
            else:
                pc, ps = base_c[j % 4], base_s[j % 4]
                c, s = pc * turn_c - ps * turn_s, ps * turn_c + pc * turn_s
                base_c[j % 4], base_s[j % 4] = c, s
            lanes = slice(j * 128, (j + 1) * 128)
            real = img[rows, lanes].astype(F32)
            imag = img[rows, PIX + j * 128:PIX + (j + 1) * 128].astype(F32)
            weight = wsel[rows, lanes]
            h, jj = j // 8, j % 8
            al[h][rows, jj * 128:(jj + 1) * 128] = ((real * c + imag * s) * weight).astype(BF16)
            al[h][rows, HP + jj * 128:HP + (jj + 1) * 128] = (
                (imag * c - real * s) * weight
            ).astype(BF16)
        return carry

    lax.fori_loop(0, 8, align, 0)

    def cross_chunk(h, slabs, r):
        many = 32 * len(slabs)
        for j in range(8):
            lanes = slice(j * 128, (j + 1) * 128)
            wide = slice(h * HP + j * 128, h * HP + (j + 1) * 128)
            value = jnp.concatenate(
                [g[h][now, r, :, :, lanes].astype(F32) for now in slabs], axis=0
            )
            real, imag = value[:, 0:8], value[:, 8:16]
            mag[0:many, lanes] = (real * real + imag * imag).reshape(many, 128)

            def put(t, shifted_real, shifted_imag):
                rows = slice(t * many, (t + 1) * many)
                s_buf[h][rows, lanes] = shifted_real.reshape(many, 128).astype(BF16)
                s_buf[h][rows, HP + j * 128:HP + (j + 1) * 128] = (
                    shifted_imag.reshape(many, 128).astype(BF16)
                )

            put(4, real, imag)
            for q, (ty, tx) in enumerate(PAIRS):
                c = table_ref[2 * q:2 * q + 1, wide][None]
                s = table_ref[2 * q + 1:2 * q + 2, wide][None]
                rc_, is_, rs_, ic_ = real * c, imag * s, real * s, imag * c
                put(offset_index(ty, tx), rc_ - is_, rs_ + ic_)
                put(offset_index(-ty, -tx), rc_ + is_, ic_ - rs_)
        high, middle, low = split3(mag[0:many])
        half = slice(h * HP, (h + 1) * HP)
        by_high = dot(jnp.concatenate([high, middle, low], axis=0), gain3[0, :, half], ((1,), (1,)))
        by_middle = dot(jnp.concatenate([high, middle], axis=0), gain3[1, :, half], ((1,), (1,)))
        by_low = dot(high, gain3[2, :, half], ((1,), (1,)))
        small = (by_low + by_high[2 * many:]) + by_middle[many:]
        energy = (small + (by_middle[0:many] + by_high[many:2 * many])) + by_high[0:many]
        energy = energy.reshape(len(slabs), 4, 8, GROUPS)
        cross = dot(s_buf[h][0:OFFSETS * many], al[h][...], ((1,), (1,))).reshape(
            OFFSETS, len(slabs), 4, 8, N
        )
        blocks = pl.ds(r * 4, 4)
        for k, now in enumerate(slabs):
            en[h, now, blocks, :, 0:GROUPS] = energy[k]
            sc[h, now, :, blocks] = cross[:, k]

    def score_slab(py, places, top):
        blocks = [(r, px) for r in range(2) for px in places]
        energies = [
            en[0, py, r * 4 + px, :, 0:GROUPS] + en[1, px, r * 4 + py, :, 0:GROUPS]
            for r, px in blocks
        ]
        high, middle, low = split3(jnp.concatenate(energies, axis=0))
        picks = onehot_t[0:GROUPS]
        picked = (
            dot(high, picks, ((1,), (0,))) + dot(middle, picks, ((1,), (0,)))
        ) + dot(low, picks, ((1,), (0,)))
        penalty = 0.5 * picked
        owner_y = ring(y + ahead_of(py))
        tops = [top]
        for k, (r, px) in enumerate(blocks):
            owner_z = lax.rem(z + r, 2)
            owner_x = ring(x + (0, 1, 3, 2)[px])
            view = views_ref[owner_y * 4 + owner_z * 2 + owner_x // 2]
            prior = psi_rows_sc[lax.rem(owner_x, 2)] + jnp.where(
                ranges == view, F32(1.5), F32(0.0)
            )
            less = penalty[k * 8:(k + 1) * 8]
            values = []
            for t in range(OFFSETS):
                value = sc[0, py, t, r * 4 + px] + sc[1, px, t, r * 4 + py]
                value = (value - less) + prior
                sc[0, py, t, r * 4 + px] = value
                values.append(value)
            tops.append(tree(jnp.maximum, values))
        return tree(jnp.maximum, tops)

    def combine(py, b, e):
        by_row = []
        for ty in range(3):
            minus, zero, plus = e[3 * ty], e[3 * ty + 1], e[3 * ty + 2]
            by_row.append((zero, plus + minus, plus - minus))
        out = []
        for k in range(3):
            minus, zero, plus = by_row[0][k], by_row[1][k], by_row[2][k]
            out.append((zero, plus + minus, plus - minus))
        order = (
            out[0][0], out[1][0], out[0][1], out[1][1], out[2][2],
            out[2][0], out[2][1], out[0][2], out[1][2],
        )
        for k in range(OFFSETS):
            sc[1, py, k, b] = order[k]
        massn[py, b] = (out[0][0] + out[1][0]) + (out[0][1] + out[1][1])

    def exp_slab(py, places, top, total, combined):
        sums = [total]
        for r in range(2):
            for px in places:
                b = r * 4 + px
                values = []
                for t in range(OFFSETS):
                    value = jnp.exp(sc[0, py, t, b] - top)
                    if not combined:
                        sc[0, py, t, b] = value
                    values.append(value)
                sums.append(tree(jnp.add, values))
                if combined:
                    combine(py, b, values)
        return tree(jnp.add, sums)

    def combine_slab(py, places):
        for r in range(2):
            for px in places:
                b = r * 4 + px
                combine(py, b, [sc[0, py, t, b] for t in range(OFFSETS)])

    nearby, every, lowest = (0, 1, 2), (0, 1, 2, 3), jnp.full((8, N), -jnp.inf, F32)
    nothing = jnp.zeros((8, N), F32)

    def early_scores():
        top = lax.fori_loop(0, 3, lambda py, v: score_slab(py, nearby, v), lowest)
        top = jnp.max(top, axis=0, keepdims=True)
        total = lax.fori_loop(
            0, 3, lambda py, v: exp_slab(py, nearby, top, v, True), nothing
        )
        early[0:1] = top
        early[1:2] = jnp.sum(total, axis=0, keepdims=True)

    def relay(arrived, onward, *ps):
        for p in ps:
            ag_wait(outer(arrived, p))
            ag_start(outer(onward, p))

    def own_step(r, carry):
        @pl.when(r == 1)
        def _():
            ag_wait(*INNER[1])
            for p in (1, 2):
                ag_start(outer(D1, p), outer(U1, p))

        for h in range(2):
            cross_chunk(h, (0,), r)
        return carry

    def sides_step(r, carry):
        @pl.when(r == 0)
        def _():
            relay(U0, UR, 1, 2)
            relay(D1, DR, 0)
            ag_wait(outer(D0, 0), outer(D0, 1), outer(D0, 2))

        @pl.when(r == 1)
        def _():
            relay(D1, DR, 1, 2)
            ag_wait(outer(U1, 0), outer(U1, 1), outer(U1, 2))

        for h in range(2):
            cross_chunk(h, (1, 2), r)
        return carry

    def far_step(r, carry):
        @pl.when(r == 0)
        def _():
            early_scores()
            ag_wait(outer(UR, 0), outer(UR, 1), outer(UR, 2))

        @pl.when(r == 1)
        def _():
            ag_wait(outer(DR, 0), outer(DR, 1), outer(DR, 2))

        for h in range(2):
            cross_chunk(h, (3,), r)
        return carry

    lax.fori_loop(0, 2, own_step, 0)
    lax.fori_loop(0, 2, sides_step, 0)
    lax.fori_loop(0, 2, far_step, 0)

    late_top = lax.fori_loop(0, 3, lambda py, v: score_slab(py, (3,), v), lowest)
    late_top = jnp.max(score_slab(3, every, late_top), axis=0, keepdims=True)
    late_total = lax.fori_loop(
        0, 3, lambda py, v: exp_slab(py, (3,), late_top, v, False), nothing
    )
    late_total = jnp.sum(
        exp_slab(3, every, late_top, late_total, False), axis=0, keepdims=True
    )
    early_top = early[0:1]
    top = jnp.maximum(early_top, late_top)
    total = early[1:2] * jnp.exp(early_top - top) + late_total * jnp.exp(late_top - top)

    for half in range(2):
        lanes = slice(half * 128, (half + 1) * 128)
        st[me_dir, half:half + 1] = top[:, lanes]
        st[me_dir, 2 + half:3 + half] = total[:, lanes]

    def dir_copy(o):
        return pltpu.make_async_remote_copy(
            src_ref=st.at[me_dir], dst_ref=st.at[me_dir], send_sem=dir_send.at[o - 1],
            recv_sem=dir_recv.at[o - 1], device_id=dir_peers[o - 1], device_id_type=MESH,
        )

    def dir_arrival(o):
        source = lax.rem(me_dir + 8 - o, 8)
        return pltpu.make_async_remote_copy(
            src_ref=st.at[source], dst_ref=st.at[source], send_sem=dir_send.at[o - 1],
            recv_sem=dir_recv.at[o - 1], device_id=dir_peers[o - 1], device_id_type=MESH,
        )

    for o in (4, 5, 3, 2, 6, 7, 1):
        dir_copy(o).start()

    def combine_late(py, carry):
        combine_slab(py, (3,))
        return carry

    lax.fori_loop(0, 3, combine_late, 0)
    combine_slab(3, every)
    for h in range(2):
        for k in range(25):
            ag(h, k).wait_send()

    for o in range(1, 8):
        dir_arrival(o).wait_recv()

    def joined(d, row):
        return jnp.concatenate([st[d, row:row + 1], st[d, row + 1:row + 2]], axis=1)

    tops = [joined(d, 0) for d in range(8)]
    best = tops[0]
    for d in range(1, 8):
        best = jnp.maximum(best, tops[d])
    mass_all = joined(0, 2) * jnp.exp(tops[0] - best)
    for d in range(1, 8):
        mass_all = mass_all + joined(d, 2) * jnp.exp(tops[d] - best)
    log_norm = best + jnp.log(mass_all)
    stats_ref[0:1] = log_norm
    stats_ref[1:2] = jnp.exp(best - log_norm)
    factor[0] = jnp.broadcast_to(jnp.exp(early_top - log_norm), (8, N))
    factor[1] = jnp.broadcast_to(jnp.exp(late_top - log_norm), (8, N))

    def insert_chunk(h, now):
        scale = [factor[now // 3]] * 3 + [factor[1]]
        for zz in range(2):
            for cp in range(2):
                pair = []
                for c in range(2):
                    cc = 2 * cp + c
                    if h == 0:
                        pair.append(sc[1, now, :, zz * 4 + cc] * scale[cc])
                    else:
                        pair.append(sc[1, cc, :, zz * 4 + now] * scale[cc])
                l_buf[h][:, zz * 2 + cp] = jnp.concatenate(pair, axis=1).astype(BF16)
        left = l_buf[h][...].reshape(OFFSETS * 64, N)
        for q in range(4):
            lanes = slice(q * 256, (q + 1) * 256)
            wide = slice(h * HP + q * 256, h * HP + (q + 1) * 256)
            real = dot(left, al[h][:, lanes], ((1,), (0,))).reshape(OFFSETS, 64, 256)
            imag = dot(
                left, al[h][:, HP + q * 256:HP + (q + 1) * 256], ((1,), (0,))
            ).reshape(OFFSETS, 64, 256)
            total_real, total_imag = real[0], imag[0]
            for k in range(4):
                w = table_ref[8 + k:9 + k, wide]
                total_real = total_real + w * real[1 + k]
                total_imag = total_imag + w * imag[1 + k]
            for k in range(4):
                w = table_ref[12 + k:13 + k, wide]
                total_real = total_real + w * imag[5 + k]
                total_imag = total_imag - w * real[5 + k]
            rp[h][now, :, 0:8, lanes] = total_real.reshape(8, 8, 256)
            rp[h][now, :, 8:16, lanes] = total_imag.reshape(8, 8, 256)
        if h == 0:
            weighted = [massn[now, b] * scale[b % 4] for b in range(8)]
            high, middle, _ = split3(jnp.concatenate(weighted, axis=0))
            masses = dot(high, onehot_t[...], ((1,), (1,))) + dot(
                middle, onehot_t[...], ((1,), (1,))
            )
            rp[h][now, :, 0:8, HP:HP + 128] = masses.reshape(8, 8, 128)
            rp[h][now, :, 8:16, HP:HP + 128] = jnp.zeros((8, 8, 128), F32)

    def rs(h, k):
        if k < 12:
            kind, part = k // 2, PARTS[k % 2]
            src, dst = sb[h].at[kind, part], rb[h].at[kind, part]
            target = up2[h] if kind < 3 else down2[h]
        elif k < 18:
            src, dst = sb2[h].at[k - 12], rb2[h].at[k - 12]
            target = (far1, up1, down1)[(k - 12) % 3][h]
        else:
            src, dst, target = sb3[h], rb3[h], z_other
        return pltpu.make_async_remote_copy(
            src_ref=src, dst_ref=dst, send_sem=rs_send.at[h, k], recv_sem=rs_recv.at[h, k],
            device_id=target, device_id_type=MESH,
        )

    def put(h, kind, place, r, p, add=None):
        part = PARTS[p]
        rows = slice(r * 4 + part.start, r * 4 + part.stop)
        value = rp[h][place, rows]
        if add is not None:
            rs(h, 2 * add + p).wait_recv()
            value = value + rb[h][add, part].astype(F32)
        sb[h][kind, part] = value.astype(BF16)
        rs(h, 2 * kind + p).start()

    def insert_step(i, carry):
        @pl.when(i == 3)
        def _():
            for h in range(2):
                put(h, 5, 2, 1, 0, add=3)
            for h in range(2):
                put(h, 2, 1, 0, 0, add=0)

        for h in range(2):
            insert_chunk(h, 3 - i)

            @pl.when(i == 0)
            def _():
                for p in range(2):
                    put(h, 0, 3, 0, p)
                    put(h, 3, 3, 1, p)

            @pl.when(i == 1)
            def _():
                put(h, 4, 2, 0, 0)

            @pl.when(i == 2)
            def _():
                put(h, 1, 1, 1, 0)

        return carry

    lax.fori_loop(0, 4, insert_step, 0)

    for h in range(2):
        put(h, 1, 1, 1, 1)
        put(h, 5, 2, 1, 1, add=3)
    for h in range(2):
        put(h, 4, 2, 0, 1)
        put(h, 2, 1, 0, 1, add=0)

    def take(h, p, r):
        part = PARTS[p]
        from_below, from_above = ((2, 4), (1, 5))[r]
        rs(h, 2 * from_below + p).wait_recv()
        rs(h, 2 * from_above + p).wait_recv()
        rows = slice(r * 4 + part.start, r * 4 + part.stop)
        return (
            rp[h][0, rows] + rb[h][from_below, part].astype(F32)
        ) + rb[h][from_above, part].astype(F32)

    for r in (1, 0):
        for h in range(2):
            above, below, far = (0, 1, 2)
            taken = take(h, 0, r)
            for k, place in enumerate((far, above, below)):
                sb2[h][3 * r + k] = taken[place].astype(BF16)
                rs(h, 12 + 3 * r + k).start()

    def own(h, r):
        total = take(h, 1, r)[0]
        for k in range(3):
            rs(h, 12 + 3 * r + k).wait_recv()
            total = total + rb2[h][3 * r + k].astype(F32)
        return total

    for h in range(2):
        sb3[h][...] = own(h, 1).astype(BF16)
        rs(h, 18).start()
    mine = [own(h, 0) for h in range(2)]

    for h in range(2):
        for k in range(18):
            rs(h, k).wait_send()
    for o in range(1, 8):
        dir_copy(o).wait_send()

    for h in range(2):
        rs(h, 18).wait_recv()
        result = mine[h] + rb3[h][...].astype(F32)
        sums_ref[:, h * HP:(h + 1) * HP] = result[0:8, 0:HP]
        sums_ref[:, PIX + h * HP:PIX + (h + 1) * HP] = result[8:16, 0:HP]
        if h == 0:
            weights_ref[...] = lax.dot_general(
                result[0:8, HP:HP + GROUPS], gain[...], (((1,), (0,)), ((), ())),
                precision=lax.Precision.HIGHEST, preferred_element_type=F32,
            )

    for h in range(2):
        rs(h, 18).wait_send()


def finish(sums_in, weights_in, stats_in, sums_ref, weights_ref, norm_ref, peak_ref):
    sums_ref[...] = sums_in[...]
    weights_ref[...] = weights_in[...]
    norm_ref[...] = stats_in[0:1]
    peak_ref[...] = stats_in[1:2]


def per_device(
    images, refs, ctf, noise_var, shifts, ctf_class, psi_prev, earlier_direction_range, view_range
):
    vmem = pl.BlockSpec(memory_space=pltpu.VMEM)
    hbm = pl.BlockSpec(memory_space=pl.ANY)
    wa, wb = WIDTHS
    dma = pltpu.SemaphoreType.DMA
    out = pl.pallas_call(
        kernel,
        out_shape=(
            jax.ShapeDtypeStruct((8, 2 * PIX), F32),
            jax.ShapeDtypeStruct((8, PIX), F32),
            jax.ShapeDtypeStruct((8, N), F32),
        ),
        in_specs=[hbm] * 10,
        out_specs=(vmem, vmem, vmem),
        scratch_shapes=[
            pltpu.SMEM((16,), jnp.int32),
            pltpu.VMEM((N, 2 * PIX), BF16),
            pltpu.VMEM((8, 2 * PIX), BF16),
            pltpu.VMEM((GROUPS, PIX), F32),
            pltpu.VMEM((1, PIX), F32),
            pltpu.VMEM((8, N), jnp.int32),
            pltpu.VMEM((2, N), jnp.int32),
            pltpu.VMEM((16, PIX), F32),
            pltpu.VMEM((4, 2, 4, 16, HP), BF16),
            pltpu.VMEM((4, 2, 4, 16, HP), BF16),
            pltpu.VMEM((N, 2 * HP), BF16),
            pltpu.VMEM((N, 2 * HP), BF16),
            pltpu.VMEM((N, PIX), F32),
            pltpu.VMEM((6, N, 128), F32),
            pltpu.VMEM((OFFSETS * 64, 2 * HP), BF16),
            pltpu.VMEM((OFFSETS * 64, 2 * HP), BF16),
            pltpu.VMEM((64, HP), F32),
            pltpu.VMEM((GROUPS, PIX), F32),
            pltpu.VMEM((3, GROUPS, PIX), BF16),
            pltpu.VMEM((2, 4, 8, 8, 128), F32),
            pltpu.VMEM((128, N), BF16),
            pltpu.VMEM((2, 8, N), F32),
            pltpu.VMEM((2, 4, OFFSETS, 8, 8, N), F32),
            pltpu.VMEM((4, 8, 8, N), F32),
            pltpu.VMEM((8, N), F32),
            pltpu.VMEM((2, 8, N), F32),
            pltpu.VMEM((OFFSETS, 4, 16, N), BF16),
            pltpu.VMEM((OFFSETS, 4, 16, N), BF16),
            pltpu.VMEM((4, 8, 16, wa), F32),
            pltpu.VMEM((4, 8, 16, wb), F32),
            pltpu.VMEM((8, 8, 128), F32),
            pltpu.VMEM((6, 4, 16, wa), BF16),
            pltpu.VMEM((6, 4, 16, wb), BF16),
            pltpu.VMEM((6, 4, 16, wa), BF16),
            pltpu.VMEM((6, 4, 16, wb), BF16),
            pltpu.VMEM((6, 16, wa), BF16),
            pltpu.VMEM((6, 16, wb), BF16),
            pltpu.VMEM((6, 16, wa), BF16),
            pltpu.VMEM((6, 16, wb), BF16),
            pltpu.VMEM((16, wa), BF16),
            pltpu.VMEM((16, wb), BF16),
            pltpu.VMEM((16, wa), BF16),
            pltpu.VMEM((16, wb), BF16),
            dma((10,)),
            dma((2, 25)),
            dma((2, 25)),
            dma((7,)),
            dma((7,)),
            dma((2, 19)),
            dma((2, 19)),
        ],
        compiler_params=pltpu.CompilerParams(
            collective_id=0, has_side_effects=True, vmem_limit_bytes=60 * 2**20
        ),
        cost_estimate=pl.CostEstimate(
            flops=10_000_000_000, bytes_accessed=4_000_000, transcendentals=600_000
        ),
        name="expectation_step",
    )(
        images, refs, ctf, noise_var.reshape(1, PIX), ctf_class.reshape(1, N),
        psi_prev.reshape(1, N), earlier_direction_range.reshape(1, N), shifts.T, view_range,
        jnp.asarray(phase_constants()),
    )
    class_sums, weight_sums, log_norm, peak_prob = pl.pallas_call(
        finish,
        out_shape=(
            jax.ShapeDtypeStruct((8, 2 * PIX), F32),
            jax.ShapeDtypeStruct((8, PIX), F32),
            jax.ShapeDtypeStruct((1, N), F32),
            jax.ShapeDtypeStruct((1, N), F32),
        ),
        in_specs=[vmem] * 3,
        out_specs=(vmem,) * 4,
        name="finish",
    )(*out)
    return class_sums, weight_sums, log_norm.reshape(N), peak_prob.reshape(N)


def solution(mesh):
    placed = (
        P("dom", None),
        P(("dir", "dom"), None),
        P(),
        P(),
        P("dom", None),
        P("dom"),
        P("dom"),
        P("dom"),
        P("dir"),
    )
    return jax.shard_map(
        per_device,
        mesh=mesh,
        in_specs=placed,
        out_specs=(P(("dir", "dom"), None), P(("dir", "dom"), None), P("dom"), P("dom")),
        check_vma=False,
    )
```
